32 devices in a mesh: fold: 4 (over x, core), samp: 4 (over z), feat: 2 (over y).
Axes of the slice: x: 2, y: 2, z: 4, core: 2. Of those that a mesh axis runs over, the one named last changes fastest.
Arguments:
- input_points: bfloat16 [4096, 128], P('samp'), may hold values from -6 to 6
- wave_numbers: bfloat16 [128, 4096], P(None, 'feat'), may hold values from -0.5 to 0.5
- offset_angles: float32 [4096], P('feat'), may hold values from -3.140625 to 3.140625
- feature_magnitudes: float32 [4096], P('feat'), may hold values from 0.3 to 3
- response_values: float32 [4096], P('samp'), may hold values from -6 to 6
- split_label: int32 [16384], P(('fold', 'samp')), parts along dimension 0, may hold values from 0 to 15
- shrinkage_levels: float32 [16], replicated, may hold values from 0.001 to 1000
Outputs:
- coefficients: float32 [64, 4096], P('fold', 'feat'), parts along dimension 0
- predictions: float32 [64, 4096], P('fold', 'samp'), parts along dimension 0
The draws below stay inside these ranges and needn't reach their ends.
There are 4 independent parts, one for each index of `fold`. The reference program is written for one: setup_inputs(seed, part) draws one part's arguments, and reference() takes and returns one part's arrays. A program takes and returns all parts, laid end to end along the dimension named above; an argument that names none is the same for every part. Nothing has to cross between parts.
Inputs may be any that keep to these rules, and one draw needn't show every extreme that they name: `split_label`: each sample's fold; samples of fold 0 are the held-out ones.
All inputs are finite; a program needn't handle non-finite values.
Results may differ from the reference program's by a relative error of at most 0.006.
Values may be sent and summed in bfloat16 or wider, within the bound.
No kernel may reach another device: no remote copies, remote signals or barrier semaphores. Data moves between devices by JAX's collectives and lax.ppermute only.
A program may use at most 64 MiB of HBM per device.

```python
import math
import jax
import jax.numpy as jnp
from jax import lax

DIM = 128
FEATURES = 4096
RIDGE_LEVELS = 16
ITERS = 3
FOLDS = 16
S_DEV = 1024
NS = 4096


def with_ends(entries, own_key, low, top_value):
    place = [jax.random.randint(jax.random.fold_in(own_key, axis), (), 0, length) for axis, length in enumerate(entries.shape)]
    widest = entries.shape.index(max(entries.shape))
    next_to = place[:widest] + [(place[widest] + 1) % entries.shape[widest]] + place[widest + 1:]
    return entries.at[tuple(place)].set(low).at[tuple(next_to)].set(top_value)


def level_of(own_key, dims, cuts, low, top_value):
    factor_of, own = 1.0, jax.random.fold_in(own_key, 6)
    for dim, shards_of in cuts:
        steps = jnp.exp(jax.random.uniform(jax.random.fold_in(own, dim), (shards_of,), jnp.float32, low / len(cuts), top_value / len(cuts)))
        factor_of = factor_of * jnp.repeat(steps, dims[dim] // shards_of).reshape([-1 if axis == dim else 1 for axis in range(len(dims))])
    return factor_of


def scatter_about(own_key, extent, spread, most, shards=(), dtype=jnp.bfloat16):
    level = level_of(own_key, extent, shards, -0.22, 0.18) if shards else 1.0
    entries = jax.random.normal(own_key, extent, jnp.float32) * spread * level
    return jnp.minimum(jnp.maximum(entries, -most), most).astype(dtype)


def setup_inputs(seed: int = 0, part: int = 0) -> dict:
    keys = jax.random.split(jax.random.key(seed), 8)
    part_splits = jax.random.split(jax.random.fold_in(keys[7], part), 8)
    input_points = scatter_about(keys[0], (NS, DIM), 1.0, 6.0, ((0, 4),))
    wave_numbers = scatter_about(keys[1], (DIM, FEATURES), DIM ** -0.5, 0.5, ((1, 2),))
    offset_angles = jnp.clip(jax.random.uniform(keys[2], (FEATURES,), jnp.float32, -3.140625, 3.140625), -3.140625, 3.140625)
    feature_magnitudes = jnp.clip(jnp.exp(math.log(3.0) - 2.3025851 * jax.random.uniform(keys[3], (FEATURES,), jnp.float32) ** level_of(keys[3], (FEATURES,), ((0, 2),), -0.2, 0.2)), 0.3, 3.0)
    response_values = scatter_about(keys[4], (NS,), 1.0, 6.0, ((0, 4),), jnp.float32)
    split_label = with_ends(jax.random.randint(part_splits[5], (NS,), 0, FOLDS), jax.random.fold_in(part_splits[5], 1), 0, FOLDS - 1).astype(jnp.int32)
    shrinkage_levels = jnp.clip(jnp.exp(jax.random.uniform(keys[6], (RIDGE_LEVELS,), jnp.float32, math.log(0.001), math.log(1000.0))), 0.001, 1000.0)
    return dict(input_points=input_points, wave_numbers=wave_numbers, offset_angles=offset_angles, feature_magnitudes=feature_magnitudes, response_values=response_values, split_label=split_label, shrinkage_levels=shrinkage_levels)


highest = lax.Precision.HIGHEST

def feature_block(rows, wave_numbers, offset_angles, feature_magnitudes):
    angles = jnp.dot(rows, wave_numbers, preferred_element_type=jnp.float32) + offset_angles
    return feature_magnitudes * math.sqrt(2.0 / FEATURES) * jnp.cos(angles)

def reference(input_points, wave_numbers, offset_angles, feature_magnitudes, response_values, split_label, shrinkage_levels):
    observation_total = shrinkage_levels.shape[0]
    blocks = input_points.reshape(-1, S_DEV, DIM)
    nblocks = blocks.shape[0]
    fitting_observations = (split_label != 0).astype(jnp.float32)
    kept_blocks = fitting_observations.reshape(nblocks, S_DEV)
    aim_blocks = (fitting_observations * response_values).reshape(nblocks, S_DEV)

    def forward(vectors):

        def visit(carried, rows):
            matrix = feature_block(rows, wave_numbers, offset_angles, feature_magnitudes)
            return (carried, lax.dot_general(vectors, matrix, (((1,), (1,)), ((), ())), precision=highest))
        _, stacked = lax.scan(visit, jnp.zeros((), jnp.float32), blocks)
        return stacked.transpose(1, 0, 2).reshape(observation_total, nblocks * S_DEV)

    def adjoint_product(weights):
        pieces = weights.reshape(observation_total, nblocks, S_DEV).transpose(1, 0, 2)

        def visit(total, item):
            rows, weight_rows = item
            matrix = feature_block(rows, wave_numbers, offset_angles, feature_magnitudes)
            return (total + jnp.dot(weight_rows, matrix, precision=highest), None)
        total, _ = lax.scan(visit, jnp.zeros((observation_total, FEATURES), jnp.float32), (blocks, pieces))
        return total

    def initial(total, item):
        rows, kept_part, aim_part = item
        matrix = feature_block(rows, wave_numbers, offset_angles, feature_magnitudes)
        gram_part = jnp.dot(kept_part, matrix * matrix, precision=highest)
        side_part = jnp.dot(aim_part, matrix, precision=highest)
        return (total + jnp.stack([gram_part, side_part]), None)
    split_moments, _ = lax.scan(initial, jnp.zeros((2, FEATURES), jnp.float32), (blocks, kept_blocks, aim_blocks))
    jacobi_reciprocal = split_moments[0][None, :] + shrinkage_levels[:, None]
    residual = jnp.broadcast_to(split_moments[1][None, :], jacobi_reciprocal.shape)
    scaled = residual / jacobi_reciprocal
    inner_now = lax.optimization_barrier(jnp.sum(residual * scaled, axis=1))

    def iterate(counter, carried):
        weights_now, residual, conjugate_step, inner_now = carried
        lifted_design = forward(conjugate_step)
        lifted_column = adjoint_product(lifted_design * fitting_observations[None, :]) + shrinkage_levels[:, None] * conjugate_step
        step_size = inner_now / lax.optimization_barrier(jnp.sum(conjugate_step * lifted_column, axis=1))
        weights_now = weights_now + step_size[:, None] * conjugate_step
        residual = residual - step_size[:, None] * lifted_column
        scaled = residual / jacobi_reciprocal
        inner_next = lax.optimization_barrier(jnp.sum(residual * scaled, axis=1))
        conjugate_step = scaled + (inner_next / inner_now)[:, None] * conjugate_step
        return (weights_now, residual, conjugate_step, inner_next)
    carried = (jnp.zeros_like(residual), residual, scaled, inner_now)
    weights_now, residual, conjugate_step, inner_now = lax.fori_loop(0, ITERS, iterate, carried)
    return (weights_now, forward(weights_now))
```

```python
import functools
import math

import jax
import jax.numpy as jnp
from jax import lax
from jax.experimental import pallas as pl
from jax.experimental.pallas import tpu as pltpu
from jax.sharding import PartitionSpec as P

f32, bf16 = jnp.float32, jnp.bfloat16
TURN = 1.0 / (2.0 * math.pi)
COSINE = (0.999999211770312, -19.738980419471126, 64.92865850463285, -85.27162830146948, 58.79050662870376, -21.071108461771125)
LANES = 128
VMEM_LIMIT = 32 * 2**20


def in_vmem(value):
    return pltpu.with_memory_space_constraint(value, pltpu.VMEM)


def call(body, outs, *args, flops=0, held=True):
    outs = [pltpu.VMEM(s, d) if held else jax.ShapeDtypeStruct(s, d) for s, d in outs]
    size = sum(math.prod(a.shape) * a.dtype.itemsize for a in args)
    return pl.pallas_call(
        body,
        out_shape=outs,
        compiler_params=pltpu.CompilerParams(vmem_limit_bytes=VMEM_LIMIT),
        cost_estimate=pl.CostEstimate(flops=flops, bytes_accessed=size, transcendentals=0),
    )(*args)


def exchange(value, axis, n):
    return [value] + [
        lax.ppermute(value, axis, [(i, i ^ s) for i in range(n)]) for s in range(1, n)
    ]


def total(refs):
    values = [r[...] for r in refs]
    while len(values) > 1:
        values = [values[i] + values[i + 1] for i in range(0, len(values), 2)]
    return values[0]


def halves(value):
    high = value.astype(bf16)
    return high, (value - high.astype(f32)).astype(bf16)


def product(rows, high_ref, low_ref, contract):
    high, low = halves(rows)
    n = rows.shape[0]
    both = jnp.concatenate([high.astype(f32), low.astype(f32)], axis=0).astype(bf16)
    dims = (((1,), (contract,)), ((), ()))
    a = lax.dot_general(both, high_ref[...], dims, preferred_element_type=f32)
    b = lax.dot_general(high, low_ref[...], dims, preferred_element_type=f32)
    return a[:n] + a[n:] + b


def pack_scalars(columns, rows):
    lane = lax.broadcasted_iota(jnp.int32, (rows, LANES), 1)
    out = jnp.zeros((rows, LANES), f32)
    for i, column in enumerate(columns):
        out = jnp.where(lane == i, column, out)
    return out


def row_sum(value):
    return jnp.sum(value, axis=1, keepdims=True)


def features_kernel(x_ref, w_ref, offset_ref, label_ref, response_ref, high_ref, low_ref, moment_ref, acc):
    samples, features = x_ref.shape[0], w_ref.shape[1]
    kept = (label_ref[...] != 0).astype(f32)
    columns = jnp.concatenate(
        [kept, kept * response_ref[...], jnp.zeros((6, samples), f32)], axis=0
    ).T
    offsets = offset_ref[...] * TURN
    acc[...] = jnp.zeros_like(acc)
    rb, cb = min(samples, 512), min(features, 512)
    for i in range(0, samples, rb):
        for j in range(0, features, cb):
            a = jnp.dot(x_ref[i : i + rb, :], w_ref[:, j : j + cb], preferred_element_type=f32)
            t = a * TURN + offsets[:, j : j + cb]
            r = t - jnp.round(t)
            u = r * r
            c = jnp.full_like(u, COSINE[-1])
            for q in COSINE[-2::-1]:
                c = c * u + q
            high, low = halves(c)
            high_ref[i : i + rb, j : j + cb] = high
            low_ref[i : i + rb, j : j + cb] = low
            square = c * c * columns[i : i + rb, 0:1]
            side = c * columns[i : i + rb, 1:2]
            acc[0, :, j : j + cb] += square.reshape(rb // 8, 8, cb).sum(0)
            acc[1, :, j : j + cb] += side.reshape(rb // 8, 8, cb).sum(0)
    moment_ref[0:1, :] = jnp.sum(acc[0], axis=0, keepdims=True)
    moment_ref[1:2, :] = jnp.sum(acc[1], axis=0, keepdims=True)


def begin_kernel(nz, *refs):
    moments, (penalty, mag, high, low), (msg, direction, precond, residual) = (
        refs[:nz],
        refs[nz : nz + 4],
        refs[nz + 4 :],
    )
    sums = total(moments)
    m = mag[...]
    pre = sums[0:1] * (m * m) + penalty[...]
    res = jnp.broadcast_to(sums[1:2] * m, pre.shape)
    s = res / pre
    precond[...] = pre
    residual[...] = res
    direction[...] = s
    send_forward(s, m, high, low, msg, [row_sum(res * s), row_sum(s * s)])


def send_forward(s, m, high, low, msg, scalars):
    samples = high.shape[0]
    msg[:, :samples] = product(s * m, high, low, 1)
    msg[:, samples:] = pack_scalars(scalars, s.shape[0])


def adjoint_kernel(ny, first, last, *refs):
    parts, refs = refs[:ny], refs[ny:]
    label, high, low, refs = refs[0], refs[1], refs[2], refs[3:]
    sums = total(parts)
    samples = label.shape[1]
    image_rows, sc = sums[:, :samples], sums[:, samples:]
    rz, dd = sc[:, 0:1], sc[:, 1:2]
    beta = jnp.zeros_like(rz)
    if not first:
        before, before_sc, refs = refs[0], refs[1], refs[2:]
        beta = rz / before_sc[:, 0:1]
        image_rows = image_rows + beta * before[...]
        dd = dd + 2.0 * beta * sc[:, 2:3] + beta * beta * before_sc[:, 1:2]
    msg, rows_out, sc_out = refs
    kept = (label[...] != 0).astype(f32)
    weighted = image_rows * kept
    scalars = pack_scalars([row_sum(weighted * image_rows)], dd.shape[0])
    if last:
        msg[...] = scalars
    else:
        features = high.shape[1]
        msg[:, :features] = product(weighted, high, low, 0)
        msg[:, features:] = scalars
    rows_out[...] = image_rows
    sc_out[...] = pack_scalars([rz, dd, beta], dd.shape[0])


def update_kernel(nz, first, *refs):
    parts, refs = refs[:nz], refs[nz:]
    sc, penalty, mag, precond, high, low, residual, scaled, refs = *refs[:8], refs[8:]
    sums = total(parts)
    features = mag.shape[1]
    lam, m = penalty[...], mag[...]
    direction = scaled[...]
    if first:
        (msg, scaled_out, direction_out, residual_out, weights_out, step_out) = refs
    else:
        (before, weights, msg, scaled_out, direction_out, residual_out, weights_out, step_out) = refs
        direction = direction + sc[:, 2:3] * before[...]
    image = sums[:, :features] * m + lam * direction
    step = sc[:, 0:1] / (sums[:, features : features + 1] + lam * sc[:, 1:2])
    moved = step * direction
    weights_out[...] = moved if first else weights[...] + moved
    res = residual[...] - step * image
    s = res / precond[...]
    residual_out[...] = res
    scaled_out[...] = s
    direction_out[...] = direction
    step_out[...] = pack_scalars([step], step.shape[0])
    send_forward(s, m, high, low, msg, [row_sum(res * s), row_sum(s * s), row_sum(s * direction)])


def finish_kernel(nz, count, *refs):
    parts, refs = refs[:nz], refs[nz:]
    sc, penalty, scaled, before, weights, refs = *refs[:5], refs[5:]
    rows, steps, (weights_out, predictions_out) = refs[:count], refs[count : 2 * count - 1], refs[2 * count - 1 :]
    sums = total(parts)
    step = sc[:, 0:1] / (sums[:, 0:1] + penalty[...] * sc[:, 1:2])
    weights_out[...] = weights[...] + step * (scaled[...] + sc[:, 2:3] * before[...])
    predictions = step * rows[-1][...]
    for r, s in zip(rows, steps):
        predictions = predictions + s[:, 0:1] * r[...]
    predictions_out[...] = predictions


ITERS = 3


def shards(
    nz,
    ny,
    input_points,
    wave_numbers,
    offset_angles,
    feature_magnitudes,
    response_values,
    split_label,
    shrinkage_levels,
):
    samples, features = input_points.shape[0], wave_numbers.shape[1]
    whole = features * ny
    levels = shrinkage_levels.shape[0]
    label = split_label.reshape(1, samples)
    penalty = shrinkage_levels.reshape(levels, 1)
    mag = feature_magnitudes.reshape(1, features) * math.sqrt(2.0 / whole)
    row_f, row_s, row_c = ((levels, features), f32), ((levels, samples), f32), ((levels, LANES), f32)
    msg_f, msg_s = ((levels, features + LANES), f32), ((levels, samples + LANES), f32)

    high, low, moments = pl.pallas_call(
        features_kernel,
        out_shape=[
            pltpu.VMEM((samples, features), bf16),
            pltpu.VMEM((samples, features), bf16),
            pltpu.VMEM((2, features), f32),
        ],
        scratch_shapes=[pltpu.VMEM((2, 8, features), f32)],
        compiler_params=pltpu.CompilerParams(vmem_limit_bytes=VMEM_LIMIT),
    )(input_points, wave_numbers, offset_angles.reshape(1, features), label, response_values.reshape(1, samples))
    high, low = in_vmem(high), in_vmem(low)
    moments = exchange(moments, "samp", nz)
    msg, scaled, precond, residual = call(
        functools.partial(begin_kernel, nz),
        [msg_s, row_f, row_f, row_f],
        *moments, penalty, mag, high, low,
    )
    before = rows = sc = weights = None
    all_rows, steps = [], []
    for it in range(ITERS):
        first, last = it == 0, it == ITERS - 1
        parts = exchange(msg, "feat", ny)
        msg, rows, sc = call(
            functools.partial(adjoint_kernel, ny, first, last),
            [row_c if last else msg_f, row_s, row_c],
            *parts, label, high, low, *(() if first else (rows, sc)),
        )
        all_rows.append(rows)
        parts = exchange(msg, "samp", nz)
        if last:
            break
        msg, scaled, before, residual, weights, step = call(
            functools.partial(update_kernel, nz, first),
            [msg_s, row_f, row_f, row_f, row_f, row_c],
            *parts, sc, penalty, mag, precond, high, low, residual, scaled,
            *(() if first else (before, weights)),
        )
        steps.append(step)
    return call(
        functools.partial(finish_kernel, nz, ITERS),
        [row_f, row_s],
        *parts, sc, penalty, scaled, before, weights, *all_rows, *steps,
        held=False,
    )


def solution(mesh):
    placed = (
        P("samp", None),
        P(None, "feat"),
        P("feat"),
        P("feat"),
        P("samp"),
        P(("fold", "samp")),
        P(),
    )
    return jax.shard_map(
        functools.partial(shards, mesh.shape["samp"], mesh.shape["feat"]),
        mesh=mesh,
        in_specs=placed,
        out_specs=(P("fold", "feat"), P("fold", "samp")),
        check_vma=False,
    )
```

```python
import functools
import math

import jax
import jax.numpy as jnp
from jax import lax
from jax.experimental import pallas as pl
from jax.experimental.pallas import tpu as pltpu
from jax.sharding import PartitionSpec as P

f32, bf16 = jnp.float32, jnp.bfloat16
TURN = 1.0 / (2.0 * math.pi)
COSINE = (0.999999211770312, -19.738980419471126, 64.92865850463285, -85.27162830146948, 58.79050662870376, -21.071108461771125)
LANES = 128
VMEM_LIMIT = 12 * 2**20


def call(body, outs, *args, flops=0, held=True):
    outs = [pltpu.VMEM(s, d) if held else jax.ShapeDtypeStruct(s, d) for s, d in outs]
    size = sum(math.prod(a.shape) * a.dtype.itemsize for a in args)
    return pl.pallas_call(
        body,
        out_shape=outs,
        compiler_params=pltpu.CompilerParams(vmem_limit_bytes=VMEM_LIMIT),
        cost_estimate=pl.CostEstimate(flops=flops, bytes_accessed=size, transcendentals=0),
    )(*args)


def exchange(value, axis, n):
    return [value] + [
        lax.ppermute(value, axis, [(i, i ^ s) for i in range(n)]) for s in range(1, n)
    ]


def total(refs):
    values = [r[...] for r in refs]
    while len(values) > 1:
        values = [values[i] + values[i + 1] for i in range(0, len(values), 2)]
    return values[0]


def halves(value):
    high = value.astype(bf16)
    return high, (value - high.astype(f32)).astype(bf16)


def product(rows, high_ref, low_ref, contract):
    high, low = halves(rows)
    n = rows.shape[0]
    both = jnp.concatenate([high.astype(f32), low.astype(f32)], axis=0).astype(bf16)
    dims = (((1,), (contract,)), ((), ()))
    a = lax.dot_general(both, high_ref[...], dims, preferred_element_type=f32)
    b = lax.dot_general(high, low_ref[...], dims, preferred_element_type=f32)
    return a[:n] + a[n:] + b


def pack_scalars(columns, rows):
    lane = lax.broadcasted_iota(jnp.int32, (rows, LANES), 1)
    out = jnp.zeros((rows, LANES), f32)
    for i, column in enumerate(columns):
        out = jnp.where(lane == i, column, out)
    return out


def row_sum(value):
    return jnp.sum(value, axis=1, keepdims=True)


def features_kernel(
    scale, x_hbm, w_hbm, offset_hbm, mag_hbm, response_hbm, label_hbm, penalty_hbm,
    high_ref, low_ref, moment_ref, mag_ref, kept_ref, penalty_ref,
    x_ref, w_ref, offset_ref, mag_in, response_ref, label_ref, penalty_in, acc, sems,
):
    samples, features = x_ref.shape[0], w_ref.shape[1]
    rb, cb = min(samples, 512), min(features, 512)
    pairs = [(x_hbm, x_ref), (offset_hbm, offset_ref), (label_hbm, label_ref), (response_hbm, response_ref)]
    pairs += [(w_hbm.at[:, j : j + cb], w_ref.at[:, j : j + cb]) for j in range(0, features, cb)]
    pairs += [(mag_hbm, mag_in), (penalty_hbm, penalty_in)]
    copies = [pltpu.make_async_copy(a, b, sems.at[i]) for i, (a, b) in enumerate(pairs)]
    for copy in copies:
        copy.start()
    acc[...] = jnp.zeros_like(acc)
    for copy in copies[:4]:
        copy.wait()
    kept = (label_ref[...] != 0).astype(f32)
    kept_ref[...] = kept
    columns = jnp.concatenate(
        [kept, kept * response_ref[...], jnp.zeros((6, samples), f32)], axis=0
    ).T
    offsets = offset_ref[...] * TURN
    for j in range(0, features, cb):
        copies[4 + j // cb].wait()
        for i in range(0, samples, rb):
            a = jnp.dot(x_ref[i : i + rb, :], w_ref[:, j : j + cb], preferred_element_type=f32)
            t = a * TURN + offsets[:, j : j + cb]
            r = t - jnp.round(t)
            u = r * r
            c = jnp.full_like(u, COSINE[-1])
            for q in COSINE[-2::-1]:
                c = c * u + q
            high, low = halves(c)
            high_ref[i : i + rb, j : j + cb] = high
            low_ref[i : i + rb, j : j + cb] = low
            square = c * c * columns[i : i + rb, 0:1]
            side = c * columns[i : i + rb, 1:2]
            acc[0, :, j : j + cb] += square.reshape(rb // 8, 8, cb).sum(0)
            acc[1, :, j : j + cb] += side.reshape(rb // 8, 8, cb).sum(0)
    moment_ref[0:1, :] = jnp.sum(acc[0], axis=0, keepdims=True)
    moment_ref[1:2, :] = jnp.sum(acc[1], axis=0, keepdims=True)
    for copy in copies[-2:]:
        copy.wait()
    mag_ref[...] = mag_in[...] * scale
    levels = penalty_in.shape[1]
    at = [lax.broadcasted_iota(jnp.int32, (levels, levels), a) for a in (0, 1)]
    penalty_ref[...] = row_sum(jnp.where(at[0] == at[1], penalty_in[...], 0.0))


def begin_kernel(nz, *refs):
    moments, (penalty, mag, high, low), (msg, direction, precond, residual) = (
        refs[:nz],
        refs[nz : nz + 4],
        refs[nz + 4 :],
    )
    sums = total(moments)
    m = mag[...]
    pre = sums[0:1] * (m * m) + penalty[...]
    res = jnp.broadcast_to(sums[1:2] * m, pre.shape)
    s = res / pre
    precond[...] = pre
    residual[...] = res
    direction[...] = s
    send_forward(s, m, high, low, msg, [row_sum(res * s), row_sum(s * s)])


def send_forward(s, m, high, low, msg, scalars):
    samples = high.shape[0]
    msg[:, :samples] = product(s * m, high, low, 1)
    msg[:, samples:] = pack_scalars(scalars, s.shape[0])


def adjoint_kernel(ny, first, last, *refs):
    parts, refs = refs[:ny], refs[ny:]
    kept, high, low, refs = refs[0], refs[1], refs[2], refs[3:]
    sums = total(parts)
    samples = kept.shape[1]
    image_rows, sc = sums[:, :samples], sums[:, samples:]
    rz, dd = sc[:, 0:1], sc[:, 1:2]
    beta = jnp.zeros_like(rz)
    if not first:
        before, before_sc, refs = refs[0], refs[1], refs[2:]
        beta = rz / before_sc[:, 0:1]
        image_rows = image_rows + beta * before[...]
        dd = dd + 2.0 * beta * sc[:, 2:3] + beta * beta * before_sc[:, 1:2]
    msg, rows_out, sc_out = refs
    weighted = image_rows * kept[...]
    scalars = pack_scalars([row_sum(weighted * image_rows)], dd.shape[0])
    if last:
        msg[...] = scalars
    else:
        features = high.shape[1]
        msg[:, :features] = product(weighted, high, low, 0)
        msg[:, features:] = scalars
    rows_out[...] = image_rows
    sc_out[...] = pack_scalars([rz, dd, beta], dd.shape[0])


def update_kernel(nz, first, *refs):
    parts, refs = refs[:nz], refs[nz:]
    sc, penalty, mag, precond, high, low, residual, scaled, refs = *refs[:8], refs[8:]
    sums = total(parts)
    features = mag.shape[1]
    lam, m = penalty[...], mag[...]
    direction = scaled[...]
    if first:
        (msg, scaled_out, direction_out, residual_out, weights_out, step_out) = refs
    else:
        (before, weights, msg, scaled_out, direction_out, residual_out, weights_out, step_out) = refs
        direction = direction + sc[:, 2:3] * before[...]
    image = sums[:, :features] * m + lam * direction
    step = sc[:, 0:1] / (sums[:, features : features + 1] + lam * sc[:, 1:2])
    moved = step * direction
    weights_out[...] = moved if first else weights[...] + moved
    res = residual[...] - step * image
    s = res / precond[...]
    residual_out[...] = res
    scaled_out[...] = s
    direction_out[...] = direction
    step_out[...] = pack_scalars([step], step.shape[0])
    send_forward(s, m, high, low, msg, [row_sum(res * s), row_sum(s * s), row_sum(s * direction)])


def finish_kernel(nz, count, *refs):
    parts, refs = refs[:nz], refs[nz:]
    sc, penalty, scaled, before, weights, refs = *refs[:5], refs[5:]
    rows, steps, (weights_out, predictions_out) = refs[:count], refs[count : 2 * count - 1], refs[2 * count - 1 :]
    sums = total(parts)
    step = sc[:, 0:1] / (sums[:, 0:1] + penalty[...] * sc[:, 1:2])
    weights_out[...] = weights[...] + step * (scaled[...] + sc[:, 2:3] * before[...])
    predictions = step * rows[-1][...]
    for r, s in zip(rows, steps):
        predictions = predictions + s[:, 0:1] * r[...]
    predictions_out[...] = predictions


ITERS = 3


def shards(
    nz,
    ny,
    input_points,
    wave_numbers,
    offset_angles,
    feature_magnitudes,
    response_values,
    split_label,
    shrinkage_levels,
):
    samples, features = input_points.shape[0], wave_numbers.shape[1]
    whole = features * ny
    levels = shrinkage_levels.shape[0]
    row_f, row_s, row_c = ((levels, features), f32), ((levels, samples), f32), ((levels, LANES), f32)
    msg_f, msg_s = ((levels, features + LANES), f32), ((levels, samples + LANES), f32)

    inputs = [input_points, wave_numbers]
    inputs += [v.reshape(1, -1) for v in (offset_angles, feature_magnitudes, response_values, split_label, shrinkage_levels)]
    high, low, moments, mag, kept, penalty = pl.pallas_call(
        functools.partial(features_kernel, math.sqrt(2.0 / whole)),
        out_shape=[
            pltpu.VMEM((samples, features), bf16),
            pltpu.VMEM((samples, features), bf16),
            pltpu.VMEM((2, features), f32),
            pltpu.VMEM((1, features), f32),
            pltpu.VMEM((1, samples), f32),
            pltpu.VMEM((levels, 1), f32),
        ],
        in_specs=[pl.BlockSpec(memory_space=pltpu.HBM)] * len(inputs),
        scratch_shapes=[pltpu.VMEM(v.shape, v.dtype) for v in inputs]
        + [pltpu.VMEM((2, 8, features), f32), pltpu.SemaphoreType.DMA((6 + features // min(features, 512),))],
        compiler_params=pltpu.CompilerParams(vmem_limit_bytes=VMEM_LIMIT),
    )(*[pltpu.with_memory_space_constraint(v, pltpu.HBM) for v in inputs])
    moments = exchange(moments, "samp", nz)
    msg, scaled, precond, residual = call(
        functools.partial(begin_kernel, nz),
        [msg_s, row_f, row_f, row_f],
        *moments, penalty, mag, high, low,
    )
    before = rows = sc = weights = None
    all_rows, steps = [], []
    for it in range(ITERS):
        first, last = it == 0, it == ITERS - 1
        parts = exchange(msg, "feat", ny)
        msg, rows, sc = call(
            functools.partial(adjoint_kernel, ny, first, last),
            [row_c if last else msg_f, row_s, row_c],
            *parts, kept, high, low, *(() if first else (rows, sc)),
        )
        all_rows.append(rows)
        parts = exchange(msg, "samp", nz)
        if last:
            break
        msg, scaled, before, residual, weights, step = call(
            functools.partial(update_kernel, nz, first),
            [msg_s, row_f, row_f, row_f, row_f, row_c],
            *parts, sc, penalty, mag, precond, high, low, residual, scaled,
            *(() if first else (before, weights)),
        )
        steps.append(step)
    return call(
        functools.partial(finish_kernel, nz, ITERS),
        [row_f, row_s],
        *parts, sc, penalty, scaled, before, weights, *all_rows, *steps,
        held=False,
    )


def solution(mesh):
    placed = (
        P("samp", None),
        P(None, "feat"),
        P("feat"),
        P("feat"),
        P("samp"),
        P(("fold", "samp")),
        P(),
    )
    return jax.shard_map(
        functools.partial(shards, mesh.shape["samp"], mesh.shape["feat"]),
        mesh=mesh,
        in_specs=placed,
        out_specs=(P("fold", "feat"), P("fold", "samp")),
        check_vma=False,
    )
```

```python
import functools
import math

import jax
import jax.numpy as jnp
from jax import lax
from jax.experimental import pallas as pl
from jax.experimental.pallas import tpu as pltpu
from jax.sharding import PartitionSpec as P

f32, bf16 = jnp.float32, jnp.bfloat16
TURN = 1.0 / (2.0 * math.pi)
COSINE = (0.999999211770312, -19.738980419471126, 64.92865850463285, -85.27162830146948, 58.79050662870376, -21.071108461771125)
LANES = 128
VMEM_LIMIT = 12 * 2**20


def call(body, outs, *args, flops=0, held=True, scratch=()):
    outs = [pltpu.VMEM(s, d) if held else jax.ShapeDtypeStruct(s, d) for s, d in outs]
    size = sum(math.prod(a.shape) * a.dtype.itemsize for a in args)
    return pl.pallas_call(
        body,
        out_shape=outs,
        scratch_shapes=list(scratch),
        compiler_params=pltpu.CompilerParams(vmem_limit_bytes=VMEM_LIMIT),
        cost_estimate=pl.CostEstimate(flops=flops, bytes_accessed=size, transcendentals=0),
    )(*args)


def total(refs):
    values = [r[...] for r in refs]
    while len(values) > 1:
        values = [values[i] + values[i + 1] for i in range(0, len(values), 2)]
    return values[0]


def halves(value):
    high = value.astype(bf16)
    return high, (value - high.astype(f32)).astype(bf16)


def product(rows, high_ref, low_ref):
    high, low = halves(rows)
    n = rows.shape[0]
    both = jnp.concatenate([high.astype(f32), low.astype(f32)], axis=0).astype(bf16)
    a = jnp.dot(both, high_ref[...], preferred_element_type=f32)
    b = jnp.dot(high, low_ref[...], preferred_element_type=f32)
    return a[:n] + a[n:] + b


def pack_scalars(columns, rows):
    lane = lax.broadcasted_iota(jnp.int32, (rows, LANES), 1)
    out = jnp.zeros((rows, LANES), f32)
    for i, column in enumerate(columns):
        out = jnp.where(lane == i, column, out)
    return out


def row_sum(value):
    return jnp.sum(value, axis=1, keepdims=True)


def flip(value, axis, n, s):
    return lax.ppermute(value, axis, [(i, i ^ s) for i in range(n)])


def exchange(value, axis, n):
    return [value] + [flip(value, axis, n, s) for s in range(1, n)]


def as_row(block):
    return jnp.concatenate([block[i : i + 1] for i in range(block.shape[0])], axis=1)


def spread(pair, rows):
    return jnp.concatenate(
        [jnp.broadcast_to(pair[e : e + 1], (rows // 2, pair.shape[1])) for e in (0, 1)], axis=0
    )


def core():
    return lax.rem(lax.axis_index("fold"), 2)


def pack_kernel(
    scale, nz, x_hbm, w_hbm, offset_hbm, mag_hbm, response_hbm, label_hbm, penalty_hbm, other_label,
    msg, w_ref, offset_ref, mag_ref, penalty_ref,
    points, offset_in, mag_in, response_ref, label_ref, penalty_in, sems,
):
    half = points.shape[0]
    c = core()
    pairs = [
        (x_hbm.at[pl.ds(pl.multiple_of(c * half, half), half), :], points),
        (label_hbm, label_ref), (response_hbm, response_ref), (w_hbm, w_ref),
        (offset_hbm, offset_in), (mag_hbm, mag_in), (penalty_hbm, penalty_in),
    ]
    copies = [pltpu.make_async_copy(a, b, sems.at[i]) for i, (a, b) in enumerate(pairs)]
    for copy in copies:
        copy.start()
    for copy in copies[1:3]:
        copy.wait()
    n = half // LANES

    def mine(block):
        return jnp.where(c == 0, block[:n], block[n:])

    own = (mine(label_ref[...]) != 0).astype(f32)
    other = (mine(other_label[...]) != 0).astype(f32)
    y = mine(response_ref[...])
    high, middle = halves(y)
    y = y - high.astype(f32)
    middle, low = halves(y)
    aux = [jnp.where(c == 0, own, other), jnp.where(c == 0, other, own)]
    aux += [v.astype(f32) for v in (high, middle, low)]
    aux += [jnp.zeros((msg.shape[0] - half - 5 * n, LANES), f32)]
    msg[half:, :] = jnp.concatenate(aux, axis=0).astype(bf16)
    copies[0].wait()
    msg[:half, :] = points[...]
    for copy in copies[3:]:
        copy.wait()
    offset_ref[...] = offset_in[...] * TURN
    mag_ref[...] = mag_in[...] * scale
    levels, rows = penalty_in.shape[1], penalty_ref.shape[0]
    row, column = [lax.broadcasted_iota(jnp.int32, (rows, levels), a) for a in (0, 1)]
    chosen = column == lax.axis_index("samp") * (rows // 2) + lax.rem(row, rows // 2)
    penalty_ref[...] = row_sum(jnp.where(chosen, penalty_in[...], 0.0))


def features_kernel(first, msg, w_ref, offset_ref, *refs):
    before, refs = (None, refs) if first else (refs[0], refs[1:])
    high_ref, low_ref, high_t, low_t, kept_ref, moment_ref, acc = refs
    samples, features = high_ref.shape
    n = samples // LANES
    aux = msg[samples:, :].astype(f32)
    kept = jnp.concatenate([as_row(aux[e * n : (e + 1) * n]) for e in (0, 1)], axis=0)
    kept_ref[...] = spread(kept, kept_ref.shape[0])
    y = (aux[2 * n : 3 * n] + aux[3 * n : 4 * n]) + aux[4 * n : 5 * n]
    y_high, y_low = halves(kept * as_row(y))
    y_both = jnp.concatenate([y_high.astype(f32), y_low.astype(f32)], axis=0).astype(bf16)
    columns = jnp.concatenate([kept, jnp.zeros((6, samples), f32)], axis=0).T
    cb = min(features, 256)
    for j in range(0, features, cb):
        a = jnp.dot(msg[:samples, :], w_ref[:, j : j + cb], preferred_element_type=f32)
        t = a * TURN + offset_ref[:, j : j + cb]
        r = t - jnp.round(t)
        u = r * r
        c = jnp.full_like(u, COSINE[-1])
        for q in COSINE[-2::-1]:
            c = c * u + q
        high, low = halves(c)
        high_ref[:, j : j + cb] = high
        low_ref[:, j : j + cb] = low
        high_t[j : j + cb, :] = high.T
        low_t[j : j + cb, :] = low.T
        square = c * c
        for e in (0, 1):
            part = square * columns[:, e : e + 1]
            acc[e, :, j : j + cb] = part.reshape(samples // 8, 8, cb).sum(0)
        side = jnp.dot(y_both, high, preferred_element_type=f32)
        side = side[:2] + side[2:] + jnp.dot(y_high, low, preferred_element_type=f32)
        moment_ref[2:4, j : j + cb] = side if first else before[2:4, j : j + cb] + side
    for e in (0, 1):
        square = jnp.sum(acc[e], axis=0, keepdims=True)
        moment_ref[e : e + 1, :] = square if first else before[e : e + 1, :] + square


def send_forward(s, m, blocks, msg, scalars):
    v = s * m
    at = 0
    for high, low in zip(blocks[::2], blocks[1::2]):
        n = high.shape[1]
        msg[:, at : at + n] = product(v, high, low)
        at += n
    msg[:, at:] = pack_scalars(scalars, s.shape[0])


def begin_kernel(nz, *refs):
    moments, penalty, mag, blocks = refs[:2], refs[2], refs[3], refs[4 : 4 + 2 * nz]
    msg, direction, precond, residual = refs[4 + 2 * nz :]
    sums = total(moments)
    m = mag[...]
    rows = penalty.shape[0]
    pre = spread(sums[0:2] * (m * m), rows) + penalty[...]
    res = spread(sums[2:4] * m, rows)
    s = res / pre
    precond[...] = pre
    residual[...] = res
    direction[...] = s
    send_forward(s, m, blocks, msg, [row_sum(res * s), row_sum(s * s)])


def adjoint_kernel(ny, nz, first, *refs):
    parts, refs = refs[:ny], refs[ny:]
    kepts, blocks, refs = refs[:nz], refs[nz : 3 * nz], refs[3 * nz :]
    sums = total(parts)
    half = kepts[0].shape[1]
    samples = half * nz
    image_rows, sc = sums[:, :samples], sums[:, samples:]
    rz, dd = sc[:, 0:1], sc[:, 1:2]
    beta = jnp.zeros_like(rz)
    if not first:
        before, before_sc, refs = refs[0], refs[1], refs[2:]
        beta = rz / before_sc[:, 0:1]
        image_rows = image_rows + beta * before[...]
        dd = dd + 2.0 * beta * sc[:, 2:3] + beta * beta * before_sc[:, 1:2]
    msg, rows_out, sc_out = refs
    squares = jnp.zeros_like(dd)
    adjoint = 0.0
    for j, (kept, high, low) in enumerate(zip(kepts, blocks[::2], blocks[1::2])):
        rows = image_rows[:, j * half : (j + 1) * half]
        weighted = rows * kept[...]
        squares = squares + row_sum(weighted * rows)
        adjoint = adjoint + product(weighted, high, low)
    msg[:, : adjoint.shape[1]] = adjoint
    msg[:, adjoint.shape[1] :] = pack_scalars([squares], dd.shape[0])
    rows_out[...] = image_rows
    sc_out[...] = pack_scalars([rz, dd, beta], dd.shape[0])


def update_kernel(nz, first, *refs):
    parts, refs = refs[:2], refs[2:]
    sc, penalty, mag, precond, residual, scaled, rows, refs = *refs[:7], refs[7:]
    blocks, refs = refs[: 2 * nz], refs[2 * nz :]
    sums = total(parts)
    features = mag.shape[1]
    lam, m = penalty[...], mag[...]
    direction = scaled[...]
    if first:
        msg, scaled_out, direction_out, residual_out, weights_out, predicted_out = refs
    else:
        before, weights, predicted = refs[:3]
        msg, scaled_out, direction_out, residual_out, weights_out, predicted_out = refs[3:]
        direction = direction + sc[:, 2:3] * before[...]
    image = sums[:, :features] * m + lam * direction
    step = sc[:, 0:1] / (sums[:, features : features + 1] + lam * sc[:, 1:2])
    moved, fitted = step * direction, step * rows[...]
    weights_out[...] = moved if first else weights[...] + moved
    predicted_out[...] = fitted if first else predicted[...] + fitted
    res = residual[...] - step * image
    s = res / precond[...]
    residual_out[...] = res
    scaled_out[...] = s
    direction_out[...] = direction
    send_forward(s, m, blocks, msg, [row_sum(res * s), row_sum(s * s), row_sum(s * direction)])


def fold_rows(value, fold):
    n = value.shape[0] // 2
    return jnp.where(fold == 0, value[:n], value[n:])


def last_kernel(ny, nz, *refs):
    parts, refs = refs[:ny], refs[ny:]
    kepts, (before, before_sc, predicted, msg, rows_out, sc_out) = refs[:nz], refs[nz:]
    sums = total(parts)
    half = kepts[0].shape[1]
    samples = half * nz
    sc = sums[:, samples:]
    rz = sc[:, 0:1]
    beta = rz / before_sc[:, 0:1]
    image_rows = sums[:, :samples] + beta * before[...]
    dd = sc[:, 1:2] + 2.0 * beta * sc[:, 2:3] + beta * beta * before_sc[:, 1:2]
    squares = jnp.zeros_like(dd)
    for j, kept in enumerate(kepts):
        rows = image_rows[:, j * half : (j + 1) * half]
        squares = squares + row_sum(rows * rows * kept[...])
    other = 1 - core()
    n = dd.shape[0] // 2
    msg[:n, :samples] = fold_rows(image_rows, other)
    msg[n:, :samples] = fold_rows(predicted[...], other)
    msg[:, samples:] = pack_scalars([squares], 2 * n)
    rows_out[...] = image_rows
    sc_out[...] = pack_scalars([rz, dd, beta], 2 * n)


def finish_kernel(nz, own, got, sc, penalty, scaled, before, weights, rows, predicted, *outs):
    samples, features = rows.shape[1], scaled.shape[1]
    half = samples // nz
    c = core()
    n = sc.shape[0] // 2
    step = sc[:, 0:1] / ((own[:, samples : samples + 1] + got[:, samples : samples + 1]) + penalty[...] * sc[:, 1:2])
    coefficients = weights[...] + step * (scaled[...] + sc[:, 2:3] * before[...])
    coefficients = fold_rows(coefficients, c)
    here = fold_rows(predicted[...] + step * rows[...], c)
    there = got[n:, :samples] + fold_rows(step, c) * got[:n, :samples]
    lower, upper = jnp.where(c == 0, here, there), jnp.where(c == 0, there, here)
    for j, out in enumerate(outs):
        out[:, :features] = coefficients
        out[:, features : features + half] = lower[:, j * half : (j + 1) * half]
        out[:, features + half :] = upper[:, j * half : (j + 1) * half]


def arrange_kernel(nz, *refs):
    parts, (weights_out, predictions_out, held) = refs[:nz], refs[nz:]
    features = weights_out.shape[1]
    n = weights_out.shape[0] // nz
    for j, part in enumerate(parts):
        held[j] = part[...]
    z = lax.axis_index("samp")
    for k in range(nz):
        part = held[lax.bitwise_xor(z, k)]
        weights_out[k * n : (k + 1) * n, :] = part[:, :features]
        predictions_out[k * n : (k + 1) * n, :] = part[:, features:]


ITERS = 3


def shards(
    nf,
    nz,
    ny,
    input_points,
    wave_numbers,
    offset_angles,
    feature_magnitudes,
    response_values,
    split_label,
    shrinkage_levels,
):
    shard, features = input_points.shape[0], wave_numbers.shape[1]
    depth = input_points.shape[1]
    levels = shrinkage_levels.shape[0]
    half, rows = shard // 2, 2 * (levels // nz)
    samples = half * nz
    tall = (shard // LANES, LANES)
    extra = pl.cdiv(5 * half // LANES, 16) * 16
    row_f, row_s, row_c = ((rows, features), f32), ((rows, samples), f32), ((rows, LANES), f32)
    msg_f, msg_s = ((rows, features + LANES), f32), ((rows, samples + LANES), f32)

    label = split_label.reshape(tall)
    other_label = flip(label, "fold", nf, 1)
    inputs = [input_points, wave_numbers, offset_angles.reshape(1, features), feature_magnitudes.reshape(1, features)]
    inputs += [response_values.reshape(tall), label, shrinkage_levels.reshape(1, levels)]
    vectors = [((1, features), f32), ((1, features), f32), (tall, f32), (tall, jnp.int32), ((1, levels), f32)]
    msg, waves, offsets, mag, penalty = pl.pallas_call(
        functools.partial(pack_kernel, math.sqrt(2.0 / (features * ny)), nz),
        out_shape=[
            pltpu.VMEM((half + extra, depth), bf16),
            pltpu.VMEM((depth, features), bf16),
            pltpu.VMEM((1, features), f32),
            pltpu.VMEM((1, features), f32),
            pltpu.VMEM((rows, 1), f32),
        ],
        in_specs=[pl.BlockSpec(memory_space=pltpu.HBM)] * len(inputs) + [pl.BlockSpec(memory_space=pltpu.VMEM)],
        scratch_shapes=[pltpu.VMEM((half, depth), bf16)]
        + [pltpu.VMEM(v, d) for v, d in vectors]
        + [pltpu.SemaphoreType.DMA((len(inputs),))],
        compiler_params=pltpu.CompilerParams(vmem_limit_bytes=VMEM_LIMIT),
    )(*[pltpu.with_memory_space_constraint(v, pltpu.HBM) for v in inputs], other_label)

    blocks, turned, kepts, moments = [], [], [], None
    tile, tile_t = ((half, features), bf16), ((features, half), bf16)
    for j, part in enumerate(exchange(msg, "samp", nz)):
        high, low, high_t, low_t, kept, moments = call(
            functools.partial(features_kernel, j == 0),
            [tile, tile, tile_t, tile_t, ((rows, half), f32), ((4, features), f32)],
            part, waves, offsets, *(() if j == 0 else (moments,)),
            scratch=[pltpu.VMEM((2, 8, features), f32)],
            flops=60 * half * features,
        )
        blocks += [high, low]
        turned += [high_t, low_t]
        kepts.append(kept)
    msg, scaled, precond, residual = call(
        functools.partial(begin_kernel, nz),
        [msg_s, row_f, row_f, row_f],
        moments, flip(moments, "fold", nf, 1), penalty, mag, *turned,
    )
    before = weights = predicted = image_rows = sc = None
    for it in range(ITERS - 1):
        first = it == 0
        msg, image_rows, sc = call(
            functools.partial(adjoint_kernel, ny, nz, first),
            [msg_f, row_s, row_c],
            *exchange(msg, "feat", ny), *kepts, *blocks, *(() if first else (image_rows, sc)),
        )
        msg, scaled, before, residual, weights, predicted = call(
            functools.partial(update_kernel, nz, first),
            [msg_s, row_f, row_f, row_f, row_f, row_s],
            msg, flip(msg, "fold", nf, 1), sc, penalty, mag, precond, residual, scaled, image_rows, *turned,
            *(() if first else (before, weights, predicted)),
        )
    msg, image_rows, sc = call(
        functools.partial(last_kernel, ny, nz),
        [msg_s, row_s, row_c],
        *exchange(msg, "feat", ny), *kepts, image_rows, sc, predicted,
    )
    outs = call(
        functools.partial(finish_kernel, nz),
        [((rows // 2, features + shard), f32)] * nz,
        msg, flip(msg, "fold", nf, 1), sc, penalty, scaled, before, weights, image_rows, predicted,
    )
    outs = [outs[0]] + [flip(out, "samp", nz, j) for j, out in enumerate(outs) if j]
    return call(
        functools.partial(arrange_kernel, nz),
        [((levels, features), f32), ((levels, shard), f32)],
        *outs,
        scratch=[pltpu.VMEM((nz, rows // 2, features + shard), f32)],
        held=False,
    )


def solution(mesh):
    placed = (
        P("samp", None),
        P(None, "feat"),
        P("feat"),
        P("feat"),
        P("samp"),
        P(("fold", "samp")),
        P(),
    )
    sizes = [mesh.shape[axis] for axis in ("fold", "samp", "feat")]
    return jax.shard_map(
        functools.partial(shards, *sizes),
        mesh=mesh,
        in_specs=placed,
        out_specs=(P("fold", "feat"), P("fold", "samp")),
        check_vma=False,
    )
```

```python
import functools
import math

import jax
import jax.numpy as jnp
from jax import lax
from jax.experimental import pallas as pl
from jax.experimental.pallas import tpu as pltpu
from jax.sharding import PartitionSpec as P

f32, bf16 = jnp.float32, jnp.bfloat16
TURN = 1.0 / (2.0 * math.pi)
SINE = (-6.283164044377446, 41.337142378931674, -81.34076911271806, 70.99343519544783)
LANES = 128
VMEM_LIMIT = 12 * 2**20


def call(body, outs, *args, flops=0, held=True, scratch=(), aliases={}):
    outs = [pltpu.VMEM(s, d) if held else jax.ShapeDtypeStruct(s, d) for s, d in outs]
    size = sum(math.prod(a.shape) * a.dtype.itemsize for a in args)
    return pl.pallas_call(
        body,
        out_shape=outs,
        scratch_shapes=list(scratch),
        input_output_aliases=aliases,
        compiler_params=pltpu.CompilerParams(vmem_limit_bytes=VMEM_LIMIT),
        cost_estimate=pl.CostEstimate(flops=flops, bytes_accessed=size, transcendentals=0),
    )(*args)


def total(refs):
    values = [r[...] for r in refs]
    while len(values) > 1:
        values = [values[i] + values[i + 1] for i in range(0, len(values), 2)]
    return values[0]


def halves(value):
    high = value.astype(bf16)
    return high, (value - high.astype(f32)).astype(bf16)


def product(rows, high_ref, low_ref):
    high, low = halves(rows)
    n = rows.shape[0]
    both = jnp.concatenate([high.astype(f32), low.astype(f32)], axis=0).astype(bf16)
    a = jnp.dot(both, high_ref[...], preferred_element_type=f32)
    b = jnp.dot(high, low_ref[...], preferred_element_type=f32)
    return a[:n] + a[n:] + b


def pack_scalars(columns, rows):
    lane = lax.broadcasted_iota(jnp.int32, (rows, LANES), 1)
    out = jnp.zeros((rows, LANES), f32)
    for i, column in enumerate(columns):
        out = jnp.where(lane == i, column, out)
    return out


def row_sum(value):
    return jnp.sum(value, axis=1, keepdims=True)


def flip(value, axis, n, s):
    return lax.ppermute(value, axis, [(i, i ^ s) for i in range(n)])


def exchange(value, axis, n):
    return [value] + [flip(value, axis, n, s) for s in range(1, n)]


def as_row(block):
    return jnp.concatenate([block[i : i + 1] for i in range(block.shape[0])], axis=1)


def spread(pair, rows):
    return jnp.concatenate(
        [jnp.broadcast_to(pair[e : e + 1], (rows // 2, pair.shape[1])) for e in (0, 1)], axis=0
    )


def core():
    return lax.rem(lax.axis_index("fold"), 2)


def pack_kernel(
    scale, x_hbm, w_hbm, offset_hbm, mag_hbm, response_hbm, label_hbm, penalty_hbm,
    msg, w_ref, offset_ref, mag_ref, penalty_ref, response_out, label_out,
    points, offset_in, mag_in, response_ref, label_ref, penalty_in, sems,
):
    half = points.shape[0]
    c = core()
    pairs = [
        (x_hbm.at[pl.ds(pl.multiple_of(c * half, half), half), :], points),
        (label_hbm, label_ref), (response_hbm, response_ref), (w_hbm, w_ref),
        (offset_hbm, offset_in), (mag_hbm, mag_in), (penalty_hbm, penalty_in),
    ]
    copies = [pltpu.make_async_copy(a, b, sems.at[i]) for i, (a, b) in enumerate(pairs)]
    for copy in copies:
        copy.start()
    for copy in copies:
        copy.wait()
    msg[:half, :] = points[...]
    msg[half:, :] = jnp.zeros_like(msg[half:, :])
    label_out[...] = label_ref[...]
    response_out[...] = response_ref[...]
    offset_ref[...] = offset_in[...] * TURN
    mag_ref[...] = mag_in[...] * scale
    levels, rows = penalty_in.shape[1], penalty_ref.shape[0]
    row, column = [lax.broadcasted_iota(jnp.int32, (rows, levels), a) for a in (0, 1)]
    chosen = column == lax.axis_index("samp") * (rows // 2) + lax.rem(row, rows // 2)
    penalty_ref[...] = row_sum(jnp.where(chosen, penalty_in[...], 0.0))


def label_kernel(half, points, label, other_label, response, msg):
    n = half // LANES
    c = core()

    def mine(block):
        return jnp.where(c == 0, block[:n], block[n:])

    own = (mine(label[...]) != 0).astype(f32)
    other = (mine(other_label[...]) != 0).astype(f32)
    y = mine(response[...])
    high, middle = halves(y)
    y = y - high.astype(f32)
    middle, low = halves(y)
    aux = [jnp.where(c == 0, own, other), jnp.where(c == 0, other, own)]
    aux += [v.astype(f32) for v in (high, middle, low)]
    aux += [jnp.zeros((msg.shape[0] - half - 5 * n, LANES), f32)]
    msg[half:, :] = jnp.concatenate(aux, axis=0).astype(bf16)


def features_kernel(first, msg, w_ref, offset_ref, *refs):
    before, refs = (None, refs) if first else (refs[0], refs[1:])
    high_ref, low_ref, high_t, low_t, kept_ref, moment_ref, acc, mask = refs
    samples, features = high_ref.shape
    n = samples // LANES
    aux = msg[samples:, :].astype(f32)
    kept = jnp.concatenate([as_row(aux[e * n : (e + 1) * n]) for e in (0, 1)], axis=0)
    kept_ref[...] = spread(kept, kept_ref.shape[0])
    y = (aux[2 * n : 3 * n] + aux[3 * n : 4 * n]) + aux[4 * n : 5 * n]
    y_high, y_low = halves(kept * as_row(y))
    y_both = jnp.concatenate([y_high.astype(f32), y_low.astype(f32)], axis=0).astype(bf16)
    columns = jnp.concatenate([kept, jnp.zeros((6, samples), f32)], axis=0).T
    for e in (0, 1):
        mask[e] = jnp.broadcast_to(columns[:, e : e + 1], (samples, LANES))
    cb = min(features, 256)
    for j in range(0, features, cb):
        a = jnp.dot(msg[:samples, :], w_ref[:, j : j + cb], preferred_element_type=f32)
        t = a * TURN + offset_ref[:, j : j + cb]
        r = t - jnp.round(t)
        q = jnp.abs(r) - 0.25
        u = q * q
        c = jnp.full_like(u, SINE[-1])
        for k in SINE[-2::-1]:
            c = c * u + k
        c = c * q
        high, low = halves(c)
        high_ref[:, j : j + cb] = high
        low_ref[:, j : j + cb] = low
        high_t[j : j + cb, :] = high.T
        low_t[j : j + cb, :] = low.T
        square = c * c
        for e in (0, 1):
            part = square * jnp.concatenate([mask[e]] * (cb // LANES), axis=1)
            acc[e, :, j : j + cb] = part.reshape(samples // 8, 8, cb).sum(0)
        side = jnp.dot(y_both, high, preferred_element_type=f32)
        side = side[:2] + side[2:] + jnp.dot(y_high, low, preferred_element_type=f32)
        moment_ref[2:4, j : j + cb] = side if first else before[2:4, j : j + cb] + side
    for e in (0, 1):
        square = jnp.sum(acc[e], axis=0, keepdims=True)
        moment_ref[e : e + 1, :] = square if first else before[e : e + 1, :] + square


def send_forward(s, m, blocks, msg, scalars):
    v = s * m
    at = 0
    for high, low in zip(blocks[::2], blocks[1::2]):
        n = high.shape[1]
        msg[:, at : at + n] = product(v, high, low)
        at += n
    msg[:, at:] = pack_scalars(scalars, s.shape[0])


def begin_kernel(nz, *refs):
    moments, penalty, mag, blocks = refs[:2], refs[2], refs[3], refs[4 : 4 + 2 * nz]
    msg, direction, precond, residual = refs[4 + 2 * nz :]
    sums = total(moments)
    m = mag[...]
    rows = penalty.shape[0]
    pre = spread(sums[0:2] * (m * m), rows) + penalty[...]
    res = spread(sums[2:4] * m, rows)
    s = res / pre
    precond[...] = pre
    residual[...] = res
    direction[...] = s
    send_forward(s, m, blocks, msg, [row_sum(res * s), row_sum(s * s)])


def adjoint_kernel(ny, nz, first, *refs):
    parts, refs = refs[:ny], refs[ny:]
    kepts, blocks, refs = refs[:nz], refs[nz : 3 * nz], refs[3 * nz :]
    sums = total(parts)
    half = kepts[0].shape[1]
    samples = half * nz
    image_rows, sc = sums[:, :samples], sums[:, samples:]
    rz, dd = sc[:, 0:1], sc[:, 1:2]
    beta = jnp.zeros_like(rz)
    if not first:
        before, before_sc, refs = refs[0], refs[1], refs[2:]
        beta = rz / before_sc[:, 0:1]
        image_rows = image_rows + beta * before[...]
        dd = dd + 2.0 * beta * sc[:, 2:3] + beta * beta * before_sc[:, 1:2]
    msg, rows_out, sc_out = refs
    squares = jnp.zeros_like(dd)
    adjoint = 0.0
    for j, (kept, high, low) in enumerate(zip(kepts, blocks[::2], blocks[1::2])):
        rows = image_rows[:, j * half : (j + 1) * half]
        weighted = rows * kept[...]
        squares = squares + row_sum(weighted * rows)
        adjoint = adjoint + product(weighted, high, low)
    msg[:, : adjoint.shape[1]] = adjoint
    msg[:, adjoint.shape[1] :] = pack_scalars([squares], dd.shape[0])
    rows_out[...] = image_rows
    sc_out[...] = pack_scalars([rz, dd, beta], dd.shape[0])


def update_kernel(nz, first, *refs):
    parts, refs = refs[:2], refs[2:]
    sc, penalty, mag, precond, residual, scaled, rows, refs = *refs[:7], refs[7:]
    blocks, refs = refs[: 2 * nz], refs[2 * nz :]
    sums = total(parts)
    features = mag.shape[1]
    lam, m = penalty[...], mag[...]
    direction = scaled[...]
    if not first:
        (before, weights, predicted), refs = refs[:3], refs[3:]
    (msg, scaled_out, direction_out, weights_out, predicted_out), refs = refs[:5], refs[5:]
    if not first:
        direction = direction + sc[:, 2:3] * before[...]
    image = sums[:, :features] * m + lam * direction
    step = sc[:, 0:1] / (sums[:, features : features + 1] + lam * sc[:, 1:2])
    moved, fitted = step * direction, step * rows[...]
    weights_out[...] = moved if first else weights[...] + moved
    predicted_out[...] = fitted if first else predicted[...] + fitted
    res = residual[...] - step * image
    s = res / precond[...]
    for residual_out in refs:
        residual_out[...] = res
    scaled_out[...] = s
    direction_out[...] = direction
    send_forward(s, m, blocks, msg, [row_sum(res * s), row_sum(s * s), row_sum(s * direction)])


def fold_rows(value, fold):
    n = value.shape[0] // 2
    return jnp.where(fold == 0, value[:n], value[n:])


def last_kernel(ny, nz, *refs):
    parts, refs = refs[:ny], refs[ny:]
    kepts, (before, before_sc, predicted, msg, rows_out, sc_out) = refs[:nz], refs[nz:]
    sums = total(parts)
    half = kepts[0].shape[1]
    samples = half * nz
    sc = sums[:, samples:]
    rz = sc[:, 0:1]
    beta = rz / before_sc[:, 0:1]
    image_rows = sums[:, :samples] + beta * before[...]
    dd = sc[:, 1:2] + 2.0 * beta * sc[:, 2:3] + beta * beta * before_sc[:, 1:2]
    squares = jnp.zeros_like(dd)
    for j, kept in enumerate(kepts):
        rows = image_rows[:, j * half : (j + 1) * half]
        squares = squares + row_sum(rows * rows * kept[...])
    other = 1 - core()
    n = dd.shape[0] // 2
    msg[:n, :samples] = fold_rows(image_rows, other)
    msg[n:, :samples] = fold_rows(predicted[...], other)
    msg[:, samples:] = pack_scalars([squares], 2 * n)
    rows_out[...] = image_rows
    sc_out[...] = pack_scalars([rz, dd, beta], 2 * n)


def finish_kernel(nz, own, got, sc, penalty, scaled, before, weights, rows, predicted, *outs):
    samples, features = rows.shape[1], scaled.shape[1]
    half = samples // nz
    c = core()
    n = sc.shape[0] // 2
    step = sc[:, 0:1] / ((own[:, samples : samples + 1] + got[:, samples : samples + 1]) + penalty[...] * sc[:, 1:2])
    coefficients = weights[...] + step * (scaled[...] + sc[:, 2:3] * before[...])
    coefficients = fold_rows(coefficients, c)
    here = fold_rows(predicted[...] + step * rows[...], c)
    there = got[n:, :samples] + fold_rows(step, c) * got[:n, :samples]
    lower, upper = jnp.where(c == 0, here, there), jnp.where(c == 0, there, here)
    for j, out in enumerate(outs):
        out[:, :features] = coefficients
        out[:, features : features + half] = lower[:, j * half : (j + 1) * half]
        out[:, features + half :] = upper[:, j * half : (j + 1) * half]


def arrange_kernel(order, *refs):
    nz = len(order)
    parts, (weights_out, predictions_out, held) = refs[:nz], refs[nz:]
    features = weights_out.shape[1]
    n = weights_out.shape[0] // nz
    for j, part in zip(order, parts):
        held[j] = part[...]
    z = lax.axis_index("samp")
    for k in range(nz):
        part = held[lax.bitwise_xor(z, k)]
        weights_out[k * n : (k + 1) * n, :] = part[:, :features]
        predictions_out[k * n : (k + 1) * n, :] = part[:, features:]


ITERS = 3


def shards(
    nf,
    nz,
    ny,
    input_points,
    wave_numbers,
    offset_angles,
    feature_magnitudes,
    response_values,
    split_label,
    shrinkage_levels,
):
    shard, features = input_points.shape[0], wave_numbers.shape[1]
    depth = input_points.shape[1]
    levels = shrinkage_levels.shape[0]
    half, rows = shard // 2, 2 * (levels // nz)
    samples = half * nz
    tall = (shard // LANES, LANES)
    extra = pl.cdiv(5 * half // LANES, 16) * 16
    row_f, row_s, row_c = ((rows, features), f32), ((rows, samples), f32), ((rows, LANES), f32)
    msg_f, msg_s = ((rows, features + LANES), f32), ((rows, samples + LANES), f32)

    label = split_label.reshape(tall)
    other_label = flip(label, "fold", nf, 1)
    inputs = [input_points, wave_numbers, offset_angles.reshape(1, features), feature_magnitudes.reshape(1, features)]
    inputs += [response_values.reshape(tall), label, shrinkage_levels.reshape(1, levels)]
    vectors = [((1, features), f32), ((1, features), f32), (tall, f32), (tall, jnp.int32), ((1, levels), f32)]
    packed = ((half + extra, depth), bf16)
    msg, waves, offsets, mag, penalty, response, label = pl.pallas_call(
        functools.partial(pack_kernel, math.sqrt(2.0 / (features * ny))),
        out_shape=[
            pltpu.VMEM(*packed),
            pltpu.VMEM((depth, features), bf16),
            pltpu.VMEM((1, features), f32),
            pltpu.VMEM((1, features), f32),
            pltpu.VMEM((rows, 1), f32),
            pltpu.VMEM(tall, f32),
            pltpu.VMEM(tall, jnp.int32),
        ],
        in_specs=[pl.BlockSpec(memory_space=pltpu.HBM)] * len(inputs),
        scratch_shapes=[pltpu.VMEM((half, depth), bf16)]
        + [pltpu.VMEM(v, d) for v, d in vectors]
        + [pltpu.SemaphoreType.DMA((len(inputs),))],
        compiler_params=pltpu.CompilerParams(vmem_limit_bytes=VMEM_LIMIT),
    )(*[pltpu.with_memory_space_constraint(v, pltpu.HBM) for v in inputs])
    (msg,) = call(
        functools.partial(label_kernel, half), [packed], msg, label, other_label, response, aliases={0: 0}
    )

    order = [j ^ (j >> 1) for j in range(nz)]
    blocks, turned, kepts, moments = [], [], [], None
    tile, tile_t = ((half, features), bf16), ((features, half), bf16)
    for j in order:
        part = flip(msg, "samp", nz, j) if j else msg
        high, low, high_t, low_t, kept, moments = call(
            functools.partial(features_kernel, j == 0),
            [tile, tile, tile_t, tile_t, ((rows, half), f32), ((4, features), f32)],
            part, waves, offsets, *(() if j == 0 else (moments,)),
            scratch=[pltpu.VMEM((2, 8, features), f32), pltpu.VMEM((2, half, LANES), f32)],
            flops=60 * half * features,
        )
        blocks += [high, low]
        turned += [high_t, low_t]
        kepts.append(kept)
    msg, scaled, precond, residual = call(
        functools.partial(begin_kernel, nz),
        [msg_s, row_f, row_f, row_f],
        moments, flip(moments, "fold", nf, 1), penalty, mag, *turned,
    )
    before = weights = predicted = image_rows = sc = None
    for it in range(ITERS - 1):
        first = it == 0
        msg, image_rows, sc = call(
            functools.partial(adjoint_kernel, ny, nz, first),
            [msg_f, row_s, row_c],
            *exchange(msg, "feat", ny), *kepts, *blocks, *(() if first else (image_rows, sc)),
        )
        msg, scaled, before, weights, predicted, *rest = call(
            functools.partial(update_kernel, nz, first),
            [msg_s, row_f, row_f, row_f, row_s] + [row_f] * (it < ITERS - 2),
            msg, flip(msg, "fold", nf, 1), sc, penalty, mag, precond, residual, scaled, image_rows, *turned,
            *(() if first else (before, weights, predicted)),
        )
        residual = rest[0] if rest else None
    msg, image_rows, sc = call(
        functools.partial(last_kernel, ny, nz),
        [msg_s, row_s, row_c],
        *exchange(msg, "feat", ny), *kepts, image_rows, sc, predicted,
    )
    outs = call(
        functools.partial(finish_kernel, nz),
        [((rows // 2, features + shard), f32)] * nz,
        msg, flip(msg, "fold", nf, 1), sc, penalty, scaled, before, weights, image_rows, predicted,
    )
    outs = [flip(out, "samp", nz, j) if j else out for j, out in zip(order, outs)]
    return call(
        functools.partial(arrange_kernel, order),
        [((levels, features), f32), ((levels, shard), f32)],
        *outs,
        scratch=[pltpu.VMEM((nz, rows // 2, features + shard), f32)],
        held=False,
    )


def solution(mesh):
    placed = (
        P("samp", None),
        P(None, "feat"),
        P("feat"),
        P("feat"),
        P("samp"),
        P(("fold", "samp")),
        P(),
    )
    sizes = [mesh.shape[axis] for axis in ("fold", "samp", "feat")]
    return jax.shard_map(
        functools.partial(shards, *sizes),
        mesh=mesh,
        in_specs=placed,
        out_specs=(P("fold", "feat"), P("fold", "samp")),
        check_vma=False,
    )
```

```python
import functools
import math

import jax
import jax.numpy as jnp
from jax import lax
from jax.experimental import pallas as pl
from jax.experimental.pallas import tpu as pltpu
from jax.sharding import PartitionSpec as P

f32, bf16 = jnp.float32, jnp.bfloat16
TURN = 1.0 / (2.0 * math.pi)
SINE = (-6.283164044377446, 41.337142378931674, -81.34076911271806, 70.99343519544783)
LANES = 128
VMEM_LIMIT = 12 * 2**20


def call(body, outs, *args, flops=0, in_vmem=True, scratch=(), aliases={}):
    outs = [pltpu.VMEM(s, d) if in_vmem else jax.ShapeDtypeStruct(s, d) for s, d in outs]
    size = sum(math.prod(a.shape) * a.dtype.itemsize for a in args)
    return pl.pallas_call(
        body,
        out_shape=outs,
        scratch_shapes=list(scratch),
        input_output_aliases=aliases,
        compiler_params=pltpu.CompilerParams(vmem_limit_bytes=VMEM_LIMIT),
        cost_estimate=pl.CostEstimate(flops=flops, bytes_accessed=size, transcendentals=0),
    )(*args)


def total(refs):
    values = [r[...] for r in refs]
    while len(values) > 1:
        values = [values[i] + values[i + 1] for i in range(0, len(values), 2)]
    return values[0]


def halves(value):
    high = value.astype(bf16)
    return high, (value - high.astype(f32)).astype(bf16)


def product(rows, high_ref, low_ref):
    high, low = halves(rows)
    n = rows.shape[0]
    both = jnp.concatenate([high.astype(f32), low.astype(f32)], axis=0).astype(bf16)
    out = jnp.dot(both, high_ref[...], preferred_element_type=f32)
    out = out + jnp.dot(both, low_ref[...], preferred_element_type=f32)
    return out[:n] + out[n:]


def held(scaled, mag):
    high, low = halves(scaled * mag)
    rounded = high.astype(f32) + low.astype(f32)
    return rounded / mag, rounded


def pack_scalars(columns, rows):
    lane = lax.broadcasted_iota(jnp.int32, (rows, LANES), 1)
    out = jnp.zeros((rows, LANES), f32)
    for i, column in enumerate(columns):
        out = jnp.where(lane == i, column, out)
    return out


def row_sum(value):
    return jnp.sum(value, axis=1, keepdims=True)


def flip(value, axis, n, s):
    return lax.ppermute(value, axis, [(i, i ^ s) for i in range(n)])


def exchange(value, axis, n):
    return [value] + [flip(value, axis, n, s) for s in range(1, n)]


def as_row(block):
    return jnp.concatenate([block[i : i + 1] for i in range(block.shape[0])], axis=1)


def spread(pair, rows):
    return jnp.concatenate(
        [jnp.broadcast_to(pair[e : e + 1], (rows // 2, pair.shape[1])) for e in (0, 1)], axis=0
    )


def core():
    return lax.rem(lax.axis_index("fold"), 2)


def pack_kernel(
    scale, x_hbm, w_hbm, offset_hbm, mag_hbm, response_hbm, label_hbm, penalty_hbm,
    msg, w_ref, offset_ref, mag_ref, penalty_ref, response_out, label_out,
    points, offset_in, mag_in, response_ref, label_ref, penalty_in, sems,
):
    half = points.shape[0]
    c = core()
    pairs = [
        (x_hbm.at[pl.ds(pl.multiple_of(c * half, half), half), :], points),
        (label_hbm, label_ref), (response_hbm, response_ref), (w_hbm, w_ref),
        (offset_hbm, offset_in), (mag_hbm, mag_in), (penalty_hbm, penalty_in),
    ]
    copies = [pltpu.make_async_copy(a, b, sems.at[i]) for i, (a, b) in enumerate(pairs)]
    for copy in copies:
        copy.start()
    for copy in copies:
        copy.wait()
    msg[:half, :] = points[...]
    msg[half:, :] = jnp.zeros_like(msg[half:, :])
    label_out[...] = label_ref[...]
    response_out[...] = response_ref[...]
    offset_ref[...] = offset_in[...] * TURN
    mag_ref[...] = mag_in[...] * scale
    levels, rows = penalty_in.shape[1], penalty_ref.shape[0]
    row, column = [lax.broadcasted_iota(jnp.int32, (rows, levels), a) for a in (0, 1)]
    chosen = column == lax.axis_index("samp") * (rows // 2) + lax.rem(row, rows // 2)
    penalty_ref[...] = row_sum(jnp.where(chosen, penalty_in[...], 0.0))


def label_kernel(half, points, label, other_label, response, msg):
    n = half // LANES
    c = core()

    def mine(block):
        return jnp.where(c == 0, block[:n], block[n:])

    own = (mine(label[...]) != 0).astype(f32)
    other = (mine(other_label[...]) != 0).astype(f32)
    y = mine(response[...])
    high, middle = halves(y)
    y = y - high.astype(f32)
    middle, low = halves(y)
    aux = [jnp.where(c == 0, own, other), jnp.where(c == 0, other, own)]
    aux += [v.astype(f32) for v in (high, middle, low)]
    aux += [jnp.zeros((msg.shape[0] - half - 5 * n, LANES), f32)]
    msg[half:, :] = jnp.concatenate(aux, axis=0).astype(bf16)


def features_kernel(first, msg, w_ref, offset_ref, *refs):
    before, refs = (None, refs) if first else (refs[0], refs[1:])
    high_ref, low_ref, high_t, low_t, kept_ref, moment_ref, acc, mask = refs
    samples, features = high_ref.shape
    n = samples // LANES
    aux = msg[samples:, :].astype(f32)
    kept = jnp.concatenate([as_row(aux[e * n : (e + 1) * n]) for e in (0, 1)], axis=0)
    kept_ref[...] = spread(kept, kept_ref.shape[0])
    y = (aux[2 * n : 3 * n] + aux[3 * n : 4 * n]) + aux[4 * n : 5 * n]
    y_high, y_low = halves(kept * as_row(y))
    y_both = jnp.concatenate([y_high.astype(f32), y_low.astype(f32)], axis=0).astype(bf16)
    columns = jnp.concatenate([kept, jnp.zeros((6, samples), f32)], axis=0).T
    for e in (0, 1):
        mask[e] = jnp.broadcast_to(columns[:, e : e + 1], (samples, LANES))
    cb = min(features, 256)
    for j in range(0, features, cb):
        a = jnp.dot(msg[:samples, :], w_ref[:, j : j + cb], preferred_element_type=f32)
        t = a * TURN + offset_ref[:, j : j + cb]
        r = t - jnp.round(t)
        q = jnp.abs(r) - 0.25
        u = q * q
        c = jnp.full_like(u, SINE[-1])
        for k in SINE[-2::-1]:
            c = c * u + k
        c = c * q
        high, low = halves(c)
        high_ref[:, j : j + cb] = high
        low_ref[:, j : j + cb] = low
        high_t[j : j + cb, :] = high.T
        low_t[j : j + cb, :] = low.T
        square = c * c
        for e in (0, 1):
            part = square * jnp.concatenate([mask[e]] * (cb // LANES), axis=1)
            acc[e, :, j : j + cb] = part.reshape(samples // 8, 8, cb).sum(0)
        side = jnp.dot(y_both, high, preferred_element_type=f32)
        side = side[:2] + side[2:] + jnp.dot(y_high, low, preferred_element_type=f32)
        moment_ref[2:4, j : j + cb] = side if first else before[2:4, j : j + cb] + side
    for e in (0, 1):
        square = jnp.sum(acc[e], axis=0, keepdims=True)
        moment_ref[e : e + 1, :] = square if first else before[e : e + 1, :] + square


def forward(v, blocks, msg):
    at = 0
    for high, low in zip(blocks[::2], blocks[1::2]):
        n = high.shape[1]
        msg[:, at : at + n] = product(v, high, low)
        at += n
    return at


def send_forward(v, blocks, msg, scalars):
    at = forward(v, blocks, msg)
    msg[:, at:] = pack_scalars(scalars, v.shape[0])


def forward_kernel(scaled, mag, *refs):
    forward(scaled[...] * mag[...], refs[:-1], refs[-1])


def begin_kernel(count, *refs):
    moments, penalty, mag, blocks = refs[:2], refs[2], refs[3], refs[4 : 4 + 2 * count]
    msg, direction, precond, residual = refs[4 + 2 * count :]
    sums = total(moments)
    m = mag[...]
    rows = penalty.shape[0]
    pre = spread(sums[0:2] * (m * m), rows) + penalty[...]
    res = spread(sums[2:4] * m, rows)
    s, v = held(res / pre, m)
    precond[...] = pre
    residual[...] = res
    direction[...] = s
    send_forward(v, blocks, msg, [row_sum(res * s), row_sum(s * s)])


def direction_scalars(sc, before_sc):
    rz, dd = sc[:, 0:1], sc[:, 1:2]
    if before_sc is None:
        return rz, dd, jnp.zeros_like(rz)
    beta = rz / before_sc[:, 0:1]
    return rz, dd + 2.0 * beta * sc[:, 2:3] + beta * beta * before_sc[:, 1:2], beta


def adjoint(image_rows, kepts, blocks):
    half = kepts[0].shape[1]
    squares, out = 0.0, 0.0
    for j, (kept, high, low) in enumerate(zip(kepts, blocks[::2], blocks[1::2])):
        rows = image_rows[:, j * half : (j + 1) * half]
        weighted = rows * kept[...]
        squares = squares + row_sum(weighted * rows)
        out = out + product(weighted, high, low)
    return out, squares


def adjoint_kernel(ny, count, first, *refs):
    parts, refs = refs[:ny], refs[ny:]
    kepts, blocks, refs = refs[:count], refs[count : 3 * count], refs[3 * count :]
    sums = total(parts)
    samples = kepts[0].shape[1] * count
    image_rows, sc = sums[:, :samples], sums[:, samples:]
    before, before_sc = (None, None) if first else refs[:2]
    partial, rows_out, sc_out = refs[-3:]
    rz, dd, beta = direction_scalars(sc, before_sc)
    if not first:
        image_rows = image_rows + beta * before[...]
    out, squares = adjoint(image_rows, kepts, blocks)
    partial[...] = out
    rows_out[...] = image_rows
    sc_out[...] = pack_scalars([rz, dd, beta, squares], dd.shape[0])


def rest_kernel(ny, count, first, *refs):
    parts, refs = refs[:ny], refs[ny:]
    kepts, blocks, refs = refs[:count], refs[count : 3 * count], refs[3 * count :]
    sc, partial, refs = refs[0], refs[1], refs[2:]
    image_rows = total(parts)
    if not first:
        image_rows = image_rows + sc[:, 2:3] * refs[0][...]
    msg, rows_out = refs[-2:]
    out, squares = adjoint(image_rows, kepts, blocks)
    features = out.shape[1]
    msg[:, :features] = partial[...] + out
    msg[:, features:] = pack_scalars([sc[:, 3:4] + squares], out.shape[0])
    rows_out[...] = image_rows


def update_kernel(count, first, *refs):
    parts, refs = refs[:2], refs[2:]
    sc, penalty, mag, precond, residual, scaled, rows, rest, refs = *refs[:8], refs[8:]
    blocks, refs = refs[: 2 * count], refs[2 * count :]
    sums = total(parts)
    features = mag.shape[1]
    lam, m = penalty[...], mag[...]
    direction = scaled[...]
    if not first:
        (before, weights, predicted), refs = refs[:3], refs[3:]
    (msg, scaled_out, direction_out, weights_out, predicted_out), refs = refs[:5], refs[5:]
    if not first:
        direction = direction + sc[:, 2:3] * before[...]
    image = sums[:, :features] * m + lam * direction
    step = sc[:, 0:1] / (sums[:, features : features + 1] + lam * sc[:, 1:2])
    moved, fitted = step * direction, step * jnp.concatenate([rows[...], rest[...]], axis=1)
    weights_out[...] = moved if first else weights[...] + moved
    predicted_out[...] = fitted if first else predicted[...] + fitted
    res = residual[...] - step * image
    s, v = held(res / precond[...], m)
    for residual_out in refs:
        residual_out[...] = res
    scaled_out[...] = s
    direction_out[...] = direction
    send_forward(v, blocks, msg, [row_sum(res * s), row_sum(s * s), row_sum(s * direction)])


def fold_rows(value, fold):
    n = value.shape[0] // 2
    return jnp.where(fold == 0, value[:n], value[n:])


def last_kernel(ny, nz, *refs):
    parts, refs = refs[:ny], refs[ny:]
    kepts, (before, before_rest, before_sc, predicted, msg, rows_out, sc_out) = refs[:nz], refs[nz:]
    sums = total(parts)
    half = kepts[0].shape[1]
    samples = half * nz
    rz, dd, beta = direction_scalars(sums[:, samples:], before_sc)
    image_rows = sums[:, :samples] + beta * jnp.concatenate([before[...], before_rest[...]], axis=1)
    squares = jnp.zeros_like(dd)
    for j, kept in enumerate(kepts):
        rows = image_rows[:, j * half : (j + 1) * half]
        squares = squares + row_sum(rows * rows * kept[...])
    other = 1 - core()
    n = dd.shape[0] // 2
    msg[:n, :samples] = fold_rows(image_rows, other)
    msg[n:, :samples] = fold_rows(predicted[...], other)
    msg[:, samples:] = pack_scalars([squares], 2 * n)
    rows_out[...] = image_rows
    sc_out[...] = pack_scalars([rz, dd, beta], 2 * n)


def finish_kernel(nz, own, got, sc, penalty, scaled, before, weights, rows, predicted, *outs):
    samples, features = rows.shape[1], scaled.shape[1]
    half = samples // nz
    c = core()
    n = sc.shape[0] // 2
    step = sc[:, 0:1] / ((own[:, samples : samples + 1] + got[:, samples : samples + 1]) + penalty[...] * sc[:, 1:2])
    coefficients = weights[...] + step * (scaled[...] + sc[:, 2:3] * before[...])
    coefficients = fold_rows(coefficients, c)
    here = fold_rows(predicted[...] + step * rows[...], c)
    there = got[n:, :samples] + fold_rows(step, c) * got[:n, :samples]
    lower, upper = jnp.where(c == 0, here, there), jnp.where(c == 0, there, here)
    for j, out in enumerate(outs):
        out[:, :features] = coefficients
        out[:, features : features + half] = lower[:, j * half : (j + 1) * half]
        out[:, features + half :] = upper[:, j * half : (j + 1) * half]


def arrange_kernel(order, *refs):
    nz = len(order)
    parts, (weights_out, predictions_out, held) = refs[:nz], refs[nz:]
    features = weights_out.shape[1]
    n = weights_out.shape[0] // nz
    for j, part in zip(order, parts):
        held[j] = part[...]
    z = lax.axis_index("samp")
    for k in range(nz):
        part = held[lax.bitwise_xor(z, k)]
        weights_out[k * n : (k + 1) * n, :] = part[:, :features]
        predictions_out[k * n : (k + 1) * n, :] = part[:, features:]


ITERS = 3


def shards(
    nf,
    nz,
    ny,
    input_points,
    wave_numbers,
    offset_angles,
    feature_magnitudes,
    response_values,
    split_label,
    shrinkage_levels,
):
    shard, features = input_points.shape[0], wave_numbers.shape[1]
    depth = input_points.shape[1]
    levels = shrinkage_levels.shape[0]
    half, rows = shard // 2, 2 * (levels // nz)
    samples = half * nz
    tall = (shard // LANES, LANES)
    extra = pl.cdiv(5 * half // LANES, 16) * 16
    row_f, row_s, row_c = ((rows, features), f32), ((rows, samples), f32), ((rows, LANES), f32)
    msg_f, msg_s = ((rows, features + LANES), f32), ((rows, samples + LANES), f32)

    label = split_label.reshape(tall)
    other_label = flip(label, "fold", nf, 1)
    inputs = [input_points, wave_numbers, offset_angles.reshape(1, features), feature_magnitudes.reshape(1, features)]
    inputs += [response_values.reshape(tall), label, shrinkage_levels.reshape(1, levels)]
    vectors = [((1, features), f32), ((1, features), f32), (tall, f32), (tall, jnp.int32), ((1, levels), f32)]
    packed = ((half + extra, depth), bf16)
    msg, waves, offsets, mag, penalty, response, label = pl.pallas_call(
        functools.partial(pack_kernel, math.sqrt(2.0 / (features * ny))),
        out_shape=[
            pltpu.VMEM(*packed),
            pltpu.VMEM((depth, features), bf16),
            pltpu.VMEM((1, features), f32),
            pltpu.VMEM((1, features), f32),
            pltpu.VMEM((rows, 1), f32),
            pltpu.VMEM(tall, f32),
            pltpu.VMEM(tall, jnp.int32),
        ],
        in_specs=[pl.BlockSpec(memory_space=pltpu.HBM)] * len(inputs),
        scratch_shapes=[pltpu.VMEM((half, depth), bf16)]
        + [pltpu.VMEM(v, d) for v, d in vectors]
        + [pltpu.SemaphoreType.DMA((len(inputs),))],
        compiler_params=pltpu.CompilerParams(vmem_limit_bytes=VMEM_LIMIT),
    )(*[pltpu.with_memory_space_constraint(v, pltpu.HBM) for v in inputs])
    (msg,) = call(
        functools.partial(label_kernel, half), [packed], msg, label, other_label, response, aliases={0: 0}
    )

    order = [j ^ (j >> 1) for j in range(nz)]
    blocks, turned, kepts, moments = [], [], [], None
    tile, tile_t = ((half, features), bf16), ((features, half), bf16)
    for j in order:
        part = flip(msg, "samp", nz, j) if j else msg
        high, low, high_t, low_t, kept, moments = call(
            functools.partial(features_kernel, j == 0),
            [tile, tile, tile_t, tile_t, ((rows, half), f32), ((4, features), f32)],
            part, waves, offsets, *(() if j == 0 else (moments,)),
            scratch=[pltpu.VMEM((2, 8, features), f32), pltpu.VMEM((2, half, LANES), f32)],
            flops=60 * half * features,
        )
        blocks += [high, low]
        turned += [high_t, low_t]
        kepts.append(kept)
    count, later = nz - 1, 1
    msg_a, row_a = ((rows, half * count + LANES), f32), ((rows, half * count), f32)
    row_b = ((rows, half * later), f32)
    work = 2 * 3 * rows * half * features
    msg, scaled, precond, residual = call(
        functools.partial(begin_kernel, count),
        [msg_a, row_f, row_f, row_f],
        moments, flip(moments, "fold", nf, 1), penalty, mag, *turned[: 2 * count],
        flops=work * count,
    )
    before = weights = predicted = sc = rows_a = rows_b = None
    for it in range(ITERS - 1):
        first, last = it == 0, it == ITERS - 2
        parts = exchange(msg, "feat", ny)
        (msg_b,) = call(forward_kernel, [row_b], scaled, mag, *turned[2 * count :], flops=work * later)
        parts_b = exchange(msg_b, "feat", ny)
        partial, new_a, new_sc = call(
            functools.partial(adjoint_kernel, ny, count, first),
            [row_f, row_a, row_c],
            *parts, *kepts[:count], *blocks[: 2 * count], *(() if first else (rows_a, sc)),
            flops=work * count,
        )
        msg, rows_b = call(
            functools.partial(rest_kernel, ny, later, first),
            [msg_f, row_b],
            *parts_b, *kepts[count:], *blocks[2 * count :], new_sc, partial, *(() if first else (rows_b,)),
            flops=work * later,
        )
        rows_a, sc = new_a, new_sc
        msg, scaled, before, weights, predicted, *rest = call(
            functools.partial(update_kernel, nz if last else count, first),
            [msg_s if last else msg_a, row_f, row_f, row_f, row_s] + [row_f] * (not last),
            msg, flip(msg, "fold", nf, 1), sc, penalty, mag, precond, residual, scaled, rows_a, rows_b,
            *(turned if last else turned[: 2 * count]),
            *(() if first else (before, weights, predicted)),
            flops=work * count,
        )
        residual = rest[0] if rest else None
    msg, image_rows, sc = call(
        functools.partial(last_kernel, ny, nz),
        [msg_s, row_s, row_c],
        *exchange(msg, "feat", ny), *kepts, rows_a, rows_b, sc, predicted,
    )
    outs = call(
        functools.partial(finish_kernel, nz),
        [((rows // 2, features + shard), f32)] * nz,
        msg, flip(msg, "fold", nf, 1), sc, penalty, scaled, before, weights, image_rows, predicted,
    )
    far_first = [0] + sorted(range(1, nz), key=lambda j: -j.bit_length())
    outs = [flip(outs[order.index(j)], "samp", nz, j) if j else outs[0] for j in far_first]
    return call(
        functools.partial(arrange_kernel, far_first),
        [((levels, features), f32), ((levels, shard), f32)],
        *outs,
        scratch=[pltpu.VMEM((nz, rows // 2, features + shard), f32)],
        in_vmem=False,
    )


def solution(mesh):
    placed = (
        P("samp", None),
        P(None, "feat"),
        P("feat"),
        P("feat"),
        P("samp"),
        P(("fold", "samp")),
        P(),
    )
    sizes = [mesh.shape[axis] for axis in ("fold", "samp", "feat")]
    return jax.shard_map(
        functools.partial(shards, *sizes),
        mesh=mesh,
        in_specs=placed,
        out_specs=(P("fold", "feat"), P("fold", "samp")),
        check_vma=False,
    )
```

```python
import functools
import math

import jax
import jax.numpy as jnp
from jax import lax
from jax.experimental import pallas as pl
from jax.experimental.pallas import tpu as pltpu
from jax.sharding import PartitionSpec as P

f32, bf16 = jnp.float32, jnp.bfloat16
TURN = 1.0 / (2.0 * math.pi)
SINE = (-6.283164044377446, 41.337142378931674, -81.34076911271806, 70.99343519544783)
LANES = 128
VMEM_LIMIT = 12 * 2**20


def call(body, outs, *args, flops=0, in_vmem=True, scratch=(), aliases={}):
    outs = [pltpu.VMEM(s, d) if in_vmem else jax.ShapeDtypeStruct(s, d) for s, d in outs]
    size = sum(math.prod(a.shape) * a.dtype.itemsize for a in args)
    return pl.pallas_call(
        body,
        out_shape=outs,
        scratch_shapes=list(scratch),
        input_output_aliases=aliases,
        compiler_params=pltpu.CompilerParams(vmem_limit_bytes=VMEM_LIMIT),
        cost_estimate=pl.CostEstimate(flops=flops, bytes_accessed=size, transcendentals=0),
    )(*args)


def total(refs):
    values = [r[...] for r in refs]
    while len(values) > 1:
        values = [values[i] + values[i + 1] for i in range(0, len(values), 2)]
    return values[0]


def halves(value):
    high = value.astype(bf16)
    return high, (value - high.astype(f32)).astype(bf16)


def product(rows, high_ref, low_ref):
    high, low = halves(rows)
    n = rows.shape[0]
    both = jnp.concatenate([high.astype(f32), low.astype(f32)], axis=0).astype(bf16)
    out = jnp.dot(both, high_ref[...], preferred_element_type=f32)
    out = out + jnp.dot(both, low_ref[...], preferred_element_type=f32)
    return out[:n] + out[n:]


def held(scaled, mag):
    high, low = halves(scaled * mag)
    rounded = high.astype(f32) + low.astype(f32)
    return rounded / mag, rounded


def pack_scalars(columns, rows):
    lane = lax.broadcasted_iota(jnp.int32, (rows, LANES), 1)
    out = jnp.zeros((rows, LANES), f32)
    for i, column in enumerate(columns):
        out = jnp.where(lane == i, column, out)
    return out


def row_sum(value):
    return jnp.sum(value, axis=1, keepdims=True)


def flip(value, axis, n, s):
    return lax.ppermute(value, axis, [(i, i ^ s) for i in range(n)])


def exchange(value, axis, n):
    return [value] + [flip(value, axis, n, s) for s in range(1, n)]


def as_row(block):
    return jnp.concatenate([block[i : i + 1] for i in range(block.shape[0])], axis=1)


def spread(pair, rows):
    return jnp.concatenate(
        [jnp.broadcast_to(pair[e : e + 1], (rows // 2, pair.shape[1])) for e in (0, 1)], axis=0
    )


def core():
    return lax.rem(lax.axis_index("fold"), 2)


def pack_kernel(
    scale, x_hbm, w_hbm, offset_hbm, mag_hbm, response_hbm, label_hbm, penalty_hbm,
    msg, w_ref, offset_ref, mag_ref, penalty_ref, response_out, label_out,
    points, offset_in, mag_in, response_ref, label_ref, penalty_in, sems,
):
    half = points.shape[0]
    c = core()
    pairs = [
        (x_hbm.at[pl.ds(pl.multiple_of(c * half, half), half), :], points),
        (label_hbm, label_ref), (response_hbm, response_ref), (w_hbm, w_ref),
        (offset_hbm, offset_in), (mag_hbm, mag_in), (penalty_hbm, penalty_in),
    ]
    copies = [pltpu.make_async_copy(a, b, sems.at[i]) for i, (a, b) in enumerate(pairs)]
    for copy in copies:
        copy.start()
    for copy in copies:
        copy.wait()
    msg[:half, :] = points[...]
    msg[half:, :] = jnp.zeros_like(msg[half:, :])
    label_out[...] = label_ref[...]
    response_out[...] = response_ref[...]
    offset_ref[...] = offset_in[...] * TURN
    mag_ref[...] = mag_in[...] * scale
    levels, rows = penalty_in.shape[1], penalty_ref.shape[0]
    row, column = [lax.broadcasted_iota(jnp.int32, (rows, levels), a) for a in (0, 1)]
    chosen = column == lax.axis_index("samp") * (rows // 2) + lax.rem(row, rows // 2)
    penalty_ref[...] = row_sum(jnp.where(chosen, penalty_in[...], 0.0))


def label_kernel(half, points, label, other_label, response, msg):
    n = half // LANES
    c = core()

    def mine(block):
        return jnp.where(c == 0, block[:n], block[n:])

    own = (mine(label[...]) != 0).astype(f32)
    other = (mine(other_label[...]) != 0).astype(f32)
    y = mine(response[...])
    high, middle = halves(y)
    y = y - high.astype(f32)
    middle, low = halves(y)
    aux = [jnp.where(c == 0, own, other), jnp.where(c == 0, other, own)]
    aux += [v.astype(f32) for v in (high, middle, low)]
    aux += [jnp.zeros((msg.shape[0] - half - 5 * n, LANES), f32)]
    msg[half:, :] = jnp.concatenate(aux, axis=0).astype(bf16)


def features_kernel(first, msg, w_ref, offset_ref, *refs):
    before, refs = (None, refs) if first else (refs[0], refs[1:])
    high_ref, low_ref, high_t, low_t, kept_ref, moment_ref, acc, mask = refs
    samples, features = high_ref.shape
    n = samples // LANES
    aux = msg[samples:, :].astype(f32)
    kept = jnp.concatenate([as_row(aux[e * n : (e + 1) * n]) for e in (0, 1)], axis=0)
    kept_ref[...] = spread(kept, kept_ref.shape[0])
    y = (aux[2 * n : 3 * n] + aux[3 * n : 4 * n]) + aux[4 * n : 5 * n]
    y_high, y_low = halves(kept * as_row(y))
    y_both = jnp.concatenate([y_high.astype(f32), y_low.astype(f32)], axis=0).astype(bf16)
    columns = jnp.concatenate([kept, jnp.zeros((6, samples), f32)], axis=0).T
    for e in (0, 1):
        mask[e] = jnp.broadcast_to(columns[:, e : e + 1], (samples, LANES))
    cb = min(features, 256)
    for j in range(0, features, cb):
        a = jnp.dot(msg[:samples, :], w_ref[:, j : j + cb], preferred_element_type=f32)
        t = a * TURN + offset_ref[:, j : j + cb]
        r = t - jnp.round(t)
        q = jnp.abs(r) - 0.25
        u = q * q
        c = jnp.full_like(u, SINE[-1])
        for k in SINE[-2::-1]:
            c = c * u + k
        c = c * q
        high, low = halves(c)
        high_ref[:, j : j + cb] = high
        low_ref[:, j : j + cb] = low
        high_t[j : j + cb, :] = high.T
        low_t[j : j + cb, :] = low.T
        square = c * c
        for e in (0, 1):
            part = square * jnp.concatenate([mask[e]] * (cb // LANES), axis=1)
            acc[e, :, j : j + cb] = part.reshape(samples // 8, 8, cb).sum(0)
        side = jnp.dot(y_both, high, preferred_element_type=f32)
        side = side[:2] + side[2:] + jnp.dot(y_high, low, preferred_element_type=f32)
        moment_ref[2:4, j : j + cb] = side if first else before[2:4, j : j + cb] + side
    for e in (0, 1):
        square = jnp.sum(acc[e], axis=0, keepdims=True)
        moment_ref[e : e + 1, :] = square if first else before[e : e + 1, :] + square


def forward(v, blocks, msg):
    at = 0
    for high, low in zip(blocks[::2], blocks[1::2]):
        n = high.shape[1]
        msg[:, at : at + n] = product(v, high, low)
        at += n
    return at


def send_forward(v, blocks, msg, scalars):
    at = forward(v, blocks, msg)
    msg[:, at:] = pack_scalars(scalars, v.shape[0])


def forward_kernel(scaled, mag, *refs):
    forward(scaled[...] * mag[...], refs[:-1], refs[-1])


def begin_kernel(count, *refs):
    moments, penalty, mag, blocks = refs[:2], refs[2], refs[3], refs[4 : 4 + 2 * count]
    msg, direction, precond, residual = refs[4 + 2 * count :]
    sums = total(moments)
    m = mag[...]
    rows = penalty.shape[0]
    pre = spread(sums[0:2] * (m * m), rows) + penalty[...]
    res = spread(sums[2:4] * m, rows)
    s, v = held(res / pre, m)
    precond[...] = pre
    residual[...] = res
    direction[...] = s
    send_forward(v, blocks, msg, [row_sum(res * s), row_sum(s * s)])


def direction_scalars(sc, before_sc):
    rz, dd = sc[:, 0:1], sc[:, 1:2]
    if before_sc is None:
        return rz, dd, jnp.zeros_like(rz), jnp.zeros_like(rz)
    beta = rz / before_sc[:, 0:1]
    dot = sc[:, 2:3] + beta * before_sc[:, 1:2]
    return rz, dd + beta * (sc[:, 2:3] + dot), beta, dot


def adjoint(image_rows, before, kepts, blocks):
    half = kepts[0].shape[1]
    out = 0.0
    squares = cross = jnp.zeros((image_rows.shape[0], 1), f32)
    for j, (kept, high, low) in enumerate(zip(kepts, blocks[::2], blocks[1::2])):
        at = slice(j * half, (j + 1) * half)
        rows = image_rows[:, at]
        weighted = rows * kept[...]
        squares = squares + row_sum(weighted * rows)
        if before is not None:
            cross = cross + row_sum(weighted * before[:, at])
        out = out + product(weighted, high, low)
    return out, squares, cross


def adjoint_kernel(ny, count, first, *refs):
    parts, refs = refs[:ny], refs[ny:]
    kepts, blocks, refs = refs[:count], refs[count : 3 * count], refs[3 * count :]
    sums = total(parts)
    samples = kepts[0].shape[1] * count
    image_rows, sc = sums[:, :samples], sums[:, samples:]
    before, before_sc = (None, None) if first else refs[:2]
    partial, rows_out, sc_out = refs[-3:]
    rz, dd, beta, dot = direction_scalars(sc, before_sc)
    if not first:
        before = before[...]
        image_rows = image_rows + beta * before
    out, squares, cross = adjoint(image_rows, before, kepts, blocks)
    partial[...] = out
    rows_out[...] = image_rows
    sc_out[...] = pack_scalars([rz, dd, beta, dot, squares, cross], dd.shape[0])


def rest_kernel(ny, count, first, *refs):
    parts, refs = refs[:ny], refs[ny:]
    kepts, blocks, refs = refs[:count], refs[count : 3 * count], refs[3 * count :]
    sc, partial, refs = refs[0], refs[1], refs[2:]
    image_rows = total(parts)
    before = None
    if not first:
        before = refs[0][...]
        image_rows = image_rows + sc[:, 2:3] * before
    msg, rows_out = refs[-2:]
    out, squares, cross = adjoint(image_rows, before, kepts, blocks)
    features = out.shape[1]
    msg[:, :features] = partial[...] + out
    msg[:, features:] = pack_scalars([sc[:, 4:5] + squares, sc[:, 5:6] + cross], out.shape[0])
    rows_out[...] = image_rows


def update_kernel(count, first, last, *refs):
    parts, refs = refs[:2], refs[2:]
    sc, penalty, mag, precond, residual, scaled, rows, rest, refs = *refs[:8], refs[8:]
    blocks, refs = refs[: 2 * count], refs[2 * count :]
    sums = total(parts)
    features = mag.shape[1]
    lam, m = penalty[...], mag[...]
    direction = scaled[...]
    image_rows = jnp.concatenate([rows[...], rest[...]], axis=1)
    image = sums[:, :features] * m
    scalars = sums[:, features:]
    if first:
        image = image + lam * direction
    else:
        (before, weights, predicted, before_image, before_curve, before_rows, before_rest), refs = refs[:7], refs[7:]
        direction = direction + sc[:, 2:3] * before[...]
        extra = (scalars[:, 1:2] + lam * sc[:, 3:4]) / before_curve[:, 0:1]
        image = image + lam * direction - extra * before_image[...]
        direction = direction - extra * before[...]
        image_rows = image_rows - extra * jnp.concatenate([before_rows[...], before_rest[...]], axis=1)
    (msg, scaled_out, direction_out, weights_out, predicted_out), refs = refs[:5], refs[5:]
    curve = scalars[:, 0:1] + lam * sc[:, 1:2]
    step = sc[:, 0:1] / curve
    moved, fitted = step * direction, step * image_rows
    weights_out[...] = moved if first else weights[...] + moved
    predicted_out[...] = fitted if first else predicted[...] + fitted
    res = residual[...] - step * image
    s, v = held(res / precond[...], m)
    scaled_out[...] = s
    direction_out[...] = direction
    if last:
        refs[0][...] = image_rows
    else:
        refs[0][...] = res
        refs[1][...] = image
        refs[2][...] = pack_scalars([curve], curve.shape[0])
    send_forward(v, blocks, msg, [row_sum(res * s), row_sum(s * s), row_sum(s * direction)])


def fold_rows(value, fold):
    n = value.shape[0] // 2
    return jnp.where(fold == 0, value[:n], value[n:])


def last_kernel(ny, nz, *refs):
    parts, refs = refs[:ny], refs[ny:]
    kepts, (before, before_sc, predicted, msg, rows_out, sc_out) = refs[:nz], refs[nz:]
    sums = total(parts)
    half = kepts[0].shape[1]
    samples = half * nz
    rz, dd, beta, _ = direction_scalars(sums[:, samples:], before_sc)
    image_rows = sums[:, :samples] + beta * before[...]
    squares = jnp.zeros_like(dd)
    for j, kept in enumerate(kepts):
        rows = image_rows[:, j * half : (j + 1) * half]
        squares = squares + row_sum(rows * rows * kept[...])
    other = 1 - core()
    n = dd.shape[0] // 2
    msg[:n, :samples] = fold_rows(image_rows, other)
    msg[n:, :samples] = fold_rows(predicted[...], other)
    msg[:, samples:] = pack_scalars([squares], 2 * n)
    rows_out[...] = image_rows
    sc_out[...] = pack_scalars([rz, dd, beta], 2 * n)


def finish_kernel(nz, own, got, sc, penalty, scaled, before, weights, rows, predicted, *outs):
    samples, features = rows.shape[1], scaled.shape[1]
    half = samples // nz
    c = core()
    n = sc.shape[0] // 2
    step = sc[:, 0:1] / ((own[:, samples : samples + 1] + got[:, samples : samples + 1]) + penalty[...] * sc[:, 1:2])
    coefficients = weights[...] + step * (scaled[...] + sc[:, 2:3] * before[...])
    coefficients = fold_rows(coefficients, c)
    here = fold_rows(predicted[...] + step * rows[...], c)
    there = got[n:, :samples] + fold_rows(step, c) * got[:n, :samples]
    lower, upper = jnp.where(c == 0, here, there), jnp.where(c == 0, there, here)
    for j, out in enumerate(outs):
        out[:, :features] = coefficients
        out[:, features : features + half] = lower[:, j * half : (j + 1) * half]
        out[:, features + half :] = upper[:, j * half : (j + 1) * half]


def arrange_kernel(order, *refs):
    nz = len(order)
    parts, (weights_out, predictions_out, held) = refs[:nz], refs[nz:]
    features = weights_out.shape[1]
    n = weights_out.shape[0] // nz
    for j, part in zip(order, parts):
        held[j] = part[...]
    z = lax.axis_index("samp")
    for k in range(nz):
        part = held[lax.bitwise_xor(z, k)]
        weights_out[k * n : (k + 1) * n, :] = part[:, :features]
        predictions_out[k * n : (k + 1) * n, :] = part[:, features:]


ITERS = 3


def shards(
    nf,
    nz,
    ny,
    input_points,
    wave_numbers,
    offset_angles,
    feature_magnitudes,
    response_values,
    split_label,
    shrinkage_levels,
):
    shard, features = input_points.shape[0], wave_numbers.shape[1]
    depth = input_points.shape[1]
    levels = shrinkage_levels.shape[0]
    half, rows = shard // 2, 2 * (levels // nz)
    samples = half * nz
    tall = (shard // LANES, LANES)
    extra = pl.cdiv(5 * half // LANES, 16) * 16
    row_f, row_s, row_c = ((rows, features), f32), ((rows, samples), f32), ((rows, LANES), f32)
    msg_f, msg_s = ((rows, features + LANES), f32), ((rows, samples + LANES), f32)

    label = split_label.reshape(tall)
    other_label = flip(label, "fold", nf, 1)
    inputs = [input_points, wave_numbers, offset_angles.reshape(1, features), feature_magnitudes.reshape(1, features)]
    inputs += [response_values.reshape(tall), label, shrinkage_levels.reshape(1, levels)]
    vectors = [((1, features), f32), ((1, features), f32), (tall, f32), (tall, jnp.int32), ((1, levels), f32)]
    packed = ((half + extra, depth), bf16)
    msg, waves, offsets, mag, penalty, response, label = pl.pallas_call(
        functools.partial(pack_kernel, math.sqrt(2.0 / (features * ny))),
        out_shape=[
            pltpu.VMEM(*packed),
            pltpu.VMEM((depth, features), bf16),
            pltpu.VMEM((1, features), f32),
            pltpu.VMEM((1, features), f32),
            pltpu.VMEM((rows, 1), f32),
            pltpu.VMEM(tall, f32),
            pltpu.VMEM(tall, jnp.int32),
        ],
        in_specs=[pl.BlockSpec(memory_space=pltpu.HBM)] * len(inputs),
        scratch_shapes=[pltpu.VMEM((half, depth), bf16)]
        + [pltpu.VMEM(v, d) for v, d in vectors]
        + [pltpu.SemaphoreType.DMA((len(inputs),))],
        compiler_params=pltpu.CompilerParams(vmem_limit_bytes=VMEM_LIMIT),
    )(*[pltpu.with_memory_space_constraint(v, pltpu.HBM) for v in inputs])
    (msg,) = call(
        functools.partial(label_kernel, half), [packed], msg, label, other_label, response, aliases={0: 0}
    )

    order = [j ^ (j >> 1) for j in range(nz)]
    blocks, turned, kepts, moments = [], [], [], None
    tile, tile_t = ((half, features), bf16), ((features, half), bf16)
    for j in order:
        part = flip(msg, "samp", nz, j) if j else msg
        high, low, high_t, low_t, kept, moments = call(
            functools.partial(features_kernel, j == 0),
            [tile, tile, tile_t, tile_t, ((rows, half), f32), ((4, features), f32)],
            part, waves, offsets, *(() if j == 0 else (moments,)),
            scratch=[pltpu.VMEM((2, 8, features), f32), pltpu.VMEM((2, half, LANES), f32)],
            flops=60 * half * features,
        )
        blocks += [high, low]
        turned += [high_t, low_t]
        kepts.append(kept)
    count, later = nz - 1, 1
    msg_a, row_a = ((rows, half * count + LANES), f32), ((rows, half * count), f32)
    row_b = ((rows, half * later), f32)
    work = 2 * 3 * rows * half * features
    msg, scaled, precond, residual = call(
        functools.partial(begin_kernel, count),
        [msg_a, row_f, row_f, row_f],
        moments, flip(moments, "fold", nf, 1), penalty, mag, *turned[: 2 * count],
        flops=work * count,
    )
    before = weights = predicted = image = curve = sc = rows_a = rows_b = None
    for it in range(ITERS - 1):
        first, last = it == 0, it == ITERS - 2
        parts = exchange(msg, "feat", ny)
        (msg_b,) = call(forward_kernel, [row_b], scaled, mag, *turned[2 * count :], flops=work * later)
        parts_b = exchange(msg_b, "feat", ny)
        partial, new_a, new_sc = call(
            functools.partial(adjoint_kernel, ny, count, first),
            [row_f, row_a, row_c],
            *parts, *kepts[:count], *blocks[: 2 * count], *(() if first else (rows_a, sc)),
            flops=work * count,
        )
        msg, new_b = call(
            functools.partial(rest_kernel, ny, later, first),
            [msg_f, row_b],
            *parts_b, *kepts[count:], *blocks[2 * count :], new_sc, partial, *(() if first else (rows_b,)),
            flops=work * later,
        )
        sc = new_sc
        msg, scaled, before, weights, predicted, *rest = call(
            functools.partial(update_kernel, nz if last else count, first, last),
            [msg_s if last else msg_a, row_f, row_f, row_f, row_s] + ([row_s] if last else [row_f, row_f, row_c]),
            msg, flip(msg, "fold", nf, 1), sc, penalty, mag, precond, residual, scaled, new_a, new_b,
            *(turned if last else turned[: 2 * count]),
            *(() if first else (before, weights, predicted, image, curve, rows_a, rows_b)),
            flops=work * count,
        )
        rows_a, rows_b = new_a, new_b
        residual, image, curve = (None, None, None) if last else rest
    msg, image_rows, sc = call(
        functools.partial(last_kernel, ny, nz),
        [msg_s, row_s, row_c],
        *exchange(msg, "feat", ny), *kepts, rest[0], sc, predicted,
    )
    outs = call(
        functools.partial(finish_kernel, nz),
        [((rows // 2, features + shard), f32)] * nz,
        msg, flip(msg, "fold", nf, 1), sc, penalty, scaled, before, weights, image_rows, predicted,
    )
    far_first = [0] + sorted(range(1, nz), key=lambda j: -j.bit_length())
    outs = [flip(outs[order.index(j)], "samp", nz, j) if j else outs[0] for j in far_first]
    return call(
        functools.partial(arrange_kernel, far_first),
        [((levels, features), f32), ((levels, shard), f32)],
        *outs,
        scratch=[pltpu.VMEM((nz, rows // 2, features + shard), f32)],
        in_vmem=False,
    )


def solution(mesh):
    placed = (
        P("samp", None),
        P(None, "feat"),
        P("feat"),
        P("feat"),
        P("samp"),
        P(("fold", "samp")),
        P(),
    )
    sizes = [mesh.shape[axis] for axis in ("fold", "samp", "feat")]
    return jax.shard_map(
        functools.partial(shards, *sizes),
        mesh=mesh,
        in_specs=placed,
        out_specs=(P("fold", "feat"), P("fold", "samp")),
        check_vma=False,
    )
```

```python
import functools
import math

import jax
import jax.numpy as jnp
from jax import lax
from jax.experimental import pallas as pl
from jax.experimental.pallas import tpu as pltpu
from jax.sharding import PartitionSpec as P

f32, bf16, f8 = jnp.float32, jnp.bfloat16, jnp.float8_e4m3fn
TURN = 1.0 / (2.0 * math.pi)
SINE = (-6.283164044377446, 41.337142378931674, -81.34076911271806, 70.99343519544783)
LANES = 128
VMEM_LIMIT = 12 * 2**20
LOW_SCALE = 512.0


def call(body, outs, *args, flops=0, in_vmem=True, scratch=(), aliases={}):
    outs = [pltpu.VMEM(s, d) if in_vmem else jax.ShapeDtypeStruct(s, d) for s, d in outs]
    size = sum(math.prod(a.shape) * a.dtype.itemsize for a in args)
    return pl.pallas_call(
        body,
        out_shape=outs,
        scratch_shapes=list(scratch),
        input_output_aliases=aliases,
        compiler_params=pltpu.CompilerParams(vmem_limit_bytes=VMEM_LIMIT),
        cost_estimate=pl.CostEstimate(flops=flops, bytes_accessed=size, transcendentals=0),
    )(*args)


def total(refs):
    values = [r[...] for r in refs]
    while len(values) > 1:
        values = [values[i] + values[i + 1] for i in range(0, len(values), 2)]
    return values[0]


def halves(value):
    high = value.astype(bf16)
    return high, (value - high.astype(f32)).astype(bf16)


def split(rows):
    high, low = halves(rows)
    both = jnp.concatenate([high.astype(f32), low.astype(f32)], axis=0).astype(bf16)
    scale = 256.0 / jnp.maximum(jnp.max(jnp.abs(rows), axis=1, keepdims=True), 1e-30)
    scaled = rows * scale
    coarse = scaled.astype(f8).astype(f32)
    small = jnp.concatenate([coarse, (scaled - coarse) * 16.0], axis=0).astype(f8)
    return both, small, 1.0 / (scale * LOW_SCALE)


def product(parts, high_ref, low_ref):
    both, small, back = parts
    n = back.shape[0]
    out = jnp.dot(both, high_ref[...], preferred_element_type=f32)
    fine = jnp.dot(small, low_ref[...], preferred_element_type=f32)
    return out[:n] + out[n:] + (fine[:n] + fine[n:] * 0.0625) * back


def held(scaled, mag):
    high, low = halves(scaled * mag)
    rounded = high.astype(f32) + low.astype(f32)
    return rounded / mag, rounded


def pack_scalars(columns, rows):
    lane = lax.broadcasted_iota(jnp.int32, (rows, LANES), 1)
    out = jnp.zeros((rows, LANES), f32)
    for i, column in enumerate(columns):
        out = jnp.where(lane == i, column, out)
    return out


def row_sum(value):
    return jnp.sum(value, axis=1, keepdims=True)


def flip(value, axis, n, s):
    return lax.ppermute(value, axis, [(i, i ^ s) for i in range(n)])


def exchange(value, axis, n):
    return [value] + [flip(value, axis, n, s) for s in range(1, n)]


def as_row(block):
    return jnp.concatenate([block[i : i + 1] for i in range(block.shape[0])], axis=1)


def spread(pair, rows):
    return jnp.concatenate(
        [jnp.broadcast_to(pair[e : e + 1], (rows // 2, pair.shape[1])) for e in (0, 1)], axis=0
    )


def core():
    return lax.rem(lax.axis_index("fold"), 2)


def pack_kernel(
    scale, x_hbm, w_hbm, offset_hbm, mag_hbm, response_hbm, label_hbm, penalty_hbm,
    msg, w_ref, offset_ref, mag_ref, penalty_ref, response_out, label_out,
    points, offset_in, mag_in, response_ref, label_ref, penalty_in, sems,
):
    half = points.shape[0]
    c = core()
    pairs = [
        (x_hbm.at[pl.ds(pl.multiple_of(c * half, half), half), :], points),
        (label_hbm, label_ref), (response_hbm, response_ref), (w_hbm, w_ref),
        (offset_hbm, offset_in), (mag_hbm, mag_in), (penalty_hbm, penalty_in),
    ]
    copies = [pltpu.make_async_copy(a, b, sems.at[i]) for i, (a, b) in enumerate(pairs)]
    for copy in copies:
        copy.start()
    for copy in copies:
        copy.wait()
    msg[:half, :] = points[...]
    msg[half:, :] = jnp.zeros_like(msg[half:, :])
    label_out[...] = label_ref[...]
    response_out[...] = response_ref[...]
    offset_ref[...] = offset_in[...] * TURN
    mag_ref[...] = mag_in[...] * scale
    levels, rows = penalty_in.shape[1], penalty_ref.shape[0]
    row, column = [lax.broadcasted_iota(jnp.int32, (rows, levels), a) for a in (0, 1)]
    chosen = column == lax.axis_index("samp") * (rows // 2) + lax.rem(row, rows // 2)
    penalty_ref[...] = row_sum(jnp.where(chosen, penalty_in[...], 0.0))


def label_kernel(half, points, label, other_label, response, msg):
    n = half // LANES
    c = core()

    def mine(block):
        return jnp.where(c == 0, block[:n], block[n:])

    own = (mine(label[...]) != 0).astype(f32)
    other = (mine(other_label[...]) != 0).astype(f32)
    y = mine(response[...])
    high, low = halves(y)
    aux = [jnp.where(c == 0, own, other), jnp.where(c == 0, other, own)]
    aux += [v.astype(f32) for v in (high, low)]
    if msg.shape[0] - half > 4 * n:
        aux += [jnp.zeros((msg.shape[0] - half - 4 * n, LANES), f32)]
    msg[half:, :] = jnp.concatenate(aux, axis=0).astype(bf16)


def features_kernel(first, msg, w_ref, offset_ref, *refs):
    before, refs = (None, refs) if first else (refs[0], refs[1:])
    high_ref, low_ref, high_t, low_t, kept_ref, moment_ref, acc, mask = refs
    samples, features = high_ref.shape
    n = samples // LANES
    aux = msg[samples:, :].astype(f32)
    kept = jnp.concatenate([as_row(aux[e * n : (e + 1) * n]) for e in (0, 1)], axis=0)
    kept_ref[...] = spread(kept, kept_ref.shape[0])
    y = aux[2 * n : 3 * n] + aux[3 * n : 4 * n]
    y_high, y_low = halves(kept * as_row(y))
    y_both = jnp.concatenate([y_high.astype(f32), y_low.astype(f32)], axis=0).astype(bf16)
    columns = jnp.concatenate([kept, jnp.zeros((6, samples), f32)], axis=0).T
    for e in (0, 1):
        mask[e] = jnp.broadcast_to(columns[:, e : e + 1], (samples, LANES))
    cb = min(features, 256)
    for j in range(0, features, cb):
        a = jnp.dot(msg[:samples, :], w_ref[:, j : j + cb], preferred_element_type=f32)
        t = a * TURN + offset_ref[:, j : j + cb]
        r = t - jnp.round(t)
        q = jnp.abs(r) - 0.25
        u = q * q
        c = jnp.full_like(u, SINE[-1])
        for k in SINE[-2::-1]:
            c = c * u + k
        c = c * q
        high, low = halves(c)
        high_ref[:, j : j + cb] = high
        small = ((c - high.astype(f32)) * LOW_SCALE).astype(f8)
        low_ref[:, j : j + cb] = small
        high_t[j : j + cb, :] = high.T
        low_t[j : j + cb, :] = small.T
        square = c * c
        for e in (0, 1):
            part = square * jnp.concatenate([mask[e]] * (cb // LANES), axis=1)
            acc[e, :, j : j + cb] = part.reshape(samples // 8, 8, cb).sum(0)
        side = jnp.dot(y_both, high, preferred_element_type=f32)
        side = side[:2] + side[2:] + jnp.dot(y_high, low, preferred_element_type=f32)
        moment_ref[2:4, j : j + cb] = side if first else before[2:4, j : j + cb] + side
    for e in (0, 1):
        square = jnp.sum(acc[e], axis=0, keepdims=True)
        moment_ref[e : e + 1, :] = square if first else before[e : e + 1, :] + square


def forward(v, blocks, msg):
    at, parts = 0, split(v)
    for high, low in zip(blocks[::2], blocks[1::2]):
        n = high.shape[1]
        msg[:, at : at + n] = product(parts, high, low)
        at += n
    return at


def send_forward(v, blocks, msg, scalars):
    at = forward(v, blocks, msg)
    msg[:, at:] = pack_scalars(scalars, v.shape[0])


def forward_kernel(scaled, mag, *refs):
    forward(scaled[...] * mag[...], refs[:-1], refs[-1])


def begin_kernel(count, *refs):
    moments, penalty, mag, blocks = refs[:2], refs[2], refs[3], refs[4 : 4 + 2 * count]
    msg, direction, precond, residual = refs[4 + 2 * count :]
    sums = total(moments)
    m = mag[...]
    rows = penalty.shape[0]
    pre = spread(sums[0:2] * (m * m), rows) + penalty[...]
    res = spread(sums[2:4] * m, rows)
    s, v = held(res / pre, m)
    precond[...] = pre
    residual[...] = res
    direction[...] = s
    send_forward(v, blocks, msg, [row_sum(res * s), row_sum(s * s)])


def direction_scalars(sc, before_sc):
    rz, dd = sc[:, 0:1], sc[:, 1:2]
    if before_sc is None:
        return rz, dd, jnp.zeros_like(rz), jnp.zeros_like(rz)
    beta = rz / before_sc[:, 0:1]
    dot = sc[:, 2:3] + beta * before_sc[:, 1:2]
    return rz, dd + beta * (sc[:, 2:3] + dot), beta, dot


def adjoint(image_rows, before, kepts, blocks):
    half = kepts[0].shape[1]
    out = 0.0
    squares = cross = jnp.zeros((image_rows.shape[0], 1), f32)
    for j, (kept, high, low) in enumerate(zip(kepts, blocks[::2], blocks[1::2])):
        at = slice(j * half, (j + 1) * half)
        rows = image_rows[:, at]
        weighted = rows * kept[...]
        squares = squares + row_sum(weighted * rows)
        if before is not None:
            cross = cross + row_sum(weighted * before[:, at])
        out = out + product(split(weighted), high, low)
    return out, squares, cross


def adjoint_kernel(ny, count, first, *refs):
    parts, refs = refs[:ny], refs[ny:]
    kepts, blocks, refs = refs[:count], refs[count : 3 * count], refs[3 * count :]
    sums = total(parts)
    samples = kepts[0].shape[1] * count
    image_rows, sc = sums[:, :samples], sums[:, samples:]
    before, before_sc = (None, None) if first else refs[:2]
    partial, rows_out, sc_out = refs[-3:]
    rz, dd, beta, dot = direction_scalars(sc, before_sc)
    if not first:
        before = before[...]
        image_rows = image_rows + beta * before
    out, squares, cross = adjoint(image_rows, before, kepts, blocks)
    partial[...] = out
    rows_out[...] = image_rows
    sc_out[...] = pack_scalars([rz, dd, beta, dot, squares, cross], dd.shape[0])


def rest_kernel(ny, count, first, *refs):
    parts, refs = refs[:ny], refs[ny:]
    kepts, blocks, refs = refs[:count], refs[count : 3 * count], refs[3 * count :]
    sc, partial, refs = refs[0], refs[1], refs[2:]
    image_rows = total(parts)
    before = None
    if not first:
        before = refs[0][...]
        image_rows = image_rows + sc[:, 2:3] * before
    msg, rows_out = refs[-2:]
    out, squares, cross = adjoint(image_rows, before, kepts, blocks)
    features = out.shape[1]
    msg[:, :features] = partial[...] + out
    msg[:, features:] = pack_scalars([sc[:, 4:5] + squares, sc[:, 5:6] + cross], out.shape[0])
    rows_out[...] = image_rows


def update_kernel(count, first, last, *refs):
    parts, refs = refs[:2], refs[2:]
    sc, penalty, mag, precond, residual, scaled, rows, rest, refs = *refs[:8], refs[8:]
    blocks, refs = refs[: 2 * count], refs[2 * count :]
    sums = total(parts)
    features = mag.shape[1]
    lam, m = penalty[...], mag[...]
    direction = scaled[...]
    image_rows = jnp.concatenate([rows[...], rest[...]], axis=1)
    image = sums[:, :features] * m
    scalars = sums[:, features:]
    if first:
        image = image + lam * direction
    else:
        (before, weights, predicted, before_image, before_curve, before_rows, before_rest), refs = refs[:7], refs[7:]
        direction = direction + sc[:, 2:3] * before[...]
        extra = (scalars[:, 1:2] + lam * sc[:, 3:4]) / before_curve[:, 0:1]
        image = image + lam * direction - extra * before_image[...]
        direction = direction - extra * before[...]
        image_rows = image_rows - extra * jnp.concatenate([before_rows[...], before_rest[...]], axis=1)
    (msg, scaled_out, direction_out, weights_out, predicted_out), refs = refs[:5], refs[5:]
    curve = scalars[:, 0:1] + lam * sc[:, 1:2]
    step = sc[:, 0:1] / curve
    moved, fitted = step * direction, step * image_rows
    weights_out[...] = moved if first else weights[...] + moved
    predicted_out[...] = fitted if first else predicted[...] + fitted
    res = residual[...] - step * image
    s, v = held(res / precond[...], m)
    scaled_out[...] = s
    direction_out[...] = direction
    if last:
        refs[0][...] = image_rows
    else:
        refs[0][...] = res
        refs[1][...] = image
        refs[2][...] = pack_scalars([curve], curve.shape[0])
    send_forward(v, blocks, msg, [row_sum(res * s), row_sum(s * s), row_sum(s * direction)])


def fold_rows(value, fold):
    n = value.shape[0] // 2
    return jnp.where(fold == 0, value[:n], value[n:])


def last_kernel(ny, nz, *refs):
    parts, refs = refs[:ny], refs[ny:]
    kepts, (before, before_sc, predicted, msg, rows_out, sc_out) = refs[:nz], refs[nz:]
    sums = total(parts)
    half = kepts[0].shape[1]
    samples = half * nz
    rz, dd, beta, _ = direction_scalars(sums[:, samples:], before_sc)
    image_rows = sums[:, :samples] + beta * before[...]
    squares = jnp.zeros_like(dd)
    for j, kept in enumerate(kepts):
        rows = image_rows[:, j * half : (j + 1) * half]
        squares = squares + row_sum(rows * rows * kept[...])
    other = 1 - core()
    n = dd.shape[0] // 2
    msg[:n, :samples] = fold_rows(image_rows, other)
    msg[n:, :samples] = fold_rows(predicted[...], other)
    msg[:, samples:] = pack_scalars([squares], 2 * n)
    rows_out[...] = image_rows
    sc_out[...] = pack_scalars([rz, dd, beta], 2 * n)


def finish_kernel(nz, own, got, sc, penalty, scaled, before, weights, rows, predicted, *outs):
    samples, features = rows.shape[1], scaled.shape[1]
    half = samples // nz
    c = core()
    n = sc.shape[0] // 2
    step = sc[:, 0:1] / ((own[:, samples : samples + 1] + got[:, samples : samples + 1]) + penalty[...] * sc[:, 1:2])
    coefficients = weights[...] + step * (scaled[...] + sc[:, 2:3] * before[...])
    coefficients = fold_rows(coefficients, c)
    here = fold_rows(predicted[...] + step * rows[...], c)
    there = got[n:, :samples] + fold_rows(step, c) * got[:n, :samples]
    lower, upper = jnp.where(c == 0, here, there), jnp.where(c == 0, there, here)
    for j, out in enumerate(outs):
        out[:, :features] = coefficients
        out[:, features : features + half] = lower[:, j * half : (j + 1) * half]
        out[:, features + half :] = upper[:, j * half : (j + 1) * half]


def arrange_kernel(order, *refs):
    nz = len(order)
    parts, (weights_out, predictions_out, held) = refs[:nz], refs[nz:]
    features = weights_out.shape[1]
    n = weights_out.shape[0] // nz
    for j, part in zip(order, parts):
        held[j] = part[...]
    z = lax.axis_index("samp")
    for k in range(nz):
        part = held[lax.bitwise_xor(z, k)]
        weights_out[k * n : (k + 1) * n, :] = part[:, :features]
        predictions_out[k * n : (k + 1) * n, :] = part[:, features:]


ITERS = 3


def shards(
    nf,
    nz,
    ny,
    input_points,
    wave_numbers,
    offset_angles,
    feature_magnitudes,
    response_values,
    split_label,
    shrinkage_levels,
):
    shard, features = input_points.shape[0], wave_numbers.shape[1]
    depth = input_points.shape[1]
    levels = shrinkage_levels.shape[0]
    half, rows = shard // 2, 2 * (levels // nz)
    samples = half * nz
    tall = (shard // LANES, LANES)
    extra = pl.cdiv(4 * half // LANES, 16) * 16
    row_f, row_s, row_c = ((rows, features), f32), ((rows, samples), f32), ((rows, LANES), f32)
    msg_f, msg_s = ((rows, features + LANES), f32), ((rows, samples + LANES), f32)

    label = split_label.reshape(tall)
    other_label = flip(label, "fold", nf, 1)
    inputs = [input_points, wave_numbers, offset_angles.reshape(1, features), feature_magnitudes.reshape(1, features)]
    inputs += [response_values.reshape(tall), label, shrinkage_levels.reshape(1, levels)]
    vectors = [((1, features), f32), ((1, features), f32), (tall, f32), (tall, jnp.int32), ((1, levels), f32)]
    packed = ((half + extra, depth), bf16)
    msg, waves, offsets, mag, penalty, response, label = pl.pallas_call(
        functools.partial(pack_kernel, math.sqrt(2.0 / (features * ny))),
        out_shape=[
            pltpu.VMEM(*packed),
            pltpu.VMEM((depth, features), bf16),
            pltpu.VMEM((1, features), f32),
            pltpu.VMEM((1, features), f32),
            pltpu.VMEM((rows, 1), f32),
            pltpu.VMEM(tall, f32),
            pltpu.VMEM(tall, jnp.int32),
        ],
        in_specs=[pl.BlockSpec(memory_space=pltpu.HBM)] * len(inputs),
        scratch_shapes=[pltpu.VMEM((half, depth), bf16)]
        + [pltpu.VMEM(v, d) for v, d in vectors]
        + [pltpu.SemaphoreType.DMA((len(inputs),))],
        compiler_params=pltpu.CompilerParams(vmem_limit_bytes=VMEM_LIMIT),
    )(*[pltpu.with_memory_space_constraint(v, pltpu.HBM) for v in inputs])
    (msg,) = call(
        functools.partial(label_kernel, half), [packed], msg, label, other_label, response, aliases={0: 0}
    )

    order = [j ^ (j >> 1) for j in range(nz)]
    blocks, turned, kepts, moments = [], [], [], None
    shapes = (half, features), (features, half)
    tiles = [(shape, kind) for shape in shapes for kind in (bf16, f8)]
    for j in order:
        part = flip(msg, "samp", nz, j) if j else msg
        high, low, high_t, low_t, kept, moments = call(
            functools.partial(features_kernel, j == 0),
            [*tiles, ((rows, half), f32), ((4, features), f32)],
            part, waves, offsets, *(() if j == 0 else (moments,)),
            scratch=[pltpu.VMEM((2, 8, features), f32), pltpu.VMEM((2, half, LANES), f32)],
            flops=60 * half * features,
        )
        blocks += [high, low]
        turned += [high_t, low_t]
        kepts.append(kept)
    count, later = nz - 1, 1
    msg_a, row_a = ((rows, half * count + LANES), f32), ((rows, half * count), f32)
    row_b = ((rows, half * later), f32)
    work = 2 * 3 * rows * half * features
    msg, scaled, precond, residual = call(
        functools.partial(begin_kernel, count),
        [msg_a, row_f, row_f, row_f],
        moments, flip(moments, "fold", nf, 1), penalty, mag, *turned[: 2 * count],
        flops=work * count,
    )
    before = weights = predicted = image = curve = sc = rows_a = rows_b = None
    for it in range(ITERS - 1):
        first, last = it == 0, it == ITERS - 2
        parts = exchange(msg, "feat", ny)
        (msg_b,) = call(forward_kernel, [row_b], scaled, mag, *turned[2 * count :], flops=work * later)
        parts_b = exchange(msg_b, "feat", ny)
        partial, new_a, new_sc = call(
            functools.partial(adjoint_kernel, ny, count, first),
            [row_f, row_a, row_c],
            *parts, *kepts[:count], *blocks[: 2 * count], *(() if first else (rows_a, sc)),
            flops=work * count,
        )
        msg, new_b = call(
            functools.partial(rest_kernel, ny, later, first),
            [msg_f, row_b],
            *parts_b, *kepts[count:], *blocks[2 * count :], new_sc, partial, *(() if first else (rows_b,)),
            flops=work * later,
        )
        sc = new_sc
        msg, scaled, before, weights, predicted, *rest = call(
            functools.partial(update_kernel, nz if last else count, first, last),
            [msg_s if last else msg_a, row_f, row_f, row_f, row_s] + ([row_s] if last else [row_f, row_f, row_c]),
            msg, flip(msg, "fold", nf, 1), sc, penalty, mag, precond, residual, scaled, new_a, new_b,
            *(turned if last else turned[: 2 * count]),
            *(() if first else (before, weights, predicted, image, curve, rows_a, rows_b)),
            flops=work * count,
        )
        rows_a, rows_b = new_a, new_b
        residual, image, curve = (None, None, None) if last else rest
    msg, image_rows, sc = call(
        functools.partial(last_kernel, ny, nz),
        [msg_s, row_s, row_c],
        *exchange(msg, "feat", ny), *kepts, rest[0], sc, predicted,
    )
    outs = call(
        functools.partial(finish_kernel, nz),
        [((rows // 2, features + shard), f32)] * nz,
        msg, flip(msg, "fold", nf, 1), sc, penalty, scaled, before, weights, image_rows, predicted,
    )
    far_first = [0] + sorted(range(1, nz), key=lambda j: -j.bit_length())
    outs = [flip(outs[order.index(j)], "samp", nz, j) if j else outs[0] for j in far_first]
    return call(
        functools.partial(arrange_kernel, far_first),
        [((levels, features), f32), ((levels, shard), f32)],
        *outs,
        scratch=[pltpu.VMEM((nz, rows // 2, features + shard), f32)],
        in_vmem=False,
    )


def solution(mesh):
    placed = (
        P("samp", None),
        P(None, "feat"),
        P("feat"),
        P("feat"),
        P("samp"),
        P(("fold", "samp")),
        P(),
    )
    sizes = [mesh.shape[axis] for axis in ("fold", "samp", "feat")]
    return jax.shard_map(
        functools.partial(shards, *sizes),
        mesh=mesh,
        in_specs=placed,
        out_specs=(P("fold", "feat"), P("fold", "samp")),
        check_vma=False,
    )
```

```python
import functools
import math

import jax
import jax.numpy as jnp
from jax import lax
from jax.experimental import pallas as pl
from jax.experimental.pallas import tpu as pltpu
from jax.sharding import PartitionSpec as P

f32, bf16, f8 = jnp.float32, jnp.bfloat16, jnp.float8_e4m3fn
TURN = 1.0 / (2.0 * math.pi)
SINE = (-6.283164044377446, 41.337142378931674, -81.34076911271806, 70.99343519544783)
LANES = 128
VMEM_LIMIT = 12 * 2**20
LOW_SCALE = 512.0


def call(body, outs, *args, flops=0, in_vmem=True, scratch=(), aliases={}):
    outs = [pltpu.VMEM(s, d) if in_vmem else jax.ShapeDtypeStruct(s, d) for s, d in outs]
    size = sum(math.prod(a.shape) * a.dtype.itemsize for a in args)
    return pl.pallas_call(
        body,
        out_shape=outs,
        scratch_shapes=list(scratch),
        input_output_aliases=aliases,
        compiler_params=pltpu.CompilerParams(vmem_limit_bytes=VMEM_LIMIT),
        cost_estimate=pl.CostEstimate(flops=flops, bytes_accessed=size, transcendentals=0),
    )(*args)


def total(refs):
    values = [r[...] for r in refs]
    while len(values) > 1:
        values = [values[i] + values[i + 1] for i in range(0, len(values), 2)]
    return values[0]


def halves(value):
    high = value.astype(bf16)
    return high, (value - high.astype(f32)).astype(bf16)


def split(rows):
    high, low = halves(rows)
    both = jnp.concatenate([high.astype(f32), low.astype(f32)], axis=0).astype(bf16)
    scale = 256.0 / jnp.maximum(jnp.max(jnp.abs(rows), axis=1, keepdims=True), 1e-30)
    scaled = rows * scale
    coarse = scaled.astype(f8).astype(f32)
    small = jnp.concatenate([coarse, (scaled - coarse) * 16.0], axis=0).astype(f8)
    return both, small, 1.0 / (scale * LOW_SCALE)


def product(parts, high_ref, low_ref):
    both, small, back = parts
    n = back.shape[0]
    out = jnp.dot(both, high_ref[...], preferred_element_type=f32)
    fine = jnp.dot(small, low_ref[...], preferred_element_type=f32)
    return out[:n] + out[n:] + (fine[:n] + fine[n:] * 0.0625) * back


def held(scaled, mag):
    high, low = halves(scaled * mag)
    rounded = high.astype(f32) + low.astype(f32)
    return rounded / mag, rounded


def pack_scalars(columns, rows):
    lane = lax.broadcasted_iota(jnp.int32, (rows, LANES), 1)
    out = jnp.zeros((rows, LANES), f32)
    for i, column in enumerate(columns):
        out = jnp.where(lane == i, column, out)
    return out


def row_sum(value):
    return jnp.sum(value, axis=1, keepdims=True)


def flip(value, axis, n, s):
    return lax.ppermute(value, axis, [(i, i ^ s) for i in range(n)])


def exchange(value, axis, n):
    return [value] + [flip(value, axis, n, s) for s in range(1, n)]


def as_row(block):
    return jnp.concatenate([block[i : i + 1] for i in range(block.shape[0])], axis=1)


def spread(pair, rows):
    return jnp.concatenate(
        [jnp.broadcast_to(pair[e : e + 1], (rows // 2, pair.shape[1])) for e in (0, 1)], axis=0
    )


def core():
    return lax.rem(lax.axis_index("fold"), 2)


def pack_kernel(
    scale, x_hbm, w_hbm, offset_hbm, mag_hbm, response_hbm, label_hbm, penalty_hbm,
    msg, w_ref, offset_ref, mag_ref, penalty_ref, response_out, label_out,
    points, offset_in, mag_in, response_ref, label_ref, penalty_in, sems,
):
    half = points.shape[0]
    c = core()
    pairs = [
        (x_hbm.at[pl.ds(pl.multiple_of(c * half, half), half), :], points),
        (label_hbm, label_ref), (response_hbm, response_ref), (w_hbm, w_ref),
        (offset_hbm, offset_in), (mag_hbm, mag_in), (penalty_hbm, penalty_in),
    ]
    copies = [pltpu.make_async_copy(a, b, sems.at[i]) for i, (a, b) in enumerate(pairs)]
    for copy in copies:
        copy.start()
    for copy in copies:
        copy.wait()
    msg[:half, :] = points[...]
    msg[half:, :] = jnp.zeros_like(msg[half:, :])
    label_out[...] = label_ref[...]
    response_out[...] = response_ref[...]
    offset_ref[...] = offset_in[...] * TURN
    mag_ref[...] = mag_in[...] * scale
    levels, rows = penalty_in.shape[1], penalty_ref.shape[0]
    row, column = [lax.broadcasted_iota(jnp.int32, (rows, levels), a) for a in (0, 1)]
    chosen = column == lax.axis_index("samp") * (rows // 2) + lax.rem(row, rows // 2)
    penalty_ref[...] = row_sum(jnp.where(chosen, penalty_in[...], 0.0))


def label_kernel(half, points, label, other_label, response, msg):
    n = half // LANES
    c = core()

    def mine(block):
        return jnp.where(c == 0, block[:n], block[n:])

    own = (mine(label[...]) != 0).astype(f32)
    other = (mine(other_label[...]) != 0).astype(f32)
    y = mine(response[...])
    high, low = halves(y)
    aux = [jnp.where(c == 0, own, other), jnp.where(c == 0, other, own)]
    aux += [v.astype(f32) for v in (high, low)]
    if msg.shape[0] - half > 4 * n:
        aux += [jnp.zeros((msg.shape[0] - half - 4 * n, LANES), f32)]
    msg[half:, :] = jnp.concatenate(aux, axis=0).astype(bf16)


def features_kernel(first, msg, w_ref, offset_ref, *refs):
    before, refs = (None, refs) if first else (refs[0], refs[1:])
    high_ref, low_ref, high_t, low_t, kept_ref, moment_ref, acc, mask = refs
    samples, features = high_ref.shape
    n = samples // LANES
    aux = msg[samples:, :].astype(f32)
    kept = jnp.concatenate([as_row(aux[e * n : (e + 1) * n]) for e in (0, 1)], axis=0)
    kept_ref[...] = spread(kept, kept_ref.shape[0])
    y = aux[2 * n : 3 * n] + aux[3 * n : 4 * n]
    y_high, y_low = halves(kept * as_row(y))
    y_both = jnp.concatenate([y_high.astype(f32), y_low.astype(f32)], axis=0).astype(bf16)
    columns = jnp.concatenate([kept, jnp.zeros((6, samples), f32)], axis=0).T
    for e in (0, 1):
        mask[e] = jnp.broadcast_to(columns[:, e : e + 1], (samples, LANES))
    cb = min(features, 256)
    for j in range(0, features, cb):
        a = jnp.dot(msg[:samples, :], w_ref[:, j : j + cb], preferred_element_type=f32)
        t = a * TURN + offset_ref[:, j : j + cb]
        r = t - jnp.round(t)
        q = jnp.abs(r) - 0.25
        u = q * q
        c = jnp.full_like(u, SINE[-1])
        for k in SINE[-2::-1]:
            c = c * u + k
        c = c * q
        high, low = halves(c)
        high_ref[:, j : j + cb] = high
        small = ((c - high.astype(f32)) * LOW_SCALE).astype(f8)
        low_ref[:, j : j + cb] = small
        high_t[j : j + cb, :] = high.T
        low_t[j : j + cb, :] = small.T
        square = c * c
        for e in (0, 1):
            part = square * jnp.concatenate([mask[e]] * (cb // LANES), axis=1)
            acc[e, :, j : j + cb] = part.reshape(samples // 8, 8, cb).sum(0)
        side = jnp.dot(y_both, high, preferred_element_type=f32)
        side = side[:2] + side[2:] + jnp.dot(y_high, low, preferred_element_type=f32)
        moment_ref[2:4, j : j + cb] = side if first else before[2:4, j : j + cb] + side
    for e in (0, 1):
        square = jnp.sum(acc[e], axis=0, keepdims=True)
        moment_ref[e : e + 1, :] = square if first else before[e : e + 1, :] + square


def forward(v, blocks, msg):
    at, parts = 0, split(v)
    for high, low in zip(blocks[::2], blocks[1::2]):
        n = high.shape[1]
        msg[:, at : at + n] = product(parts, high, low)
        at += n
    return at


def send_forward(v, blocks, msg, scalars):
    at = forward(v, blocks, msg)
    msg[:, at:] = pack_scalars(scalars, v.shape[0])


def forward_kernel(scaled, mag, *refs):
    forward(scaled[...] * mag[...], refs[:-1], refs[-1])


def begin_kernel(count, *refs):
    moments, penalty, mag, blocks = refs[:2], refs[2], refs[3], refs[4 : 4 + 2 * count]
    msg, direction, precond, residual = refs[4 + 2 * count :]
    sums = total(moments)
    m = mag[...]
    rows = penalty.shape[0]
    pre = spread(sums[0:2] * (m * m), rows) + penalty[...]
    res = spread(sums[2:4] * m, rows)
    s, v = held(res / pre, m)
    precond[...] = pre
    residual[...] = res
    direction[...] = s
    send_forward(v, blocks, msg, [row_sum(res * s), row_sum(s * s)])


def direction_scalars(sc, before_sc):
    rz, dd = sc[:, 0:1], sc[:, 1:2]
    if before_sc is None:
        return rz, dd, jnp.zeros_like(rz), jnp.zeros_like(rz)
    beta = rz / before_sc[:, 0:1]
    dot = sc[:, 2:3] + beta * before_sc[:, 1:2]
    return rz, dd + beta * (sc[:, 2:3] + dot), beta, dot


def adjoint(image_rows, before, kepts, blocks):
    half = kepts[0].shape[1]
    out = 0.0
    squares = cross = jnp.zeros((image_rows.shape[0], 1), f32)
    for j, (kept, high, low) in enumerate(zip(kepts, blocks[::2], blocks[1::2])):
        at = slice(j * half, (j + 1) * half)
        rows = image_rows[:, at]
        weighted = rows * kept[...]
        squares = squares + row_sum(weighted * rows)
        if before is not None:
            cross = cross + row_sum(weighted * before[:, at])
        out = out + product(split(weighted), high, low)
    return out, squares, cross


def adjoint_kernel(ny, count, first, *refs):
    parts, refs = refs[:ny], refs[ny:]
    kepts, blocks, refs = refs[:count], refs[count : 3 * count], refs[3 * count :]
    sums = total(parts)
    samples = kepts[0].shape[1] * count
    image_rows, sc = sums[:, :samples], sums[:, samples:]
    before, before_sc = (None, None) if first else refs[:2]
    partial, rows_out, sc_out = refs[-3:]
    rz, dd, beta, dot = direction_scalars(sc, before_sc)
    if not first:
        before = before[...]
        image_rows = image_rows + beta * before
    out, squares, cross = adjoint(image_rows, before, kepts, blocks)
    partial[...] = out
    rows_out[...] = image_rows
    sc_out[...] = pack_scalars([rz, dd, beta, dot, squares, cross], dd.shape[0])


def rest_kernel(ny, count, first, *refs):
    parts, refs = refs[:ny], refs[ny:]
    kepts, blocks, refs = refs[:count], refs[count : 3 * count], refs[3 * count :]
    sc, partial, refs = refs[0], refs[1], refs[2:]
    image_rows = total(parts)
    before = None
    if not first:
        before = refs[0][...]
        image_rows = image_rows + sc[:, 2:3] * before
    msg, rows_out = refs[-2:]
    out, squares, cross = adjoint(image_rows, before, kepts, blocks)
    features = out.shape[1]
    msg[:, :features] = partial[...] + out
    msg[:, features:] = pack_scalars([sc[:, 4:5] + squares, sc[:, 5:6] + cross], out.shape[0])
    rows_out[...] = image_rows


def update_kernel(count, first, last, *refs):
    parts, refs = refs[:2], refs[2:]
    sc, penalty, mag, precond, residual, scaled, rows, rest, refs = *refs[:8], refs[8:]
    blocks, refs = refs[: 2 * count], refs[2 * count :]
    sums = total(parts)
    features = mag.shape[1]
    lam, m = penalty[...], mag[...]
    direction = scaled[...]
    image_rows = jnp.concatenate([rows[...], rest[...]], axis=1)
    image = sums[:, :features] * m
    scalars = sums[:, features:]
    if first:
        image = image + lam * direction
    else:
        (before, weights, predicted, before_image, before_curve, before_rows, before_rest), refs = refs[:7], refs[7:]
        direction = direction + sc[:, 2:3] * before[...]
        extra = (scalars[:, 1:2] + lam * sc[:, 3:4]) / before_curve[:, 0:1]
        image = image + lam * direction - extra * before_image[...]
        direction = direction - extra * before[...]
        image_rows = image_rows - extra * jnp.concatenate([before_rows[...], before_rest[...]], axis=1)
    (msg, scaled_out, direction_out, weights_out, predicted_out), refs = refs[:5], refs[5:]
    curve = scalars[:, 0:1] + lam * sc[:, 1:2]
    step = sc[:, 0:1] / curve
    moved, fitted = step * direction, step * image_rows
    weights_out[...] = moved if first else weights[...] + moved
    predicted_out[...] = fitted if first else predicted[...] + fitted
    res = residual[...] - step * image
    s, v = held(res / precond[...], m)
    scaled_out[...] = s
    direction_out[...] = direction
    if last:
        refs[0][...] = image_rows
    else:
        refs[0][...] = res
        refs[1][...] = image
        refs[2][...] = pack_scalars([curve], curve.shape[0])
    send_forward(v, blocks, msg, [row_sum(res * s), row_sum(s * s), row_sum(s * direction)])


def fold_rows(value, fold):
    n = value.shape[0] // 2
    return jnp.where(fold == 0, value[:n], value[n:])


def last_kernel(ny, nz, *refs):
    parts, refs = refs[:ny], refs[ny:]
    kepts, (before, before_sc, predicted, msg, rows_out, sc_out) = refs[:nz], refs[nz:]
    sums = total(parts)
    half = kepts[0].shape[1]
    samples = half * nz
    rz, dd, beta, _ = direction_scalars(sums[:, samples:], before_sc)
    image_rows = sums[:, :samples] + beta * before[...]
    squares = jnp.zeros_like(dd)
    for j, kept in enumerate(kepts):
        rows = image_rows[:, j * half : (j + 1) * half]
        squares = squares + row_sum(rows * rows * kept[...])
    other = 1 - core()
    n = dd.shape[0] // 2
    msg[:n, :samples] = fold_rows(image_rows, other)
    msg[n:, :samples] = fold_rows(predicted[...], other)
    msg[:, samples:] = pack_scalars([squares], 2 * n)
    rows_out[...] = image_rows
    sc_out[...] = pack_scalars([rz, dd, beta], 2 * n)


def finish_kernel(nz, own, got, sc, penalty, scaled, before, weights, rows, predicted, *outs):
    samples, features = rows.shape[1], scaled.shape[1]
    half = samples // nz
    c = core()
    n = sc.shape[0] // 2
    step = sc[:, 0:1] / ((own[:, samples : samples + 1] + got[:, samples : samples + 1]) + penalty[...] * sc[:, 1:2])
    coefficients = weights[...] + step * (scaled[...] + sc[:, 2:3] * before[...])
    coefficients = fold_rows(coefficients, c)
    here = fold_rows(predicted[...] + step * rows[...], c)
    there = got[n:, :samples] + fold_rows(step, c) * got[:n, :samples]
    lower, upper = jnp.where(c == 0, here, there), jnp.where(c == 0, there, here)
    for j, out in enumerate(outs):
        out[:, :features] = coefficients
        out[:, features : features + half] = lower[:, j * half : (j + 1) * half]
        out[:, features + half :] = upper[:, j * half : (j + 1) * half]


def arrange_kernel(order, *refs):
    nz = len(order)
    parts, (weights_out, predictions_out, held) = refs[:nz], refs[nz:]
    features = weights_out.shape[1]
    n = weights_out.shape[0] // nz
    for j, part in zip(order, parts):
        held[j] = part[...]
    z = lax.axis_index("samp")
    for k in range(nz):
        part = held[lax.bitwise_xor(z, k)]
        weights_out[k * n : (k + 1) * n, :] = part[:, :features]
        predictions_out[k * n : (k + 1) * n, :] = part[:, features:]


ITERS = 3


def shards(
    nf,
    nz,
    ny,
    input_points,
    wave_numbers,
    offset_angles,
    feature_magnitudes,
    response_values,
    split_label,
    shrinkage_levels,
):
    shard, features = input_points.shape[0], wave_numbers.shape[1]
    depth = input_points.shape[1]
    levels = shrinkage_levels.shape[0]
    half, rows = shard // 2, 2 * (levels // nz)
    samples = half * nz
    tall = (shard // LANES, LANES)
    extra = pl.cdiv(4 * half // LANES, 16) * 16
    row_f, row_s, row_c = ((rows, features), f32), ((rows, samples), f32), ((rows, LANES), f32)
    msg_f, msg_s = ((rows, features + LANES), f32), ((rows, samples + LANES), f32)

    label = split_label.reshape(tall)
    other_label = flip(label, "fold", nf, 1)
    inputs = [input_points, wave_numbers, offset_angles.reshape(1, features), feature_magnitudes.reshape(1, features)]
    inputs += [response_values.reshape(tall), label, shrinkage_levels.reshape(1, levels)]
    vectors = [((1, features), f32), ((1, features), f32), (tall, f32), (tall, jnp.int32), ((1, levels), f32)]
    packed = ((half + extra, depth), bf16)
    msg, waves, offsets, mag, penalty, response, label = pl.pallas_call(
        functools.partial(pack_kernel, math.sqrt(2.0 / (features * ny))),
        out_shape=[
            pltpu.VMEM(*packed),
            pltpu.VMEM((depth, features), bf16),
            pltpu.VMEM((1, features), f32),
            pltpu.VMEM((1, features), f32),
            pltpu.VMEM((rows, 1), f32),
            pltpu.VMEM(tall, f32),
            pltpu.VMEM(tall, jnp.int32),
        ],
        in_specs=[pl.BlockSpec(memory_space=pltpu.HBM)] * len(inputs),
        scratch_shapes=[pltpu.VMEM((half, depth), bf16)]
        + [pltpu.VMEM(v, d) for v, d in vectors]
        + [pltpu.SemaphoreType.DMA((len(inputs),))],
        compiler_params=pltpu.CompilerParams(vmem_limit_bytes=VMEM_LIMIT),
    )(*[pltpu.with_memory_space_constraint(v, pltpu.HBM) for v in inputs])
    (msg,) = call(
        functools.partial(label_kernel, half), [packed], msg, label, other_label, response, aliases={0: 0}
    )

    order = [0] + [j for i in range(1, nz // 2 + 1) for j in sorted({nz - i, i}, reverse=True)]
    blocks, turned, kepts, moments = [], [], [], None
    shapes = (half, features), (features, half)
    tiles = [(shape, kind) for shape in shapes for kind in (bf16, f8)]
    for j in order:
        part = flip(msg, "samp", nz, j) if j else msg
        high, low, high_t, low_t, kept, moments = call(
            functools.partial(features_kernel, j == 0),
            [*tiles, ((rows, half), f32), ((4, features), f32)],
            part, waves, offsets, *(() if j == 0 else (moments,)),
            scratch=[pltpu.VMEM((2, 8, features), f32), pltpu.VMEM((2, half, LANES), f32)],
            flops=60 * half * features,
        )
        blocks += [high, low]
        turned += [high_t, low_t]
        kepts.append(kept)
    count, later = nz - 1, 1
    msg_a, row_a = ((rows, half * count + LANES), f32), ((rows, half * count), f32)
    row_b = ((rows, half * later), f32)
    work = 2 * 3 * rows * half * features
    msg, scaled, precond, residual = call(
        functools.partial(begin_kernel, count),
        [msg_a, row_f, row_f, row_f],
        moments, flip(moments, "fold", nf, 1), penalty, mag, *turned[: 2 * count],
        flops=work * count,
    )
    before = weights = predicted = image = curve = sc = rows_a = rows_b = None
    for it in range(ITERS - 1):
        first, last = it == 0, it == ITERS - 2
        parts = exchange(msg, "feat", ny)
        (msg_b,) = call(forward_kernel, [row_b], scaled, mag, *turned[2 * count :], flops=work * later)
        parts_b = exchange(msg_b, "feat", ny)
        partial, new_a, new_sc = call(
            functools.partial(adjoint_kernel, ny, count, first),
            [row_f, row_a, row_c],
            *parts, *kepts[:count], *blocks[: 2 * count], *(() if first else (rows_a, sc)),
            flops=work * count,
        )
        msg, new_b = call(
            functools.partial(rest_kernel, ny, later, first),
            [msg_f, row_b],
            *parts_b, *kepts[count:], *blocks[2 * count :], new_sc, partial, *(() if first else (rows_b,)),
            flops=work * later,
        )
        sc = new_sc
        msg, scaled, before, weights, predicted, *rest = call(
            functools.partial(update_kernel, nz if last else count, first, last),
            [msg_s if last else msg_a, row_f, row_f, row_f, row_s] + ([row_s] if last else [row_f, row_f, row_c]),
            msg, flip(msg, "fold", nf, 1), sc, penalty, mag, precond, residual, scaled, new_a, new_b,
            *(turned if last else turned[: 2 * count]),
            *(() if first else (before, weights, predicted, image, curve, rows_a, rows_b)),
            flops=work * count,
        )
        rows_a, rows_b = new_a, new_b
        residual, image, curve = (None, None, None) if last else rest
    msg, image_rows, sc = call(
        functools.partial(last_kernel, ny, nz),
        [msg_s, row_s, row_c],
        *exchange(msg, "feat", ny), *kepts, rest[0], sc, predicted,
    )
    outs = call(
        functools.partial(finish_kernel, nz),
        [((rows // 2, features + shard), f32)] * nz,
        msg, flip(msg, "fold", nf, 1), sc, penalty, scaled, before, weights, image_rows, predicted,
    )
    far_first = [0, *range(nz - 1, 0, -1)]
    outs = [flip(outs[order.index(j)], "samp", nz, j) if j else outs[0] for j in far_first]
    return call(
        functools.partial(arrange_kernel, far_first),
        [((levels, features), f32), ((levels, shard), f32)],
        *outs,
        scratch=[pltpu.VMEM((nz, rows // 2, features + shard), f32)],
        in_vmem=False,
    )


def solution(mesh):
    placed = (
        P("samp", None),
        P(None, "feat"),
        P("feat"),
        P("feat"),
        P("samp"),
        P(("fold", "samp")),
        P(),
    )
    sizes = [mesh.shape[axis] for axis in ("fold", "samp", "feat")]
    return jax.shard_map(
        functools.partial(shards, *sizes),
        mesh=mesh,
        in_specs=placed,
        out_specs=(P("fold", "feat"), P("fold", "samp")),
        check_vma=False,
    )
```

```python
import functools
import math

import jax
import jax.numpy as jnp
from jax import lax
from jax.experimental import pallas as pl
from jax.experimental.pallas import tpu as pltpu
from jax.sharding import PartitionSpec as P

f32, bf16, f8 = jnp.float32, jnp.bfloat16, jnp.float8_e4m3fn
TURN = 1.0 / (2.0 * math.pi)
SINE = (-6.283164044377446, 41.337142378931674, -81.34076911271806, 70.99343519544783)
LANES = 128
VMEM_LIMIT = 12 * 2**20
RAISE = 512.0


def call(body, outs, *args, flops=0, in_vmem=True, scratch=(), aliases={}):
    outs = [pltpu.VMEM(s, d) if in_vmem else jax.ShapeDtypeStruct(s, d) for s, d in outs]
    size = sum(math.prod(a.shape) * a.dtype.itemsize for a in args)
    return pl.pallas_call(
        body,
        out_shape=outs,
        scratch_shapes=list(scratch),
        input_output_aliases=aliases,
        compiler_params=pltpu.CompilerParams(vmem_limit_bytes=VMEM_LIMIT),
        cost_estimate=pl.CostEstimate(flops=flops, bytes_accessed=size, transcendentals=0),
    )(*args)


def total(refs):
    values = [r[...] for r in refs]
    while len(values) > 1:
        values = [values[i] + values[i + 1] for i in range(0, len(values), 2)]
    return values[0]


def halves(value):
    high = value.astype(bf16)
    return high, (value - high.astype(f32)).astype(bf16)


def split(rows):
    high, low = halves(rows)
    both = jnp.concatenate([high.astype(f32), low.astype(f32)], axis=0).astype(bf16)
    scale = 256.0 / jnp.maximum(jnp.max(jnp.abs(rows), axis=1, keepdims=True), 1e-30)
    scaled = rows * scale
    coarse = scaled.astype(f8).astype(f32)
    small = jnp.concatenate([coarse, (scaled - coarse) * 16.0], axis=0).astype(f8)
    return both, small, 1.0 / scale


def product(parts, high_ref, low_ref):
    both, small, back = parts
    n = back.shape[0]
    out = jnp.dot(both, high_ref[...], preferred_element_type=f32)
    fine = jnp.dot(small, low_ref[...], preferred_element_type=f32)
    return out[:n] + out[n:] + (fine[:n] + fine[n:] * 0.0625) * back


def held(scaled, mag):
    high, low = halves(scaled * mag)
    rounded = high.astype(f32) + low.astype(f32)
    return rounded / mag, rounded


def pack_scalars(columns, rows):
    lane = lax.broadcasted_iota(jnp.int32, (rows, LANES), 1)
    out = jnp.zeros((rows, LANES), f32)
    for i, column in enumerate(columns):
        out = jnp.where(lane == i, column, out)
    return out


def row_sum(value):
    return jnp.sum(value, axis=1, keepdims=True)


def flip(value, axis, n, s):
    return lax.ppermute(value, axis, [(i, i ^ s) for i in range(n)])


def exchange(value, axis, n):
    return [value] + [flip(value, axis, n, s) for s in range(1, n)]


def as_row(block):
    return jnp.concatenate([block[i : i + 1] for i in range(block.shape[0])], axis=1)


def spread(pair, rows):
    return jnp.concatenate(
        [jnp.broadcast_to(pair[e : e + 1], (rows // 2, pair.shape[1])) for e in (0, 1)], axis=0
    )


def core():
    return lax.rem(lax.axis_index("fold"), 2)


def pack_kernel(
    scale, x_hbm, w_hbm, offset_hbm, mag_hbm, response_hbm, label_hbm, penalty_hbm,
    msg, w_ref, offset_ref, mag_ref, penalty_ref, response_out, label_out,
    offset_in, mag_in, response_ref, label_ref, penalty_in, sems,
):
    half = x_hbm.shape[0] // 2
    c = core()
    pairs = [
        (x_hbm.at[pl.ds(pl.multiple_of(c * half, half), half), :], msg.at[pl.ds(0, half), :]),
        (label_hbm, label_ref), (response_hbm, response_ref), (w_hbm, w_ref),
        (offset_hbm, offset_in), (mag_hbm, mag_in), (penalty_hbm, penalty_in),
    ]
    copies = [pltpu.make_async_copy(a, b, sems.at[i]) for i, (a, b) in enumerate(pairs)]
    for copy in copies:
        copy.start()
    for copy in copies:
        copy.wait()
    msg[half:, :] = jnp.zeros_like(msg[half:, :])
    label_out[...] = label_ref[...]
    response_out[...] = response_ref[...]
    offset_ref[...] = offset_in[...] * TURN
    mag_ref[...] = mag_in[...] * (scale / RAISE)
    levels, rows = penalty_in.shape[1], penalty_ref.shape[0]
    row, column = [lax.broadcasted_iota(jnp.int32, (rows, levels), a) for a in (0, 1)]
    chosen = column == lax.axis_index("samp") * (rows // 2) + lax.rem(row, rows // 2)
    penalty_ref[...] = row_sum(jnp.where(chosen, penalty_in[...], 0.0))


def label_kernel(half, points, label, other_label, response, msg):
    n = half // LANES
    c = core()

    def mine(block):
        return jnp.where(c == 0, block[:n], block[n:])

    own = (mine(label[...]) != 0).astype(f32)
    other = (mine(other_label[...]) != 0).astype(f32)
    y = mine(response[...])
    high, low = halves(y)
    aux = [jnp.where(c == 0, own, other), jnp.where(c == 0, other, own)]
    aux += [v.astype(f32) for v in (high, low)]
    if msg.shape[0] - half > 4 * n:
        aux += [jnp.zeros((msg.shape[0] - half - 4 * n, LANES), f32)]
    msg[half:, :] = jnp.concatenate(aux, axis=0).astype(bf16)


def features_kernel(first, msg, w_ref, offset_ref, *refs):
    before, refs = (None, refs) if first else (refs[0], refs[1:])
    high_ref, low_ref, high_t, low_t, kept_ref, moment_ref, acc, mask = refs
    samples, features = high_ref.shape
    n = samples // LANES
    aux = msg[samples:, :].astype(f32)
    kept = jnp.concatenate([as_row(aux[e * n : (e + 1) * n]) for e in (0, 1)], axis=0)
    kept_ref[...] = spread(kept, kept_ref.shape[0])
    y = aux[2 * n : 3 * n] + aux[3 * n : 4 * n]
    y_high, y_low = halves(kept * as_row(y))
    y_both = jnp.concatenate([y_high.astype(f32), y_low.astype(f32)], axis=0).astype(bf16)
    columns = jnp.concatenate([kept, jnp.zeros((6, samples), f32)], axis=0).T
    for e in (0, 1):
        mask[e] = jnp.broadcast_to(columns[:, e : e + 1], (samples, LANES))
    cb = min(features, 256)
    for j in range(0, features, cb):
        a = jnp.dot(msg[:samples, :], w_ref[:, j : j + cb], preferred_element_type=f32)
        t = a * TURN + offset_ref[:, j : j + cb]
        r = t - jnp.round(t)
        q = jnp.abs(r) - 0.25
        u = q * q
        c = jnp.full_like(u, SINE[-1] * RAISE)
        for k in SINE[-2::-1]:
            c = c * u + k * RAISE
        c = c * q
        high, low = halves(c)
        high_ref[:, j : j + cb] = high
        small = (c - high.astype(f32)).astype(f8)
        low_ref[:, j : j + cb] = small
        high_t[j : j + cb, :] = high.T
        low_t[j : j + cb, :] = small.T
        square = c * c
        for e in (0, 1):
            part = square * jnp.concatenate([mask[e]] * (cb // LANES), axis=1)
            acc[e, :, j : j + cb] = part.reshape(samples // 8, 8, cb).sum(0)
        side = jnp.dot(y_both, high, preferred_element_type=f32)
        side = side[:2] + side[2:] + jnp.dot(y_high, low, preferred_element_type=f32)
        moment_ref[2:4, j : j + cb] = side if first else before[2:4, j : j + cb] + side
    for e in (0, 1):
        square = jnp.sum(acc[e], axis=0, keepdims=True)
        moment_ref[e : e + 1, :] = square if first else before[e : e + 1, :] + square


def forward(v, blocks, msg):
    at, parts = 0, split(v)
    for high, low in zip(blocks[::2], blocks[1::2]):
        n = high.shape[1]
        msg[:, at : at + n] = product(parts, high, low)
        at += n
    return at


def send_forward(v, blocks, msg, scalars):
    at = forward(v, blocks, msg)
    msg[:, at:] = pack_scalars(scalars, v.shape[0])


def forward_kernel(scaled, mag, *refs):
    forward(scaled[...] * mag[...], refs[:-1], refs[-1])


def begin_kernel(count, *refs):
    moments, penalty, mag, blocks = refs[:2], refs[2], refs[3], refs[4 : 4 + 2 * count]
    msg, direction, precond, residual = refs[4 + 2 * count :]
    sums = total(moments)
    m = mag[...]
    rows = penalty.shape[0]
    pre = spread(sums[0:2] * (m * m), rows) + penalty[...]
    res = spread(sums[2:4] * m, rows)
    s, v = held(res / pre, m)
    precond[...] = pre
    residual[...] = res
    direction[...] = s
    send_forward(v, blocks, msg, [row_sum(res * s), row_sum(s * s)])


def direction_scalars(sc, before_sc):
    rz, dd = sc[:, 0:1], sc[:, 1:2]
    if before_sc is None:
        return rz, dd, jnp.zeros_like(rz), jnp.zeros_like(rz)
    beta = rz / before_sc[:, 0:1]
    dot = sc[:, 2:3] + beta * before_sc[:, 1:2]
    return rz, dd + beta * (sc[:, 2:3] + dot), beta, dot


def adjoint(image_rows, before, kepts, blocks):
    half = kepts[0].shape[1]
    out = 0.0
    squares = cross = jnp.zeros((image_rows.shape[0], 1), f32)
    for j, (kept, high, low) in enumerate(zip(kepts, blocks[::2], blocks[1::2])):
        at = slice(j * half, (j + 1) * half)
        rows = image_rows[:, at]
        weighted = rows * kept[...]
        squares = squares + row_sum(weighted * rows)
        if before is not None:
            cross = cross + row_sum(weighted * before[:, at])
        out = out + product(split(weighted), high, low)
    return out, squares, cross


def adjoint_kernel(ny, count, first, *refs):
    parts, refs = refs[:ny], refs[ny:]
    kepts, blocks, refs = refs[:count], refs[count : 3 * count], refs[3 * count :]
    sums = total(parts)
    samples = kepts[0].shape[1] * count
    image_rows, sc = sums[:, :samples], sums[:, samples:]
    before, before_sc = (None, None) if first else refs[:2]
    partial, rows_out, sc_out = refs[-3:]
    rz, dd, beta, dot = direction_scalars(sc, before_sc)
    if not first:
        before = before[...]
        image_rows = image_rows + beta * before
    out, squares, cross = adjoint(image_rows, before, kepts, blocks)
    partial[...] = out
    rows_out[...] = image_rows
    sc_out[...] = pack_scalars([rz, dd, beta, dot, squares, cross], dd.shape[0])


def rest_kernel(ny, count, first, *refs):
    parts, refs = refs[:ny], refs[ny:]
    kepts, blocks, refs = refs[:count], refs[count : 3 * count], refs[3 * count :]
    sc, partial, refs = refs[0], refs[1], refs[2:]
    image_rows = total(parts)
    before = None
    if not first:
        before = refs[0][...]
        image_rows = image_rows + sc[:, 2:3] * before
    msg, rows_out = refs[-2:]
    out, squares, cross = adjoint(image_rows, before, kepts, blocks)
    features = out.shape[1]
    msg[:, :features] = partial[...] + out
    msg[:, features:] = pack_scalars([sc[:, 4:5] + squares, sc[:, 5:6] + cross], out.shape[0])
    rows_out[...] = image_rows


def update_kernel(count, first, last, *refs):
    parts, refs = refs[:2], refs[2:]
    sc, penalty, mag, precond, residual, scaled, rows, rest, refs = *refs[:8], refs[8:]
    blocks, refs = refs[: 2 * count], refs[2 * count :]
    sums = total(parts)
    features = mag.shape[1]
    lam, m = penalty[...], mag[...]
    direction = scaled[...]
    image_rows = jnp.concatenate([rows[...], rest[...]], axis=1)
    image = sums[:, :features] * m
    scalars = sums[:, features:]
    if first:
        image = image + lam * direction
    else:
        (before, weights, predicted, before_image, before_curve, before_rows, before_rest), refs = refs[:7], refs[7:]
        direction = direction + sc[:, 2:3] * before[...]
        extra = (scalars[:, 1:2] + lam * sc[:, 3:4]) / before_curve[:, 0:1]
        image = image + lam * direction - extra * before_image[...]
        direction = direction - extra * before[...]
        image_rows = image_rows - extra * jnp.concatenate([before_rows[...], before_rest[...]], axis=1)
    (msg, scaled_out, direction_out, weights_out, predicted_out), refs = refs[:5], refs[5:]
    curve = scalars[:, 0:1] + lam * sc[:, 1:2]
    step = sc[:, 0:1] / curve
    moved, fitted = step * direction, step * image_rows
    weights_out[...] = moved if first else weights[...] + moved
    predicted_out[...] = fitted if first else predicted[...] + fitted
    res = residual[...] - step * image
    s, v = held(res / precond[...], m)
    scaled_out[...] = s
    direction_out[...] = direction
    if last:
        refs[0][...] = image_rows
    else:
        refs[0][...] = res
        refs[1][...] = image
        refs[2][...] = pack_scalars([curve], curve.shape[0])
    send_forward(v, blocks, msg, [row_sum(res * s), row_sum(s * s), row_sum(s * direction)])


def fold_rows(value, fold):
    n = value.shape[0] // 2
    return jnp.where(fold == 0, value[:n], value[n:])


def last_kernel(ny, nz, *refs):
    parts, refs = refs[:ny], refs[ny:]
    kepts, (before, before_sc, predicted, msg, rows_out, sc_out) = refs[:nz], refs[nz:]
    sums = total(parts)
    half = kepts[0].shape[1]
    samples = half * nz
    rz, dd, beta, _ = direction_scalars(sums[:, samples:], before_sc)
    image_rows = sums[:, :samples] + beta * before[...]
    squares = jnp.zeros_like(dd)
    for j, kept in enumerate(kepts):
        rows = image_rows[:, j * half : (j + 1) * half]
        squares = squares + row_sum(rows * rows * kept[...])
    other = 1 - core()
    n = dd.shape[0] // 2
    msg[:n, :samples] = fold_rows(image_rows, other)
    msg[n:, :samples] = fold_rows(predicted[...], other)
    msg[:, samples:] = pack_scalars([squares], 2 * n)
    rows_out[...] = image_rows
    sc_out[...] = pack_scalars([rz, dd, beta], 2 * n)


def finish_kernel(nz, own, got, sc, penalty, scaled, before, weights, rows, predicted, *outs):
    samples, features = rows.shape[1], scaled.shape[1]
    half = samples // nz
    c = core()
    n = sc.shape[0] // 2
    step = sc[:, 0:1] / ((own[:, samples : samples + 1] + got[:, samples : samples + 1]) + penalty[...] * sc[:, 1:2])
    coefficients = weights[...] + step * (scaled[...] + sc[:, 2:3] * before[...])
    coefficients = fold_rows(coefficients, c)
    here = fold_rows(predicted[...] + step * rows[...], c)
    there = got[n:, :samples] + fold_rows(step, c) * got[:n, :samples]
    lower, upper = jnp.where(c == 0, here, there), jnp.where(c == 0, there, here)
    for j, out in enumerate(outs):
        out[:, :features] = coefficients
        out[:, features : features + half] = lower[:, j * half : (j + 1) * half]
        out[:, features + half :] = upper[:, j * half : (j + 1) * half]


def arrange_kernel(order, *refs):
    nz = len(order)
    parts, (weights_out, predictions_out, held) = refs[:nz], refs[nz:]
    features = weights_out.shape[1]
    n = weights_out.shape[0] // nz
    for j, part in zip(order, parts):
        held[j] = part[...]
    z = lax.axis_index("samp")
    for k in range(nz):
        part = held[lax.bitwise_xor(z, k)]
        weights_out[k * n : (k + 1) * n, :] = part[:, :features]
        predictions_out[k * n : (k + 1) * n, :] = part[:, features:]


ITERS = 3


def shards(
    nf,
    nz,
    ny,
    input_points,
    wave_numbers,
    offset_angles,
    feature_magnitudes,
    response_values,
    split_label,
    shrinkage_levels,
):
    shard, features = input_points.shape[0], wave_numbers.shape[1]
    depth = input_points.shape[1]
    levels = shrinkage_levels.shape[0]
    half, rows = shard // 2, 2 * (levels // nz)
    samples = half * nz
    tall = (shard // LANES, LANES)
    extra = pl.cdiv(4 * half // LANES, 16) * 16
    row_f, row_s, row_c = ((rows, features), f32), ((rows, samples), f32), ((rows, LANES), f32)
    msg_f, msg_s = ((rows, features + LANES), f32), ((rows, samples + LANES), f32)

    label = split_label.reshape(tall)
    other_label = flip(label, "fold", nf, 1)
    inputs = [input_points, wave_numbers, offset_angles.reshape(1, features), feature_magnitudes.reshape(1, features)]
    inputs += [response_values.reshape(tall), label, shrinkage_levels.reshape(1, levels)]
    vectors = [((1, features), f32), ((1, features), f32), (tall, f32), (tall, jnp.int32), ((1, levels), f32)]
    packed = ((half + extra, depth), bf16)
    msg, waves, offsets, mag, penalty, response, label = pl.pallas_call(
        functools.partial(pack_kernel, math.sqrt(2.0 / (features * ny))),
        out_shape=[
            pltpu.VMEM(*packed),
            pltpu.VMEM((depth, features), bf16),
            pltpu.VMEM((1, features), f32),
            pltpu.VMEM((1, features), f32),
            pltpu.VMEM((rows, 1), f32),
            pltpu.VMEM(tall, f32),
            pltpu.VMEM(tall, jnp.int32),
        ],
        in_specs=[pl.BlockSpec(memory_space=pltpu.HBM)] * len(inputs),
        scratch_shapes=[pltpu.VMEM(v, d) for v, d in vectors]
        + [pltpu.SemaphoreType.DMA((len(inputs),))],
        compiler_params=pltpu.CompilerParams(vmem_limit_bytes=VMEM_LIMIT),
    )(*[pltpu.with_memory_space_constraint(v, pltpu.HBM) for v in inputs])
    (msg,) = call(
        functools.partial(label_kernel, half), [packed], msg, label, other_label, response, aliases={0: 0}
    )

    order = [0] + [j for i in range(1, nz // 2 + 1) for j in sorted({nz - i, i}, reverse=True)]
    blocks, turned, kepts, moments = [], [], [], None
    shapes = (half, features), (features, half)
    tiles = [(shape, kind) for shape in shapes for kind in (bf16, f8)]
    for j in order:
        part = flip(msg, "samp", nz, j) if j else msg
        high, low, high_t, low_t, kept, moments = call(
            functools.partial(features_kernel, j == 0),
            [*tiles, ((rows, half), f32), ((4, features), f32)],
            part, waves, offsets, *(() if j == 0 else (moments,)),
            scratch=[pltpu.VMEM((2, 8, features), f32), pltpu.VMEM((2, half, LANES), f32)],
            flops=60 * half * features,
        )
        blocks += [high, low]
        turned += [high_t, low_t]
        kepts.append(kept)
    count, later = nz - 1, 1
    msg_a, row_a = ((rows, half * count + LANES), f32), ((rows, half * count), f32)
    row_b = ((rows, half * later), f32)
    work = 2 * 3 * rows * half * features
    msg, scaled, precond, residual = call(
        functools.partial(begin_kernel, count),
        [msg_a, row_f, row_f, row_f],
        moments, flip(moments, "fold", nf, 1), penalty, mag, *turned[: 2 * count],
        flops=work * count,
    )
    before = weights = predicted = image = curve = sc = rows_a = rows_b = None
    for it in range(ITERS - 1):
        first, last = it == 0, it == ITERS - 2
        parts = exchange(msg, "feat", ny)
        (msg_b,) = call(forward_kernel, [row_b], scaled, mag, *turned[2 * count :], flops=work * later)
        parts_b = exchange(msg_b, "feat", ny)
        partial, new_a, new_sc = call(
            functools.partial(adjoint_kernel, ny, count, first),
            [row_f, row_a, row_c],
            *parts, *kepts[:count], *blocks[: 2 * count], *(() if first else (rows_a, sc)),
            flops=work * count,
        )
        msg, new_b = call(
            functools.partial(rest_kernel, ny, later, first),
            [msg_f, row_b],
            *parts_b, *kepts[count:], *blocks[2 * count :], new_sc, partial, *(() if first else (rows_b,)),
            flops=work * later,
        )
        sc = new_sc
        msg, scaled, before, weights, predicted, *rest = call(
            functools.partial(update_kernel, nz if last else count, first, last),
            [msg_s if last else msg_a, row_f, row_f, row_f, row_s] + ([row_s] if last else [row_f, row_f, row_c]),
            msg, flip(msg, "fold", nf, 1), sc, penalty, mag, precond, residual, scaled, new_a, new_b,
            *(turned if last else turned[: 2 * count]),
            *(() if first else (before, weights, predicted, image, curve, rows_a, rows_b)),
            flops=work * count,
        )
        rows_a, rows_b = new_a, new_b
        residual, image, curve = (None, None, None) if last else rest
    msg, image_rows, sc = call(
        functools.partial(last_kernel, ny, nz),
        [msg_s, row_s, row_c],
        *exchange(msg, "feat", ny), *kepts, rest[0], sc, predicted,
    )
    outs = call(
        functools.partial(finish_kernel, nz),
        [((rows // 2, features + shard), f32)] * nz,
        msg, flip(msg, "fold", nf, 1), sc, penalty, scaled, before, weights, image_rows, predicted,
    )
    far_first = [0, *range(nz - 1, 0, -1)]
    outs = [flip(outs[order.index(j)], "samp", nz, j) if j else outs[0] for j in far_first]
    return call(
        functools.partial(arrange_kernel, far_first),
        [((levels, features), f32), ((levels, shard), f32)],
        *outs,
        scratch=[pltpu.VMEM((nz, rows // 2, features + shard), f32)],
        in_vmem=False,
    )


def solution(mesh):
    placed = (
        P("samp", None),
        P(None, "feat"),
        P("feat"),
        P("feat"),
        P("samp"),
        P(("fold", "samp")),
        P(),
    )
    sizes = [mesh.shape[axis] for axis in ("fold", "samp", "feat")]
    return jax.shard_map(
        functools.partial(shards, *sizes),
        mesh=mesh,
        in_specs=placed,
        out_specs=(P("fold", "feat"), P("fold", "samp")),
        check_vma=False,
    )
```

```python
import functools
import math

import jax
import jax.numpy as jnp
from jax import lax
from jax.experimental import pallas as pl
from jax.experimental.pallas import tpu as pltpu
from jax.sharding import PartitionSpec as P

f32, bf16, f8 = jnp.float32, jnp.bfloat16, jnp.float8_e4m3fn
TURN = 1.0 / (2.0 * math.pi)
SINE = (-6.283164044377446, 41.337142378931674, -81.34076911271806, 70.99343519544783)
LANES = 128
VMEM_LIMIT = 12 * 2**20
RAISE = 512.0


def call(body, outs, *args, flops=0, in_vmem=True, scratch=(), aliases={}):
    outs = [pltpu.VMEM(s, d) if in_vmem else jax.ShapeDtypeStruct(s, d) for s, d in outs]
    size = sum(math.prod(a.shape) * a.dtype.itemsize for a in args)
    return pl.pallas_call(
        body,
        out_shape=outs,
        scratch_shapes=list(scratch),
        input_output_aliases=aliases,
        compiler_params=pltpu.CompilerParams(vmem_limit_bytes=VMEM_LIMIT),
        cost_estimate=pl.CostEstimate(flops=flops, bytes_accessed=size, transcendentals=0),
    )(*args)


def total(refs):
    values = [r[...] for r in refs]
    while len(values) > 1:
        values = [values[i] + values[i + 1] for i in range(0, len(values), 2)]
    return values[0]


def halves(value):
    high = value.astype(bf16)
    return high, (value - high.astype(f32)).astype(bf16)


def split(rows):
    high, low = halves(rows)
    both = jnp.concatenate([high.astype(f32), low.astype(f32)], axis=0).astype(bf16)
    scale = 256.0 / jnp.maximum(jnp.max(jnp.abs(rows), axis=1, keepdims=True), 1e-30)
    scaled = rows * scale
    coarse = scaled.astype(f8).astype(f32)
    small = jnp.concatenate([coarse, (scaled - coarse) * 16.0], axis=0).astype(f8)
    return both, small, 1.0 / scale


def product(parts, high_ref, low_ref):
    both, small, back = parts
    n = back.shape[0]
    out = jnp.dot(both, high_ref[...], preferred_element_type=f32)
    fine = jnp.dot(small, low_ref[...], preferred_element_type=f32)
    return out[:n] + out[n:] + (fine[:n] + fine[n:] * 0.0625) * back


def held(scaled, mag):
    high, low = halves(scaled * mag)
    rounded = high.astype(f32) + low.astype(f32)
    return rounded / mag, rounded


def pack_scalars(columns, rows):
    lane = lax.broadcasted_iota(jnp.int32, (rows, LANES), 1)
    out = jnp.zeros((rows, LANES), f32)
    for i, column in enumerate(columns):
        out = jnp.where(lane == i, column, out)
    return out


def row_sum(value):
    return jnp.sum(value, axis=1, keepdims=True)


def flip(value, axis, n, s):
    return lax.ppermute(value, axis, [(i, i ^ s) for i in range(n)])


def exchange(value, axis, n):
    return [value] + [flip(value, axis, n, s) for s in range(1, n)]


def as_row(block):
    return jnp.concatenate([block[i : i + 1] for i in range(block.shape[0])], axis=1)


def spread(pair, rows):
    return jnp.concatenate(
        [jnp.broadcast_to(pair[e : e + 1], (rows // 2, pair.shape[1])) for e in (0, 1)], axis=0
    )


def core():
    return lax.rem(lax.axis_index("fold"), 2)


def pack_kernel(
    scale, x_hbm, w_hbm, offset_hbm, mag_hbm, response_hbm, label_hbm, penalty_hbm,
    msg, w_ref, offset_ref, mag_ref, penalty_ref, response_out, label_out,
    offset_in, mag_in, response_ref, label_ref, penalty_in, sems,
):
    half = x_hbm.shape[0] // 2
    c = core()
    pairs = [
        (x_hbm.at[pl.ds(pl.multiple_of(c * half, half), half), :], msg.at[pl.ds(0, half), :]),
        (label_hbm, label_ref), (response_hbm, response_ref), (w_hbm, w_ref),
        (offset_hbm, offset_in), (mag_hbm, mag_in), (penalty_hbm, penalty_in),
    ]
    copies = [pltpu.make_async_copy(a, b, sems.at[i]) for i, (a, b) in enumerate(pairs)]
    for copy in copies:
        copy.start()
    for copy in copies:
        copy.wait()
    msg[half:, :] = jnp.zeros_like(msg[half:, :])
    label_out[...] = label_ref[...]
    response_out[...] = response_ref[...]
    offset_ref[...] = offset_in[...] * TURN
    mag_ref[...] = mag_in[...] * (scale / RAISE)
    levels, rows = penalty_in.shape[1], penalty_ref.shape[0]
    row, column = [lax.broadcasted_iota(jnp.int32, (rows, levels), a) for a in (0, 1)]
    chosen = column == lax.axis_index("samp") * (rows // 2) + lax.rem(row, rows // 2)
    penalty_ref[...] = row_sum(jnp.where(chosen, penalty_in[...], 0.0))


def label_kernel(half, points, label, other_label, response, msg):
    n = half // LANES
    c = core()

    def mine(block):
        return jnp.where(c == 0, block[:n], block[n:])

    own = (mine(label[...]) != 0).astype(f32)
    other = (mine(other_label[...]) != 0).astype(f32)
    y = mine(response[...])
    high, low = halves(y)
    aux = [jnp.where(c == 0, own, other), jnp.where(c == 0, other, own)]
    aux += [v.astype(f32) for v in (high, low)]
    if msg.shape[0] - half > 4 * n:
        aux += [jnp.zeros((msg.shape[0] - half - 4 * n, LANES), f32)]
    msg[half:, :] = jnp.concatenate(aux, axis=0).astype(bf16)


def features_kernel(first, msg, w_ref, offset_ref, *refs):
    before, refs = (None, refs) if first else (refs[0], refs[1:])
    high_ref, low_ref, high_t, low_t, kept_ref, moment_ref, acc, mask = refs
    samples, features = high_ref.shape
    n = samples // LANES
    aux = msg[samples:, :].astype(f32)
    kept = jnp.concatenate([as_row(aux[e * n : (e + 1) * n]) for e in (0, 1)], axis=0)
    kept_ref[...] = spread(kept, kept_ref.shape[0])
    y = aux[2 * n : 3 * n] + aux[3 * n : 4 * n]
    y_high, y_low = halves(kept * as_row(y))
    y_both = jnp.concatenate([y_high.astype(f32), y_low.astype(f32)], axis=0).astype(bf16)
    columns = jnp.concatenate([kept, jnp.zeros((6, samples), f32)], axis=0).T
    for e in (0, 1):
        mask[e] = jnp.broadcast_to(columns[:, e : e + 1], (samples, LANES))
    cb = min(features, 256)
    for j in range(0, features, cb):
        a = jnp.dot(msg[:samples, :], w_ref[:, j : j + cb], preferred_element_type=f32)
        t = a * TURN + offset_ref[:, j : j + cb]
        r = t - jnp.round(t)
        q = jnp.abs(r) - 0.25
        u = q * q
        c = jnp.full_like(u, SINE[-1] * RAISE)
        for k in SINE[-2::-1]:
            c = c * u + k * RAISE
        c = c * q
        high, low = halves(c)
        high_ref[:, j : j + cb] = high
        small = (c - high.astype(f32)).astype(f8)
        low_ref[:, j : j + cb] = small
        high_t[j : j + cb, :] = high.T
        low_t[j : j + cb, :] = small.T
        square = c * c
        for e in (0, 1):
            part = square * jnp.concatenate([mask[e]] * (cb // LANES), axis=1)
            acc[e, :, j : j + cb] = part.reshape(samples // 8, 8, cb).sum(0)
        side = jnp.dot(y_both, high, preferred_element_type=f32)
        fine = jnp.dot(y_both, low, preferred_element_type=f32)
        side = side[:2] + side[2:] + (fine[:2] + fine[2:])
        moment_ref[2:4, j : j + cb] = side if first else before[2:4, j : j + cb] + side
    for e in (0, 1):
        square = jnp.sum(acc[e], axis=0, keepdims=True)
        moment_ref[e : e + 1, :] = square if first else before[e : e + 1, :] + square


def forward(v, blocks, msg):
    at, parts = 0, split(v)
    for high, low in zip(blocks[::2], blocks[1::2]):
        n = high.shape[1]
        msg[:, at : at + n] = product(parts, high, low)
        at += n
    return at


def send_forward(v, blocks, msg, scalars):
    at = forward(v, blocks, msg)
    msg[:, at:] = pack_scalars(scalars, v.shape[0])


def forward_kernel(scaled, mag, *refs):
    forward(scaled[...] * mag[...], refs[:-1], refs[-1])


def begin_kernel(count, *refs):
    moments, penalty, mag, blocks = refs[:2], refs[2], refs[3], refs[4 : 4 + 2 * count]
    msg, direction, precond, residual = refs[4 + 2 * count :]
    sums = total(moments)
    m = mag[...]
    rows = penalty.shape[0]
    pre = spread(sums[0:2] * (m * m), rows) + penalty[...]
    res = spread(sums[2:4] * m, rows)
    s, v = held(res / pre, m)
    precond[...] = pre
    residual[...] = res
    direction[...] = s
    send_forward(v, blocks, msg, [row_sum(res * s), row_sum(s * s)])


def direction_scalars(sc, before_sc):
    rz, dd = sc[:, 0:1], sc[:, 1:2]
    if before_sc is None:
        return rz, dd, jnp.zeros_like(rz), jnp.zeros_like(rz)
    beta = rz / before_sc[:, 0:1]
    dot = sc[:, 2:3] + beta * before_sc[:, 1:2]
    return rz, dd + beta * (sc[:, 2:3] + dot), beta, dot


def adjoint(image_rows, before, kepts, blocks):
    half = kepts[0].shape[1]
    out = 0.0
    squares = cross = jnp.zeros((image_rows.shape[0], 1), f32)
    for j, (kept, high, low) in enumerate(zip(kepts, blocks[::2], blocks[1::2])):
        at = slice(j * half, (j + 1) * half)
        rows = image_rows[:, at]
        weighted = rows * kept[...]
        squares = squares + row_sum(weighted * rows)
        if before is not None:
            cross = cross + row_sum(weighted * before[:, at])
        out = out + product(split(weighted), high, low)
    return out, squares, cross


def adjoint_kernel(ny, count, first, *refs):
    parts, refs = refs[:ny], refs[ny:]
    kepts, blocks, refs = refs[:count], refs[count : 3 * count], refs[3 * count :]
    sums = total(parts)
    samples = kepts[0].shape[1] * count
    image_rows, sc = sums[:, :samples], sums[:, samples:]
    before, before_sc = (None, None) if first else refs[:2]
    partial, rows_out, sc_out = refs[-3:]
    rz, dd, beta, dot = direction_scalars(sc, before_sc)
    if not first:
        before = before[...]
        image_rows = image_rows + beta * before
    out, squares, cross = adjoint(image_rows, before, kepts, blocks)
    partial[...] = out
    rows_out[...] = image_rows
    sc_out[...] = pack_scalars([rz, dd, beta, dot, squares, cross], dd.shape[0])


def rest_kernel(ny, count, first, *refs):
    parts, refs = refs[:ny], refs[ny:]
    kepts, blocks, refs = refs[:count], refs[count : 3 * count], refs[3 * count :]
    sc, partial, refs = refs[0], refs[1], refs[2:]
    image_rows = total(parts)
    before = None
    if not first:
        before = refs[0][...]
        image_rows = image_rows + sc[:, 2:3] * before
    msg, rows_out = refs[-2:]
    out, squares, cross = adjoint(image_rows, before, kepts, blocks)
    features = out.shape[1]
    msg[:, :features] = partial[...] + out
    msg[:, features:] = pack_scalars([sc[:, 4:5] + squares, sc[:, 5:6] + cross], out.shape[0])
    rows_out[...] = image_rows


def update_kernel(count, first, last, *refs):
    parts, refs = refs[:2], refs[2:]
    sc, penalty, mag, precond, residual, scaled, rows, rest, refs = *refs[:8], refs[8:]
    blocks, refs = refs[: 2 * count], refs[2 * count :]
    sums = total(parts)
    features = mag.shape[1]
    lam, m = penalty[...], mag[...]
    direction = scaled[...]
    image_rows = jnp.concatenate([rows[...], rest[...]], axis=1)
    image = sums[:, :features] * m
    scalars = sums[:, features:]
    if first:
        image = image + lam * direction
    else:
        (before, weights, predicted, before_image, before_curve, before_rows, before_rest), refs = refs[:7], refs[7:]
        direction = direction + sc[:, 2:3] * before[...]
        extra = (scalars[:, 1:2] + lam * sc[:, 3:4]) / before_curve[:, 0:1]
        image = image + lam * direction - extra * before_image[...]
        direction = direction - extra * before[...]
        image_rows = image_rows - extra * jnp.concatenate([before_rows[...], before_rest[...]], axis=1)
    (msg, scaled_out, direction_out, weights_out, predicted_out), refs = refs[:5], refs[5:]
    curve = scalars[:, 0:1] + lam * sc[:, 1:2]
    step = sc[:, 0:1] / curve
    moved, fitted = step * direction, step * image_rows
    weights_out[...] = moved if first else weights[...] + moved
    predicted_out[...] = fitted if first else predicted[...] + fitted
    res = residual[...] - step * image
    s, v = held(res / precond[...], m)
    scaled_out[...] = s
    direction_out[...] = direction
    if last:
        refs[0][...] = image_rows
    else:
        refs[0][...] = res
        refs[1][...] = image
        refs[2][...] = pack_scalars([curve], curve.shape[0])
    send_forward(v, blocks, msg, [row_sum(res * s), row_sum(s * s), row_sum(s * direction)])


def fold_rows(value, fold):
    n = value.shape[0] // 2
    return jnp.where(fold == 0, value[:n], value[n:])


def last_kernel(ny, nz, *refs):
    parts, refs = refs[:ny], refs[ny:]
    kepts, (before, before_sc, predicted, msg, rows_out, sc_out) = refs[:nz], refs[nz:]
    sums = total(parts)
    half = kepts[0].shape[1]
    samples = half * nz
    rz, dd, beta, _ = direction_scalars(sums[:, samples:], before_sc)
    image_rows = sums[:, :samples] + beta * before[...]
    squares = jnp.zeros_like(dd)
    for j, kept in enumerate(kepts):
        rows = image_rows[:, j * half : (j + 1) * half]
        squares = squares + row_sum(rows * rows * kept[...])
    other = 1 - core()
    n = dd.shape[0] // 2
    msg[:n, :samples] = fold_rows(image_rows, other)
    msg[n:, :samples] = fold_rows(predicted[...], other)
    msg[:, samples:] = pack_scalars([squares], 2 * n)
    rows_out[...] = image_rows
    sc_out[...] = pack_scalars([rz, dd, beta], 2 * n)


def finish_kernel(nz, own, got, sc, penalty, scaled, before, weights, rows, predicted, *outs):
    samples, features = rows.shape[1], scaled.shape[1]
    half = samples // nz
    c = core()
    n = sc.shape[0] // 2
    step = sc[:, 0:1] / ((own[:, samples : samples + 1] + got[:, samples : samples + 1]) + penalty[...] * sc[:, 1:2])
    coefficients = weights[...] + step * (scaled[...] + sc[:, 2:3] * before[...])
    coefficients = fold_rows(coefficients, c)
    here = fold_rows(predicted[...] + step * rows[...], c)
    there = got[n:, :samples] + fold_rows(step, c) * got[:n, :samples]
    lower, upper = jnp.where(c == 0, here, there), jnp.where(c == 0, there, here)
    for j, out in enumerate(outs):
        out[:, :features] = coefficients
        out[:, features : features + half] = lower[:, j * half : (j + 1) * half]
        out[:, features + half :] = upper[:, j * half : (j + 1) * half]


def arrange_kernel(order, *refs):
    nz = len(order)
    parts, (weights_out, predictions_out, held) = refs[:nz], refs[nz:]
    features = weights_out.shape[1]
    n = weights_out.shape[0] // nz
    for j, part in zip(order, parts):
        held[j] = part[...]
    z = lax.axis_index("samp")
    for k in range(nz):
        part = held[lax.bitwise_xor(z, k)]
        weights_out[k * n : (k + 1) * n, :] = part[:, :features]
        predictions_out[k * n : (k + 1) * n, :] = part[:, features:]


ITERS = 3


def shards(
    nf,
    nz,
    ny,
    input_points,
    wave_numbers,
    offset_angles,
    feature_magnitudes,
    response_values,
    split_label,
    shrinkage_levels,
):
    shard, features = input_points.shape[0], wave_numbers.shape[1]
    depth = input_points.shape[1]
    levels = shrinkage_levels.shape[0]
    half, rows = shard // 2, 2 * (levels // nz)
    samples = half * nz
    tall = (shard // LANES, LANES)
    extra = pl.cdiv(4 * half // LANES, 16) * 16
    row_f, row_s, row_c = ((rows, features), f32), ((rows, samples), f32), ((rows, LANES), f32)
    msg_f, msg_s = ((rows, features + LANES), f32), ((rows, samples + LANES), f32)

    label = split_label.reshape(tall)
    other_label = flip(label, "fold", nf, 1)
    inputs = [input_points, wave_numbers, offset_angles.reshape(1, features), feature_magnitudes.reshape(1, features)]
    inputs += [response_values.reshape(tall), label, shrinkage_levels.reshape(1, levels)]
    vectors = [((1, features), f32), ((1, features), f32), (tall, f32), (tall, jnp.int32), ((1, levels), f32)]
    packed = ((half + extra, depth), bf16)
    msg, waves, offsets, mag, penalty, response, label = pl.pallas_call(
        functools.partial(pack_kernel, math.sqrt(2.0 / (features * ny))),
        out_shape=[
            pltpu.VMEM(*packed),
            pltpu.VMEM((depth, features), bf16),
            pltpu.VMEM((1, features), f32),
            pltpu.VMEM((1, features), f32),
            pltpu.VMEM((rows, 1), f32),
            pltpu.VMEM(tall, f32),
            pltpu.VMEM(tall, jnp.int32),
        ],
        in_specs=[pl.BlockSpec(memory_space=pltpu.HBM)] * len(inputs),
        scratch_shapes=[pltpu.VMEM(v, d) for v, d in vectors]
        + [pltpu.SemaphoreType.DMA((len(inputs),))],
        compiler_params=pltpu.CompilerParams(vmem_limit_bytes=VMEM_LIMIT),
    )(*[pltpu.with_memory_space_constraint(v, pltpu.HBM) for v in inputs])
    (msg,) = call(
        functools.partial(label_kernel, half), [packed], msg, label, other_label, response, aliases={0: 0}
    )

    order = [0] + [j for i in range(1, nz // 2 + 1) for j in sorted({nz - i, i}, reverse=True)]
    blocks, turned, kepts, moments = [], [], [], None
    shapes = (half, features), (features, half)
    tiles = [(shape, kind) for shape in shapes for kind in (bf16, f8)]
    for j in order:
        part = flip(msg, "samp", nz, j) if j else msg
        high, low, high_t, low_t, kept, moments = call(
            functools.partial(features_kernel, j == 0),
            [*tiles, ((rows, half), f32), ((4, features), f32)],
            part, waves, offsets, *(() if j == 0 else (moments,)),
            scratch=[pltpu.VMEM((2, 8, features), f32), pltpu.VMEM((2, half, LANES), f32)],
            flops=60 * half * features,
        )
        blocks += [high, low]
        turned += [high_t, low_t]
        kepts.append(kept)
    count, later = nz - 1, 1
    msg_a, row_a = ((rows, half * count + LANES), f32), ((rows, half * count), f32)
    row_b = ((rows, half * later), f32)
    work = 2 * 3 * rows * half * features
    msg, scaled, precond, residual = call(
        functools.partial(begin_kernel, count),
        [msg_a, row_f, row_f, row_f],
        moments, flip(moments, "fold", nf, 1), penalty, mag, *turned[: 2 * count],
        flops=work * count,
    )
    before = weights = predicted = image = curve = sc = rows_a = rows_b = None
    for it in range(ITERS - 1):
        first, last = it == 0, it == ITERS - 2
        parts = exchange(msg, "feat", ny)
        (msg_b,) = call(forward_kernel, [row_b], scaled, mag, *turned[2 * count :], flops=work * later)
        parts_b = exchange(msg_b, "feat", ny)
        partial, new_a, new_sc = call(
            functools.partial(adjoint_kernel, ny, count, first),
            [row_f, row_a, row_c],
            *parts, *kepts[:count], *blocks[: 2 * count], *(() if first else (rows_a, sc)),
            flops=work * count,
        )
        msg, new_b = call(
            functools.partial(rest_kernel, ny, later, first),
            [msg_f, row_b],
            *parts_b, *kepts[count:], *blocks[2 * count :], new_sc, partial, *(() if first else (rows_b,)),
            flops=work * later,
        )
        sc = new_sc
        msg, scaled, before, weights, predicted, *rest = call(
            functools.partial(update_kernel, nz if last else count, first, last),
            [msg_s if last else msg_a, row_f, row_f, row_f, row_s] + ([row_s] if last else [row_f, row_f, row_c]),
            msg, flip(msg, "fold", nf, 1), sc, penalty, mag, precond, residual, scaled, new_a, new_b,
            *(turned if last else turned[: 2 * count]),
            *(() if first else (before, weights, predicted, image, curve, rows_a, rows_b)),
            flops=work * count,
        )
        rows_a, rows_b = new_a, new_b
        residual, image, curve = (None, None, None) if last else rest
    msg, image_rows, sc = call(
        functools.partial(last_kernel, ny, nz),
        [msg_s, row_s, row_c],
        *exchange(msg, "feat", ny), *kepts, rest[0], sc, predicted,
    )
    outs = call(
        functools.partial(finish_kernel, nz),
        [((rows // 2, features + shard), f32)] * nz,
        msg, flip(msg, "fold", nf, 1), sc, penalty, scaled, before, weights, image_rows, predicted,
    )
    far_first = [0, *range(nz - 1, 0, -1)]
    outs = [flip(outs[order.index(j)], "samp", nz, j) if j else outs[0] for j in far_first]
    return call(
        functools.partial(arrange_kernel, far_first),
        [((levels, features), f32), ((levels, shard), f32)],
        *outs,
        scratch=[pltpu.VMEM((nz, rows // 2, features + shard), f32)],
        in_vmem=False,
    )


def solution(mesh):
    placed = (
        P("samp", None),
        P(None, "feat"),
        P("feat"),
        P("feat"),
        P("samp"),
        P(("fold", "samp")),
        P(),
    )
    sizes = [mesh.shape[axis] for axis in ("fold", "samp", "feat")]
    return jax.shard_map(
        functools.partial(shards, *sizes),
        mesh=mesh,
        in_specs=placed,
        out_specs=(P("fold", "feat"), P("fold", "samp")),
        check_vma=False,
    )
```

```python
import functools
import math

import jax
import jax.numpy as jnp
from jax import lax
from jax.experimental import pallas as pl
from jax.experimental.pallas import tpu as pltpu
from jax.sharding import PartitionSpec as P

f32, bf16, f8 = jnp.float32, jnp.bfloat16, jnp.float8_e4m3fn
TURN = 1.0 / (2.0 * math.pi)
SINE = (-6.283164044377446, 41.337142378931674, -81.34076911271806, 70.99343519544783)
LANES = 128
VMEM_LIMIT = 12 * 2**20
RAISE = 512.0


def call(body, outs, *args, flops=0, in_vmem=True, scratch=(), aliases={}):
    outs = [pltpu.VMEM(s, d) if in_vmem else jax.ShapeDtypeStruct(s, d) for s, d in outs]
    size = sum(math.prod(a.shape) * a.dtype.itemsize for a in args)
    return pl.pallas_call(
        body,
        out_shape=outs,
        scratch_shapes=list(scratch),
        input_output_aliases=aliases,
        compiler_params=pltpu.CompilerParams(vmem_limit_bytes=VMEM_LIMIT),
        cost_estimate=pl.CostEstimate(flops=flops, bytes_accessed=size, transcendentals=0),
    )(*args)


def total(refs):
    values = [r[...] for r in refs]
    while len(values) > 1:
        values = [values[i] + values[i + 1] for i in range(0, len(values), 2)]
    return values[0]


def halves(value):
    high = value.astype(bf16)
    return high, (value - high.astype(f32)).astype(bf16)


def split(rows):
    high, low = halves(rows)
    both = jnp.concatenate([high.astype(f32), low.astype(f32)], axis=0).astype(bf16)
    scale = 256.0 / jnp.maximum(jnp.max(jnp.abs(rows), axis=1, keepdims=True), 1e-30)
    scaled = rows * scale
    coarse = scaled.astype(f8).astype(f32)
    small = jnp.concatenate([coarse, (scaled - coarse) * 16.0], axis=0).astype(f8)
    return both, small, 1.0 / scale


def product(parts, high_ref, low_ref):
    both, small, back = parts
    n = back.shape[0]
    out = jnp.dot(both, high_ref[...], preferred_element_type=f32)
    fine = jnp.dot(small, low_ref[...], preferred_element_type=f32)
    return out[:n] + out[n:] + (fine[:n] + fine[n:] * 0.0625) * back


def held(scaled, mag):
    high, low = halves(scaled * mag)
    rounded = high.astype(f32) + low.astype(f32)
    return rounded / mag, rounded


def pack_scalars(columns, rows):
    lane = lax.broadcasted_iota(jnp.int32, (rows, LANES), 1)
    out = jnp.zeros((rows, LANES), f32)
    for i, column in enumerate(columns):
        out = jnp.where(lane == i, column, out)
    return out


def row_sum(value):
    return jnp.sum(value, axis=1, keepdims=True)


def flip(value, axis, n, s):
    return lax.ppermute(value, axis, [(i, i ^ s) for i in range(n)])


def exchange(value, axis, n):
    return [value] + [flip(value, axis, n, s) for s in range(1, n)]


def as_row(block):
    return jnp.concatenate([block[i : i + 1] for i in range(block.shape[0])], axis=1)


def spread(pair, rows):
    return jnp.concatenate(
        [jnp.broadcast_to(pair[e : e + 1], (rows // 2, pair.shape[1])) for e in (0, 1)], axis=0
    )


def core():
    return lax.rem(lax.axis_index("fold"), 2)


def pack_kernel(
    scale, x_hbm, w_hbm, offset_hbm, mag_hbm, response_hbm, label_hbm, penalty_hbm,
    msg, w_ref, offset_ref, mag_ref, penalty_ref, response_out, label_out,
    offset_in, mag_in, response_ref, label_ref, penalty_in, sems,
):
    half = x_hbm.shape[0] // 2
    c = core()
    pairs = [
        (x_hbm.at[pl.ds(pl.multiple_of(c * half, half), half), :], msg.at[pl.ds(0, half), :]),
        (label_hbm, label_ref), (response_hbm, response_ref), (w_hbm, w_ref),
        (offset_hbm, offset_in), (mag_hbm, mag_in), (penalty_hbm, penalty_in),
    ]
    copies = [pltpu.make_async_copy(a, b, sems.at[i]) for i, (a, b) in enumerate(pairs)]
    for copy in copies:
        copy.start()
    for copy in copies:
        copy.wait()
    msg[half:, :] = jnp.zeros_like(msg[half:, :])
    label_out[...] = label_ref[...]
    response_out[...] = response_ref[...]
    offset_ref[...] = offset_in[...] * TURN
    mag_ref[...] = mag_in[...] * (scale / RAISE)
    levels, rows = penalty_in.shape[1], penalty_ref.shape[0]
    row, column = [lax.broadcasted_iota(jnp.int32, (rows, levels), a) for a in (0, 1)]
    chosen = column == lax.axis_index("samp") * (rows // 2) + lax.rem(row, rows // 2)
    penalty_ref[...] = row_sum(jnp.where(chosen, penalty_in[...], 0.0))


def label_kernel(half, points, label, other_label, response, msg):
    n = half // LANES
    c = core()

    def mine(block):
        return jnp.where(c == 0, block[:n], block[n:])

    own = (mine(label[...]) != 0).astype(f32)
    other = (mine(other_label[...]) != 0).astype(f32)
    y = mine(response[...])
    high, low = halves(y)
    aux = [jnp.where(c == 0, own, other), jnp.where(c == 0, other, own)]
    aux += [v.astype(f32) for v in (high, low)]
    if msg.shape[0] - half > 4 * n:
        aux += [jnp.zeros((msg.shape[0] - half - 4 * n, LANES), f32)]
    msg[half:, :] = jnp.concatenate(aux, axis=0).astype(bf16)


def features_kernel(first, msg, w_ref, offset_ref, *refs):
    before, refs = (None, refs) if first else (refs[0], refs[1:])
    high_ref, low_ref, high_t, low_t, kept_ref, moment_ref, acc, mask = refs
    samples, features = high_ref.shape
    n = samples // LANES
    aux = msg[samples:, :].astype(f32)
    kept = jnp.concatenate([as_row(aux[e * n : (e + 1) * n]) for e in (0, 1)], axis=0)
    kept_ref[...] = spread(kept, kept_ref.shape[0])
    y = aux[2 * n : 3 * n] + aux[3 * n : 4 * n]
    y_high, y_low = halves(kept * as_row(y))
    y_both = jnp.concatenate([y_high.astype(f32), y_low.astype(f32)], axis=0).astype(bf16)
    columns = jnp.concatenate([kept, jnp.zeros((6, samples), f32)], axis=0).T
    for e in (0, 1):
        mask[e] = jnp.broadcast_to(columns[:, e : e + 1], (samples, LANES))
    cb = min(features, 256)
    for j in range(0, features, cb):
        a = jnp.dot(msg[:samples, :], w_ref[:, j : j + cb], preferred_element_type=f32)
        t = a * TURN + offset_ref[:, j : j + cb]
        r = t - jnp.round(t)
        q = jnp.abs(r) - 0.25
        u = q * q
        c = jnp.full_like(u, SINE[-1] * RAISE)
        for k in SINE[-2::-1]:
            c = c * u + k * RAISE
        c = c * q
        high, low = halves(c)
        high_ref[:, j : j + cb] = high
        small = (c - high.astype(f32)).astype(f8)
        low_ref[:, j : j + cb] = small
        high_t[j : j + cb, :] = high.T
        low_t[j : j + cb, :] = small.T
        square = c * c
        for e in (0, 1):
            part = square * jnp.concatenate([mask[e]] * (cb // LANES), axis=1)
            acc[e, :, j : j + cb] = part.reshape(samples // 8, 8, cb).sum(0)
        side = jnp.dot(y_both, high, preferred_element_type=f32)
        side = side[:2] + side[2:] + jnp.dot(y_high, low, preferred_element_type=f32)
        moment_ref[2:4, j : j + cb] = side if first else before[2:4, j : j + cb] + side
    for e in (0, 1):
        square = jnp.sum(acc[e], axis=0, keepdims=True)
        moment_ref[e : e + 1, :] = square if first else before[e : e + 1, :] + square


def window(refs, each, axis, low, high):
    out, at = [], 0
    for i in range(0, len(refs), each):
        size = refs[i].shape[axis]
        a, b = max(low - at, 0), min(high - at, size)
        if a < b:
            take = (slice(None), slice(a, b)) if axis else (slice(a, b), slice(None))
            out += [r.at[take] for r in refs[i : i + each]]
        at += size
    return out


def forward(v, blocks, msg):
    at, parts = 0, split(v)
    for high, low in zip(blocks[::2], blocks[1::2]):
        n = high.shape[1]
        msg[:, at : at + n] = product(parts, high, low)
        at += n
    return at


def send_forward(v, blocks, msg, scalars):
    at = forward(v, blocks, msg)
    msg[:, at:] = pack_scalars(scalars, v.shape[0])


def forward_kernel(skip, scaled, mag, *refs):
    forward(scaled[...] * mag[...], window(refs[:-1], 2, 1, skip, refs[0].shape[1]), refs[-1])


def begin_kernel(nz, cut, *refs):
    moments, penalty, mag, blocks = refs[:2], refs[2], refs[3], refs[4 : 4 + 2 * nz]
    msg, direction, precond, residual = refs[4 + 2 * nz :]
    blocks = window(blocks, 2, 1, 0, cut)
    sums = total(moments)
    m = mag[...]
    rows = penalty.shape[0]
    pre = spread(sums[0:2] * (m * m), rows) + penalty[...]
    res = spread(sums[2:4] * m, rows)
    s, v = held(res / pre, m)
    precond[...] = pre
    residual[...] = res
    direction[...] = s
    send_forward(v, blocks, msg, [row_sum(res * s), row_sum(s * s)])


def direction_scalars(sc, before_sc):
    rz, dd = sc[:, 0:1], sc[:, 1:2]
    if before_sc is None:
        return rz, dd, jnp.zeros_like(rz), jnp.zeros_like(rz)
    beta = rz / before_sc[:, 0:1]
    dot = sc[:, 2:3] + beta * before_sc[:, 1:2]
    return rz, dd + beta * (sc[:, 2:3] + dot), beta, dot


def adjoint(image_rows, before, kepts, blocks):
    start, out = 0, 0.0
    squares = cross = jnp.zeros((image_rows.shape[0], 1), f32)
    for kept, high, low in zip(kepts, blocks[::2], blocks[1::2]):
        at = slice(start, start + kept.shape[1])
        start = at.stop
        rows = image_rows[:, at]
        weighted = rows * kept[...]
        squares = squares + row_sum(weighted * rows)
        if before is not None:
            cross = cross + row_sum(weighted * before[:, at])
        out = out + product(split(weighted), high, low)
    return out, squares, cross


def adjoint_kernel(ny, nz, cut, first, *refs):
    parts, refs = refs[:ny], refs[ny:]
    kepts, blocks, refs = refs[:nz], refs[nz : 3 * nz], refs[3 * nz :]
    kepts, blocks = window(kepts, 1, 1, 0, cut), window(blocks, 2, 0, 0, cut)
    sums = total(parts)
    image_rows, sc = sums[:, :cut], sums[:, cut:]
    before, before_sc = (None, None) if first else refs[:2]
    partial, rows_out, sc_out = refs[-3:]
    rz, dd, beta, dot = direction_scalars(sc, before_sc)
    if not first:
        before = before[...]
        image_rows = image_rows + beta * before
    out, squares, cross = adjoint(image_rows, before, kepts, blocks)
    partial[...] = out
    rows_out[...] = image_rows
    sc_out[...] = pack_scalars([rz, dd, beta, dot, squares, cross], dd.shape[0])


def rest_kernel(ny, skip, first, *refs):
    parts, refs = refs[:ny], refs[ny:]
    half = refs[0].shape[1]
    kepts, blocks, refs = window(refs[:1], 1, 1, skip, half), window(refs[1:3], 2, 0, skip, half), refs[3:]
    sc, partial, refs = refs[0], refs[1], refs[2:]
    image_rows = total(parts)
    before = None
    if not first:
        before = refs[0][...]
        image_rows = image_rows + sc[:, 2:3] * before
    msg, rows_out = refs[-2:]
    out, squares, cross = adjoint(image_rows, before, kepts, blocks)
    features = out.shape[1]
    msg[:, :features] = partial[...] + out
    msg[:, features:] = pack_scalars([sc[:, 4:5] + squares, sc[:, 5:6] + cross], out.shape[0])
    rows_out[...] = image_rows


def update_kernel(nz, cut, first, last, *refs):
    parts, refs = refs[:2], refs[2:]
    sc, penalty, mag, precond, residual, scaled, rows, rest, refs = *refs[:8], refs[8:]
    blocks, refs = window(refs[: 2 * nz], 2, 1, 0, cut), refs[2 * nz :]
    sums = total(parts)
    features = mag.shape[1]
    lam, m = penalty[...], mag[...]
    direction = scaled[...]
    image_rows = jnp.concatenate([rows[...], rest[...]], axis=1)
    image = sums[:, :features] * m
    scalars = sums[:, features:]
    if first:
        image = image + lam * direction
    else:
        (before, weights, predicted, before_image, before_curve, before_rows, before_rest), refs = refs[:7], refs[7:]
        direction = direction + sc[:, 2:3] * before[...]
        extra = (scalars[:, 1:2] + lam * sc[:, 3:4]) / before_curve[:, 0:1]
        image = image + lam * direction - extra * before_image[...]
        direction = direction - extra * before[...]
        image_rows = image_rows - extra * jnp.concatenate([before_rows[...], before_rest[...]], axis=1)
    (msg, scaled_out, direction_out, weights_out, predicted_out), refs = refs[:5], refs[5:]
    curve = scalars[:, 0:1] + lam * sc[:, 1:2]
    step = sc[:, 0:1] / curve
    moved, fitted = step * direction, step * image_rows
    weights_out[...] = moved if first else weights[...] + moved
    predicted_out[...] = fitted if first else predicted[...] + fitted
    res = residual[...] - step * image
    s, v = held(res / precond[...], m)
    scaled_out[...] = s
    direction_out[...] = direction
    if last:
        refs[0][...] = image_rows
    else:
        refs[0][...] = res
        refs[1][...] = image
        refs[2][...] = pack_scalars([curve], curve.shape[0])
    send_forward(v, blocks, msg, [row_sum(res * s), row_sum(s * s), row_sum(s * direction)])


def fold_rows(value, fold):
    n = value.shape[0] // 2
    return jnp.where(fold == 0, value[:n], value[n:])


def last_kernel(ny, nz, *refs):
    parts, refs = refs[:ny], refs[ny:]
    kepts, (before, before_sc, predicted, msg, rows_out, sc_out) = refs[:nz], refs[nz:]
    sums = total(parts)
    half = kepts[0].shape[1]
    samples = half * nz
    rz, dd, beta, _ = direction_scalars(sums[:, samples:], before_sc)
    image_rows = sums[:, :samples] + beta * before[...]
    squares = jnp.zeros_like(dd)
    for j, kept in enumerate(kepts):
        rows = image_rows[:, j * half : (j + 1) * half]
        squares = squares + row_sum(rows * rows * kept[...])
    other = 1 - core()
    n = dd.shape[0] // 2
    msg[:n, :samples] = fold_rows(image_rows, other)
    msg[n:, :samples] = fold_rows(predicted[...], other)
    msg[:, samples:] = pack_scalars([squares], 2 * n)
    rows_out[...] = image_rows
    sc_out[...] = pack_scalars([rz, dd, beta], 2 * n)


def finish_kernel(nz, own, got, sc, penalty, scaled, before, weights, rows, predicted, *outs):
    samples, features = rows.shape[1], scaled.shape[1]
    half = samples // nz
    c = core()
    n = sc.shape[0] // 2
    step = sc[:, 0:1] / ((own[:, samples : samples + 1] + got[:, samples : samples + 1]) + penalty[...] * sc[:, 1:2])
    coefficients = weights[...] + step * (scaled[...] + sc[:, 2:3] * before[...])
    coefficients = fold_rows(coefficients, c)
    here = fold_rows(predicted[...] + step * rows[...], c)
    there = got[n:, :samples] + fold_rows(step, c) * got[:n, :samples]
    lower, upper = jnp.where(c == 0, here, there), jnp.where(c == 0, there, here)
    for j, out in enumerate(outs):
        out[:, :features] = coefficients
        out[:, features : features + half] = lower[:, j * half : (j + 1) * half]
        out[:, features + half :] = upper[:, j * half : (j + 1) * half]


def arrange_kernel(order, *refs):
    nz = len(order)
    parts, (weights_out, predictions_out, held) = refs[:nz], refs[nz:]
    features = weights_out.shape[1]
    n = weights_out.shape[0] // nz
    for j, part in zip(order, parts):
        held[j] = part[...]
    z = lax.axis_index("samp")
    for k in range(nz):
        part = held[lax.bitwise_xor(z, k)]
        weights_out[k * n : (k + 1) * n, :] = part[:, :features]
        predictions_out[k * n : (k + 1) * n, :] = part[:, features:]


ITERS = 3


def shards(
    nf,
    nz,
    ny,
    input_points,
    wave_numbers,
    offset_angles,
    feature_magnitudes,
    response_values,
    split_label,
    shrinkage_levels,
):
    shard, features = input_points.shape[0], wave_numbers.shape[1]
    depth = input_points.shape[1]
    levels = shrinkage_levels.shape[0]
    half, rows = shard // 2, 2 * (levels // nz)
    samples = half * nz
    tall = (shard // LANES, LANES)
    extra = pl.cdiv(4 * half // LANES, 16) * 16
    row_f, row_s, row_c = ((rows, features), f32), ((rows, samples), f32), ((rows, LANES), f32)
    msg_f, msg_s = ((rows, features + LANES), f32), ((rows, samples + LANES), f32)

    label = split_label.reshape(tall)
    other_label = flip(label, "fold", nf, 1)
    inputs = [input_points, wave_numbers, offset_angles.reshape(1, features), feature_magnitudes.reshape(1, features)]
    inputs += [response_values.reshape(tall), label, shrinkage_levels.reshape(1, levels)]
    vectors = [((1, features), f32), ((1, features), f32), (tall, f32), (tall, jnp.int32), ((1, levels), f32)]
    packed = ((half + extra, depth), bf16)
    msg, waves, offsets, mag, penalty, response, label = pl.pallas_call(
        functools.partial(pack_kernel, math.sqrt(2.0 / (features * ny))),
        out_shape=[
            pltpu.VMEM(*packed),
            pltpu.VMEM((depth, features), bf16),
            pltpu.VMEM((1, features), f32),
            pltpu.VMEM((1, features), f32),
            pltpu.VMEM((rows, 1), f32),
            pltpu.VMEM(tall, f32),
            pltpu.VMEM(tall, jnp.int32),
        ],
        in_specs=[pl.BlockSpec(memory_space=pltpu.HBM)] * len(inputs),
        scratch_shapes=[pltpu.VMEM(v, d) for v, d in vectors]
        + [pltpu.SemaphoreType.DMA((len(inputs),))],
        compiler_params=pltpu.CompilerParams(vmem_limit_bytes=VMEM_LIMIT),
    )(*[pltpu.with_memory_space_constraint(v, pltpu.HBM) for v in inputs])
    (msg,) = call(
        functools.partial(label_kernel, half), [packed], msg, label, other_label, response, aliases={0: 0}
    )

    order = [0] + [j for i in range(1, nz // 2 + 1) for j in sorted({nz - i, i}, reverse=True)]
    blocks, turned, kepts, moments = [], [], [], None
    shapes = (half, features), (features, half)
    tiles = [(shape, kind) for shape in shapes for kind in (bf16, f8)]
    for j in order:
        part = flip(msg, "samp", nz, j) if j else msg
        high, low, high_t, low_t, kept, moments = call(
            functools.partial(features_kernel, j == 0),
            [*tiles, ((rows, half), f32), ((4, features), f32)],
            part, waves, offsets, *(() if j == 0 else (moments,)),
            scratch=[pltpu.VMEM((2, 8, features), f32), pltpu.VMEM((2, half, LANES), f32)],
            flops=60 * half * features,
        )
        blocks += [high, low]
        turned += [high_t, low_t]
        kepts.append(kept)
    skip = half // 2
    cut = samples - half + skip
    msg_a, row_a = ((rows, cut + LANES), f32), ((rows, cut), f32)
    row_b = ((rows, samples - cut), f32)
    work, work_b = 6 * rows * cut * features, 6 * rows * (samples - cut) * features
    msg, scaled, precond, residual = call(
        functools.partial(begin_kernel, nz, cut),
        [msg_a, row_f, row_f, row_f],
        moments, flip(moments, "fold", nf, 1), penalty, mag, *turned,
        flops=work,
    )
    before = weights = predicted = image = curve = sc = rows_a = rows_b = None
    for it in range(ITERS - 1):
        first, last = it == 0, it == ITERS - 2
        parts = exchange(msg, "feat", ny)
        (msg_b,) = call(functools.partial(forward_kernel, skip), [row_b], scaled, mag, *turned[-2:], flops=work_b)
        parts_b = exchange(msg_b, "feat", ny)
        partial, new_a, new_sc = call(
            functools.partial(adjoint_kernel, ny, nz, cut, first),
            [row_f, row_a, row_c],
            *parts, *kepts, *blocks, *(() if first else (rows_a, sc)),
            flops=work,
        )
        msg, new_b = call(
            functools.partial(rest_kernel, ny, skip, first),
            [msg_f, row_b],
            *parts_b, kepts[-1], *blocks[-2:], new_sc, partial, *(() if first else (rows_b,)),
            flops=work_b,
        )
        sc = new_sc
        msg, scaled, before, weights, predicted, *rest = call(
            functools.partial(update_kernel, nz, samples if last else cut, first, last),
            [msg_s if last else msg_a, row_f, row_f, row_f, row_s] + ([row_s] if last else [row_f, row_f, row_c]),
            msg, flip(msg, "fold", nf, 1), sc, penalty, mag, precond, residual, scaled, new_a, new_b,
            *turned,
            *(() if first else (before, weights, predicted, image, curve, rows_a, rows_b)),
            flops=work,
        )
        rows_a, rows_b = new_a, new_b
        residual, image, curve = (None, None, None) if last else rest
    msg, image_rows, sc = call(
        functools.partial(last_kernel, ny, nz),
        [msg_s, row_s, row_c],
        *exchange(msg, "feat", ny), *kepts, rest[0], sc, predicted,
    )
    outs = call(
        functools.partial(finish_kernel, nz),
        [((rows // 2, features + shard), f32)] * nz,
        msg, flip(msg, "fold", nf, 1), sc, penalty, scaled, before, weights, image_rows, predicted,
    )
    far_first = [0, *range(nz - 1, 0, -1)]
    outs = [flip(outs[order.index(j)], "samp", nz, j) if j else outs[0] for j in far_first]
    return call(
        functools.partial(arrange_kernel, far_first),
        [((levels, features), f32), ((levels, shard), f32)],
        *outs,
        scratch=[pltpu.VMEM((nz, rows // 2, features + shard), f32)],
        in_vmem=False,
    )


def solution(mesh):
    placed = (
        P("samp", None),
        P(None, "feat"),
        P("feat"),
        P("feat"),
        P("samp"),
        P(("fold", "samp")),
        P(),
    )
    sizes = [mesh.shape[axis] for axis in ("fold", "samp", "feat")]
    return jax.shard_map(
        functools.partial(shards, *sizes),
        mesh=mesh,
        in_specs=placed,
        out_specs=(P("fold", "feat"), P("fold", "samp")),
        check_vma=False,
    )
```
